128 devices in a mesh: sfc: 32 (over y, z, core), sub: 4 (over x).
Axes of the slice: x: 4, y: 4, z: 4, core: 2. Of those that a mesh axis runs over, the one named last changes fastest.
Arguments:
- solution: float32 [64, 5, 65536], P(None, None, ('sfc', 'sub')), as said below
- register: float32 [64, 5, 65536], P(None, None, ('sfc', 'sub')), may hold values from -6 to 6
- metric: float32 [3, 3, 65536], P(None, None, ('sfc', 'sub')), may hold values from -1.5 to 1.5
- face_normal: float32 [3, 393216], P(None, ('sfc', 'sub')), as said below
- partner: int32 [393216], P(('sfc', 'sub')), may hold values from 0 to 11263, as said below
- flip_code: int32 [393216], P(('sfc', 'sub')), may hold values from 0 to 7, as said below
- face_role: int32 [393216], P(('sfc', 'sub')), may hold values from 0 to 2
- send_face: int32 [128, 128, 64], P(('sfc', 'sub')), may hold values from -1 to 3071, as said below
Outputs:
- section_register: float32 [64, 5, 65536], P(None, None, ('sfc', 'sub'))
- advanced_state: float32 [64, 5, 65536], P(None, None, ('sfc', 'sub'))
The draws below stay inside these ranges and needn't reach their ends.
Inputs may be any that keep to these rules, and one draw needn't show every extreme that they name: `solution`: density and pressure of every node are positive. `face_normal`: the two sides of every face have normals of opposite sign. For face_role 0, a local column of the other side, whose partner is this column. For face_role 1 or 2, 3072 + q * 64 + k for the k-th face shared with device q, where q differs from this device's index by 1 to 24; all faces shared by two devices have their master on one of them. The other side's flip_code is the inverse orientation. `send_face`: row (q, p) lists device q's slave faces shared with device p, in slots k = 0, 1, ...; other slots hold -1. Rows with p and q more than 24 apart hold only -1. In every draw some device fills all 64 slots toward one peer.
All inputs are finite; a program needn't handle non-finite values.
Results may differ from the reference program's by a relative error of at most 0.0003.
Values sent between devices are 32-bit elements; how exact they have to be, the bound alone decides.
No kernel may reach another device: no remote copies, remote signals or barrier semaphores. Data moves between devices by JAX's collectives and lax.ppermute only.
A program may use at most 256 MiB of HBM per device.

```python
import jax
import jax.numpy as jnp
import numpy as np
from jax import lax

NODES = 64
VARIABLES = 5
E_DEV = 512
CAP = 64
ELEMS = 65536
N_SFC = 32
N_SUB = 4


OFFSETS = tuple(range(1, 25))


def inverse_flip(codes):
    return jnp.where(codes >= 4, 4 + 2 * (codes % 2) + codes // 2 % 2, codes)


def face_tables(key, pair_vectors, inner_vectors):
    devices = N_SFC * N_SUB
    columns = 6 * E_DEV
    count = len(OFFSETS)
    subkeys = jax.random.split(key, 6)
    shifts = jnp.array(OFFSETS, jnp.int32)
    device_rank = jnp.arange(devices, dtype=jnp.int32)
    device_rows = device_rank[:, None]
    offset_ids = jnp.arange(count)[None, :]
    pair_count = 2 * jax.random.randint(subkeys[0], (devices, count), max(1, CAP // 4), CAP // 2 + 1)
    valid_up = device_rows + shifts[None, :] < devices
    full_rank = jax.random.randint(subkeys[1], (), 0, devices - 1)
    forced = ((device_rows == full_rank) | (device_rows == devices - 2)) & (offset_ids == 0)
    pair_count = jnp.where(forced, CAP, pair_count)
    pair_count = jnp.where(valid_up, pair_count, 0).astype(jnp.int32)
    lower_master = jax.random.randint(subkeys[2], (devices, count), 0, 2)
    lower_master = jnp.where((device_rows == devices - 2) & (offset_ids == 0), 1, lower_master)
    pair_flip = jax.random.randint(subkeys[3], (devices, count, CAP), 0, 8)
    down_source = device_rows - shifts[None, :]
    down_valid = down_source >= 0
    down_count = jnp.where(down_valid, pair_count[jnp.clip(down_source, 0, devices - 1), offset_ids], 0)
    counts = jnp.concatenate([pair_count, down_count], axis=1)
    segment_end = jnp.cumsum(counts, axis=1)
    segment_start = segment_end - counts
    partition_total = segment_end[:, -1]
    position = jnp.arange(columns, dtype=jnp.int32)
    segment = jax.vmap(lambda ends: jnp.searchsorted(ends, position, side='right'))(segment_end).astype(jnp.int32)
    partition = segment < 2 * count
    segment_clip = jnp.minimum(segment, 2 * count - 1)
    slot_index = position[None, :] - jnp.take_along_axis(segment_start, segment_clip, axis=1)
    slot_clip = jnp.clip(slot_index, 0, CAP - 1)
    which = segment_clip % count
    upward = segment_clip < count
    peer_rank = jnp.where(upward, device_rows + shifts[which], device_rows - shifts[which])
    lower_rank = jnp.clip(jnp.minimum(device_rows, peer_rank), 0, devices - 1)
    chosen = lower_master[lower_rank, which]
    is_master = jnp.where(upward, chosen == 1, chosen == 0)
    pair_code = pair_flip[lower_rank, which, slot_clip]
    pair_code = jnp.where(is_master, pair_code, inverse_flip(pair_code))
    side_sign = jnp.where(is_master, 1.0, -1.0)
    pair_normal = pair_vectors[:, lower_rank, which, slot_clip] * side_sign[None]
    inner_index = position[None, :] - partition_total[:, None]
    parity = inner_index % 2
    pair_index = jnp.clip(inner_index // 2, 0, columns // 2 - 1)
    mate_position = jnp.clip(partition_total[:, None] + inner_index + 1 - 2 * parity, 0, columns - 1)
    column_perm = jax.vmap(lambda subkey: jax.random.permutation(subkey, columns))(jax.random.split(subkeys[4], devices)).astype(jnp.int32)
    first_entry = column_perm[:, 0:1]
    swapped_perm = jnp.where(column_perm == columns - 1, first_entry, jnp.where(position[None, :] == 0, columns - 1, column_perm))
    column_perm = jnp.where(device_rows == devices - 1, swapped_perm, column_perm).astype(jnp.int32)
    mate_column = jnp.take_along_axis(column_perm, mate_position, axis=1)
    inner_codes = jax.random.randint(subkeys[5], (devices, columns // 2), 0, 8)
    inner_code = inner_codes[device_rows, pair_index]
    inner_code = jnp.where(parity == 0, inner_code, inverse_flip(inner_code))
    inner_sign = jnp.where(parity == 0, 1.0, -1.0)
    inner_normal = inner_vectors[:, device_rows, pair_index] * inner_sign[None]
    partner_value = jnp.where(partition, columns + peer_rank * CAP + slot_index, mate_column).astype(jnp.int32)
    role_value = jnp.where(partition, jnp.where(is_master, 1, 2), 0).astype(jnp.int32)
    flip_value = jnp.where(partition, pair_code, inner_code).astype(jnp.int32)
    normal_value = jnp.where(partition[None], pair_normal, inner_normal).astype(jnp.float32)
    partner_grid = jnp.zeros((devices, columns), jnp.int32).at[device_rows, column_perm].set(partner_value)
    role_grid = jnp.zeros((devices, columns), jnp.int32).at[device_rows, column_perm].set(role_value)
    flip_grid = jnp.zeros((devices, columns), jnp.int32).at[device_rows, column_perm].set(flip_value)
    normal_grid = jnp.zeros((3, devices, columns), jnp.float32).at[:, device_rows, column_perm].set(normal_value)
    slave = partition & jnp.logical_not(is_master)
    target_peer = jnp.where(slave, peer_rank, devices)
    send_grid = jnp.full((devices, devices, CAP), -1, jnp.int32).at[device_rows, target_peer, slot_clip].set(column_perm, mode='drop')
    return (partner_grid.reshape(-1), flip_grid.reshape(-1), role_grid.reshape(-1), send_grid, normal_grid.reshape(3, -1))


def empty_vectors():
    devices = N_SFC * N_SUB
    return (jnp.zeros((3, devices, len(OFFSETS), CAP), jnp.float32), jnp.zeros((3, devices, 3 * E_DEV), jnp.float32))


def draw_partner(key, part):
    vectors = empty_vectors()
    return face_tables(key, vectors[0], vectors[1])[0]


def draw_flip_code(key, part):
    vectors = empty_vectors()
    return face_tables(key, vectors[0], vectors[1])[1]


def draw_face_role(key, part):
    vectors = empty_vectors()
    return face_tables(key, vectors[0], vectors[1])[2]


def draw_send_face(key, part):
    vectors = empty_vectors()
    return face_tables(key, vectors[0], vectors[1])[3]


def draw_face_normal(key, part):
    devices = N_SFC * N_SUB
    base_key = key
    key = jax.random.fold_in(key, 17)
    subkeys = jax.random.split(key, 2)
    pair_shape = (3, devices, len(OFFSETS), CAP)
    inner_shape = (3, devices, 3 * E_DEV)
    pair_vectors = 0.3 * jax.random.truncated_normal(subkeys[0], -2.0, 2.0, pair_shape, jnp.float32)
    inner_vectors = 0.3 * jax.random.truncated_normal(subkeys[1], -2.0, 2.0, inner_shape, jnp.float32)
    return face_tables(base_key, pair_vectors, inner_vectors)[4]


def draw_solution(key, part):
    key = jax.random.fold_in(key, 11)
    subkeys = jax.random.split(key, 3)
    node_shape = (64, ELEMS)
    ramp = jnp.arange(ELEMS, dtype=jnp.float32) / max(ELEMS - 1, 1)
    density = jnp.exp(jax.random.uniform(subkeys[0], node_shape, jnp.float32, jnp.log(0.5), jnp.log(2.0)))
    velocity = 0.2 * jax.random.truncated_normal(subkeys[1], -2.0, 2.0, (64, 3, ELEMS), jnp.float32)
    pressure = jnp.exp(jax.random.uniform(subkeys[2], node_shape, jnp.float32, jnp.log(0.5), jnp.log(2.0))) * (1.0 + 8.0 * ramp)[None]
    momentum = density[:, None] * velocity
    energy = pressure / 0.4 + 0.5 * density * jnp.sum(velocity * velocity, axis=1)
    return jnp.concatenate([density[:, None], momentum, energy[:, None]], axis=1)


def steps_of(stream_key, shape, cuts, least, high):
    factor_of, own = 1.0, jax.random.fold_in(stream_key, 6)
    for axis_at, parts in cuts:
        steps = jnp.exp(jax.random.uniform(jax.random.fold_in(own, axis_at), (parts,), jnp.float32, least / len(cuts), high / len(cuts)))
        factor_of = factor_of * jnp.repeat(steps, shape[axis_at] // parts).reshape([-1 if axis == axis_at else 1 for axis in range(len(shape))])
    return factor_of


def gaussian(key, dims, width, limit, cuts=(), kind=jnp.bfloat16):
    level = steps_of(key, dims, cuts, -0.22, 0.18) if cuts else 1.0
    values = jax.random.normal(key, dims, jnp.float32) * width * level
    return jnp.minimum(jnp.maximum(values, -limit), limit).astype(kind)


def setup_inputs(seed: int = 0) -> dict:
    arg_keys = jax.random.split(jax.random.key(seed), 9)
    return {
        "solution": draw_solution(jax.random.fold_in(arg_keys[8], 71), 0),
        "register": gaussian(arg_keys[1], (NODES, VARIABLES, ELEMS), 1.0, 6.0, ((2, 128),), jnp.float32),
        "metric": gaussian(arg_keys[2], (3, 3, ELEMS), 0.3, 1.5, ((2, 128),), jnp.float32),
        "face_normal": draw_face_normal(jax.random.fold_in(arg_keys[8], 71), 0),
        "partner": draw_partner(jax.random.fold_in(arg_keys[8], 71), 0),
        "flip_code": draw_flip_code(jax.random.fold_in(arg_keys[8], 71), 0),
        "face_role": draw_face_role(jax.random.fold_in(arg_keys[8], 71), 0),
        "send_face": draw_send_face(jax.random.fold_in(arg_keys[8], 71), 0),
    }


HEAT_RATIO = 1.4
LIFT_FACTOR = 6.0
PENALTY = 0.5
CFL_NUMBER = 0.3
SECTION_KEEP = -0.4178904745
SECTION_STEP = 0.4432226

def derivative_table():
    points = np.array([-1.0, -1.0 / np.sqrt(5.0), 1.0 / np.sqrt(5.0), 1.0])
    weights = np.array([1.0 / np.prod([points[target] - points[source] for source in range(4) if source != target]) for target in range(4)])
    matrix = np.zeros((4, 4))
    for target in range(4):
        for source in range(4):
            if target != source:
                matrix[target, source] = weights[source] / weights[target] / (points[target] - points[source])
        matrix[target, target] = -np.sum(matrix[target])
    identity = np.eye(4)
    first_dir = np.kron(matrix, np.kron(identity, identity))
    second_dir = np.kron(identity, np.kron(matrix, identity))
    third_dir = np.kron(identity, np.kron(identity, matrix))
    return jnp.asarray(np.concatenate([first_dir, second_dir, third_dir], axis=1), jnp.float32)

def face_traces(state_block):
    elements = state_block.shape[2]
    nodal_cube = state_block.reshape(4, 4, 4, 5, elements)
    face_list = [nodal_cube[0], nodal_cube[3], nodal_cube[:, 0], nodal_cube[:, 3], nodal_cube[:, :, 0], nodal_cube[:, :, 3]]
    return jnp.stack(face_list, axis=3).reshape(4, 4, 5, 6 * elements)

def lift_faces(surface, elements):
    pieces = surface.reshape(4, 4, 5, 6, elements)
    volume = jnp.zeros((4, 4, 4, 5, elements), surface.dtype)
    volume = volume.at[0].add(pieces[:, :, :, 0]).at[3].add(pieces[:, :, :, 1])
    volume = volume.at[:, 0].add(pieces[:, :, :, 2]).at[:, 3].add(pieces[:, :, :, 3])
    volume = volume.at[:, :, 0].add(pieces[:, :, :, 4]).at[:, :, 3].add(pieces[:, :, :, 5])
    return volume.reshape(64, 5, elements)

def orient(trace, codes):
    flip_first = (codes % 2 == 1)[None, None, None, :]
    flip_second = (codes // 2 % 2 == 1)[None, None, None, :]
    swapped = (codes >= 4)[None, None, None, :]
    trace = jnp.where(flip_first, trace[::-1], trace)
    trace = jnp.where(flip_second, trace[:, ::-1], trace)
    return jnp.where(swapped, jnp.swapaxes(trace, 0, 1), trace)

def normal_flux(values, normal):
    density = values[:, :, 0]
    momentum = values[:, :, 1:4]
    energy = values[:, :, 4]
    velocity = momentum / density[:, :, None]
    pressure = (HEAT_RATIO - 1.0) * (energy - 0.5 * lax.optimization_barrier(jnp.sum(momentum * velocity, axis=2)))
    normal_speed = lax.optimization_barrier(jnp.sum(velocity * normal[None, None], axis=2))
    flux_terms = jnp.concatenate([(density * normal_speed)[:, :, None], momentum * normal_speed[:, :, None] + pressure[:, :, None] * normal[None, None], ((energy + pressure) * normal_speed)[:, :, None]], axis=2)
    length = jnp.sqrt(lax.optimization_barrier(jnp.sum(normal * normal, axis=0)))
    wave = jnp.abs(normal_speed) + jnp.sqrt(HEAT_RATIO * pressure / density) * length[None, None]
    return (flux_terms, wave, length)

def face_flux(own, other_side, normal):
    own_flux, own_wave, length = normal_flux(own, normal)
    other_result = normal_flux(other_side, normal)
    wave_bound = jnp.maximum(own_wave, other_result[1])[:, :, None]
    jump_term = other_side - own
    viscous = jnp.array([0.0, 1.0, 1.0, 1.0, 1.0], jnp.float32)[None, None, :, None]
    star_flux = 0.5 * (own_flux + other_result[0]) - 0.5 * wave_bound * jump_term - PENALTY * length[None, None, None] * viscous * jump_term
    return (star_flux, own_flux)

def volume_rate(state_block, metric_block, derivative):
    elements = state_block.shape[2]
    density = state_block[:, 0]
    momentum = state_block[:, 1:4]
    energy = state_block[:, 4]
    velocity = momentum / density[:, None]
    pressure = (HEAT_RATIO - 1.0) * (energy - 0.5 * lax.optimization_barrier(jnp.sum(momentum * velocity, axis=1)))
    contravariant = []
    for direction in range(3):
        along = lax.optimization_barrier(jnp.sum(metric_block[direction][None] * velocity, axis=1))
        component = [(density * along)[:, None], momentum * along[:, None] + pressure[:, None] * metric_block[direction][None], ((energy + pressure) * along)[:, None]]
        contravariant.append(jnp.concatenate(component, axis=1))
    stacked = jnp.stack(contravariant, axis=0).reshape(192, 5 * elements)
    divergence = jnp.dot(derivative, stacked, precision=lax.Precision.HIGHEST, preferred_element_type=jnp.float32)
    return -divergence.reshape(64, 5, elements)

def node_speed(state_block):
    density = state_block[:, 0]
    momentum = state_block[:, 1:4]
    energy = state_block[:, 4]
    velocity = momentum / density[:, None]
    pressure = (HEAT_RATIO - 1.0) * (energy - 0.5 * lax.optimization_barrier(jnp.sum(momentum * velocity, axis=1)))
    return jnp.sqrt(lax.optimization_barrier(jnp.sum(velocity * velocity, axis=1))) + jnp.sqrt(HEAT_RATIO * pressure / density)

def reference(solution, register, metric, face_normal, partner, flip_code, face_role, send_face):
    devices = N_SFC * N_SUB
    elements = E_DEV
    columns = 6 * E_DEV
    slot_count = devices * CAP
    derivative = derivative_table()
    blocks = jnp.moveaxis(solution.reshape(64, 5, devices, elements), 2, 0)
    metric_all = jnp.moveaxis(metric.reshape(3, 3, devices, elements), 2, 0)
    normals_all = jnp.moveaxis(face_normal.reshape(3, devices, columns), 1, 0)
    partner_all = partner.reshape(devices, columns)
    codes_all = flip_code.reshape(devices, columns)
    roles_all = face_role.reshape(devices, columns)
    device_ids = jnp.arange(devices, dtype=jnp.int32)
    traces_all = lax.map(face_traces, blocks)

    def direct_flux(inputs):
        device_rank, own, normal, partner_row, flip_codes, face_kind = inputs
        local_side = jnp.take(own, jnp.clip(partner_row, 0, columns - 1), axis=3)
        remote_at = jnp.clip(partner_row - columns, 0, slot_count - 1)
        sender = (remote_at // CAP).astype(jnp.int32)
        slot_index = (remote_at % CAP).astype(jnp.int32)
        source_column = jnp.clip(send_face[sender, device_rank, slot_index], 0, columns - 1)
        remote = jnp.moveaxis(traces_all[sender, :, :, :, source_column], 0, 3)
        other_side = jnp.where((face_kind == 1)[None, None, None, :], remote, local_side)
        other_side = jnp.where((face_kind == 2)[None, None, None, :], own, other_side)
        return face_flux(own, orient(other_side, flip_codes), normal)
    stars, own_fluxes = lax.map(direct_flux, (device_ids, traces_all, normals_all, partner_all, codes_all, roles_all))
    master_position = jnp.where(roles_all == 1, partner_all - columns, slot_count)
    column_ids = jnp.broadcast_to(jnp.arange(columns, dtype=jnp.int32)[None, :], (devices, columns))
    owner_column = jnp.zeros((devices, slot_count), jnp.int32).at[device_ids[:, None], master_position].set(column_ids, mode='drop')

    def finish(inputs):
        device_rank, state_block, metric_block, star_flux, own_flux, partner_row, flip_codes, face_kind = inputs
        remote_at = jnp.clip(partner_row - columns, 0, slot_count - 1)
        master = (remote_at // CAP).astype(jnp.int32)
        slot_index = (remote_at % CAP).astype(jnp.int32)
        master_column = owner_column[master, device_rank * CAP + slot_index]
        returned = jnp.moveaxis(stars[master, :, :, :, master_column], 0, 3)
        slave_star = -orient(returned, flip_codes)
        final = jnp.where((face_kind == 2)[None, None, None, :], slave_star, star_flux)
        surface = LIFT_FACTOR * (own_flux - final)
        return volume_rate(state_block, metric_block, derivative) + lift_faces(surface, elements)
    rates = lax.map(finish, (device_ids, blocks, metric_all, stars, own_fluxes, partner_all, codes_all, roles_all))
    rate_field = jnp.moveaxis(rates, 0, 2).reshape(64, 5, devices * elements)
    top_speed = jnp.max(node_speed(solution))
    section_register = SECTION_KEEP * register + rate_field
    advanced_state = solution + CFL_NUMBER / top_speed * SECTION_STEP * section_register
    return (section_register, advanced_state)
```

```python
import jax
import jax.numpy as jnp
import numpy as np
from jax import lax
from jax.experimental import pallas as pl
from jax.experimental.pallas import tpu as pltpu
from jax.sharding import PartitionSpec as P

HEAT_RATIO = 1.4
LIFT_FACTOR = 6.0
CFL_NUMBER = 0.3
SECTION_KEEP = -0.4178904745
SECTION_STEP = 0.4432226
DEVICES = 128
ELEMENTS = 512
COLUMNS = 6 * ELEMENTS
SLOTS = 64
REACH = 24
LANES = 128
BLOCKS = ELEMENTS // LANES
TRACE = 80
MESSAGE = TRACE * SLOTS // LANES
UNROLL = 16
AXES = ("sfc", "sub")
VMEM_LIMIT = 48 * 1024 * 1024


def derivative_matrix():
    points = np.array([-1.0, -1.0 / np.sqrt(5.0), 1.0 / np.sqrt(5.0), 1.0])
    weights = np.array(
        [
            1.0
            / np.prod([points[target] - points[source] for source in range(4) if source != target])
            for target in range(4)
        ]
    )
    matrix = np.zeros((4, 4))
    for target in range(4):
        for source in range(4):
            if target != source:
                matrix[target, source] = (
                    weights[source] / weights[target] / (points[target] - points[source])
                )
        matrix[target, target] = -np.sum(matrix[target])
    return matrix


def face_nodes(face):
    side = 3 * (face % 2)
    if face < 2:
        return [side * 16 + i * 4 + j for i in range(4) for j in range(4)]
    if face < 4:
        return [i * 16 + side * 4 + j for i in range(4) for j in range(4)]
    return [i * 16 + j * 4 + side for i in range(4) for j in range(4)]


def spread_variables(state_ref, rows_ref):
    for node in range(64):
        for block in range(BLOCKS):
            rows_ref[pl.ds(node * BLOCKS + block, 5, stride=64 * BLOCKS), :] = state_ref[
                node, :, block * LANES : (block + 1) * LANES
            ]


def lane_index(shape):
    return lax.broadcasted_iota(jnp.int32, shape, 1)


def compact(rows):
    lane = lane_index((8, LANES))
    low = lane < 80
    mid = lane < 112

    def turn(value, shift):
        return pltpu.roll(value, shift, 1)

    first = [jnp.where(low, rows[k], turn(rows[5 + k], 80)) for k in range(3)]
    fourth = jnp.where(low, rows[3], jnp.where(mid, turn(rows[5], 32), turn(rows[7], 64)))
    fifth = jnp.where(low, rows[4], jnp.where(mid, turn(rows[6], 32), turn(rows[7], 48)))
    return first + [fourth, fifth]


def expand(parts):
    lane = lane_index((8, LANES))
    head = lane < 48
    body = lane < 64

    def turn(value, shift):
        return pltpu.roll(value, shift, 1)

    sixth = jnp.where(head, turn(parts[0], 48), turn(parts[3], 96))
    seventh = jnp.where(head, turn(parts[1], 48), turn(parts[4], 96))
    eighth = jnp.where(
        head, turn(parts[2], 48), jnp.where(body, turn(parts[3], 64), turn(parts[4], 80))
    )
    return list(parts) + [sixth, seventh, eighth]


def pack_kernel(rank_ref, partner_ref, state_ref, own_ref, table_ref, send_ref, rows_ref, board_ref):
    spread_variables(state_ref, rows_ref)
    for face in range(6):
        nodes = face_nodes(face)
        for block in range(BLOCKS):
            pieces = [state_ref[n, :, block * LANES : (block + 1) * LANES] for n in nodes]
            trace = jnp.concatenate(pieces, axis=0)
            place = face * BLOCKS + block
            own_ref[place * TRACE : (place + 1) * TRACE, :] = trace
            square = jnp.concatenate([trace, jnp.zeros((LANES - TRACE, LANES), jnp.float32)], axis=0)
            table_ref[place * LANES : (place + 1) * LANES, :] = square.T

    def scatter(step, carry):
        base = step * UNROLL
        for k in range(UNROLL):
            board_ref[pl.ds(partner_ref[base + k], 1), :] = table_ref[pl.ds(base + k, 1), :]
        return carry

    lax.fori_loop(0, COLUMNS // UNROLL, scatter, 0)

    def speeds(step, best):
        density, mom_x, mom_y, mom_z, energy = [
            rows_ref[pl.ds(pl.multiple_of(v * 256 + step * 64, 64), 64), :] for v in range(5)
        ]
        inverse = 1.0 / density
        square = (mom_x * mom_x + mom_y * mom_y + mom_z * mom_z) * inverse
        pressure = (HEAT_RATIO - 1.0) * (energy - 0.5 * square)
        wave = jnp.sqrt(square * inverse) + jnp.sqrt(HEAT_RATIO * pressure * inverse)
        return jnp.maximum(best, jnp.max(wave.reshape(8, 8, LANES), axis=0))

    best = lax.fori_loop(0, 4, speeds, jnp.zeros((8, LANES), jnp.float32))
    top = jnp.full((8, LANES), jnp.max(best), jnp.float32)
    rank = rank_ref[0]

    def fill(peer, carry):
        send_ref[peer, MESSAGE:, :] = top
        return carry

    lax.fori_loop(0, DEVICES, fill, 0)

    def message(peer, carry):
        base = pl.multiple_of(COLUMNS + peer * SLOTS, SLOTS)
        parts = compact([board_ref[pl.ds(base + 8 * k, 8), :] for k in range(8)])
        for k in range(5):
            send_ref[peer, 8 * k : 8 * k + 8, :] = parts[k]
        return carry

    lax.fori_loop(
        jnp.maximum(rank - REACH, 0), jnp.minimum(rank + REACH + 1, DEVICES), message, 0
    )


def volume_kernel(state_ref, metric_ref, rate_ref, rows_ref, tensor_ref, flux_ref):
    spread_variables(state_ref, rows_ref)
    for direction in range(3):
        for half in range(2):
            for block in range(BLOCKS):
                tensor_ref[pl.ds(direction * 24 + half * 4 + block, 3, stride=8), :] = metric_ref[
                    direction, :, block * LANES : (block + 1) * LANES
                ]

    def fluxes(step, carry):
        at = pl.multiple_of(step * 8, 8)
        density, mom_x, mom_y, mom_z, energy = [
            rows_ref[pl.ds(v * 256 + at, 8), :] for v in range(5)
        ]
        inverse = 1.0 / density
        momentum = [mom_x, mom_y, mom_z]
        velocity = [m * inverse for m in momentum]
        pressure = (HEAT_RATIO - 1.0) * (
            energy
            - 0.5 * (mom_x * velocity[0] + mom_y * velocity[1] + mom_z * velocity[2])
        )
        enthalpy = energy + pressure
        for direction in range(3):
            tensor = [tensor_ref[direction * 24 + k * 8 : direction * 24 + k * 8 + 8, :] for k in range(3)]
            along = tensor[0] * velocity[0] + tensor[1] * velocity[1] + tensor[2] * velocity[2]
            values = [density * along]
            values += [momentum[k] * along + pressure * tensor[k] for k in range(3)]
            values += [enthalpy * along]
            for v in range(5):
                flux_ref[direction, pl.ds(v * 256 + at, 8), :] = values[v]
        return carry

    lax.fori_loop(0, 32, fluxes, 0)
    matrix = derivative_matrix()
    upper = lax.broadcasted_iota(jnp.int32, (8, LANES), 0) < 4

    def pair(first, second):
        return jnp.where(upper, jnp.float32(first), jnp.float32(second))

    straight = [[pair(matrix[2 * t, 2 * s], matrix[2 * t + 1, 2 * s + 1]) for s in range(2)] for t in range(2)]
    crossed = [[pair(matrix[2 * t, 2 * s + 1], matrix[2 * t + 1, 2 * s]) for s in range(2)] for t in range(2)]

    def combine(values, target):
        total = values[0] * float(matrix[target, 0])
        for source in range(1, 4):
            total = total + values[source] * float(matrix[target, source])
        return total

    def diverge(v, carry):
        base = pl.multiple_of(v * 256, 256)
        for rest in range(8):
            values = [flux_ref[0, pl.ds(base + a * 64 + rest * 8, 8), :] for a in range(4)]
            for a in range(4):
                rate_ref[pl.ds(base + a * 64 + rest * 8, 8), :] = -combine(values, a)
        for a in range(4):
            for half in range(2):
                values = [flux_ref[1, pl.ds(base + a * 64 + b * 16 + half * 8, 8), :] for b in range(4)]
                third = [flux_ref[2, pl.ds(base + a * 64 + b * 16 + half * 8, 8), :] for b in range(4)]
                other = [flux_ref[2, pl.ds(base + a * 64 + b * 16 + (1 - half) * 8, 8), :] for b in range(4)]
                for b in range(4):
                    at = pl.ds(base + a * 64 + b * 16 + half * 8, 8)
                    same, far = third[b], other[b]
                    total = combine(values, b)
                    total = total + straight[half][half] * same
                    total = total + crossed[half][half] * pltpu.roll(same, 4, 0)
                    total = total + straight[half][1 - half] * far
                    total = total + crossed[half][1 - half] * pltpu.roll(far, 4, 0)
                    rate_ref[at, :] = rate_ref[at, :] - total
        return carry

    lax.fori_loop(0, 5, diverge, 0)


def normal_flux(values, normal, length):
    density, momentum, energy = values[0], values[1:4], values[4]
    inverse = 1.0 / density
    velocity = [m * inverse for m in momentum]
    pressure = (HEAT_RATIO - 1.0) * (
        energy
        - 0.5 * (momentum[0] * velocity[0] + momentum[1] * velocity[1] + momentum[2] * velocity[2])
    )
    speed = velocity[0] * normal[0] + velocity[1] * normal[1] + velocity[2] * normal[2]
    terms = [density * speed]
    terms += [momentum[k] * speed + pressure * normal[k] for k in range(3)]
    terms += [(energy + pressure) * speed]
    wave = jnp.abs(speed) + jnp.sqrt(HEAT_RATIO * pressure * inverse) * length
    return terms, wave


def finish_kernel(
    rank_ref,
    partner_ref,
    table_ref,
    own_ref,
    got_ref,
    code_ref,
    normal_ref,
    rate_in_ref,
    state_ref,
    register_ref,
    section_ref,
    advanced_ref,
    board_ref,
    picked_ref,
    other_ref,
    turned_ref,
    side_ref,
    rate_ref,
):
    rank = rank_ref[0]
    board_ref[0:COLUMNS, :] = table_ref[...]
    rate_ref[...] = rate_in_ref[...]

    def message(peer, carry):
        base = pl.multiple_of(COLUMNS + peer * SLOTS, SLOTS)
        rows = expand([got_ref[peer, 8 * k : 8 * k + 8, :] for k in range(5)])
        for k in range(8):
            board_ref[pl.ds(base + 8 * k, 8), :] = rows[k]
        return carry

    lax.fori_loop(
        jnp.maximum(rank - REACH, 0), jnp.minimum(rank + REACH + 1, DEVICES), message, 0
    )

    def gather(step, carry):
        base = step * UNROLL
        for k in range(UNROLL):
            picked_ref[pl.ds(base + k, 1), :] = board_ref[pl.ds(partner_ref[base + k], 1), :]
        return carry

    lax.fori_loop(0, COLUMNS // UNROLL, gather, 0)
    for place in range(COLUMNS // LANES):
        square = picked_ref[place * LANES : (place + 1) * LANES, :].T
        other_ref[place * TRACE : (place + 1) * TRACE, :] = square[0:TRACE]
        side_ref[pl.ds(place, 3, stride=24), :] = normal_ref[:, place * LANES : (place + 1) * LANES]

    for group in range(3):
        code = code_ref[group * 8 : group * 8 + 8, :]
        flip_first = code % 2 == 1
        flip_second = (code // 2) % 2 == 1
        swapped = code >= 4
        start = group * 8 * TRACE
        for v in range(5):
            grid = [
                [other_ref[pl.ds(start + (i * 4 + j) * 5 + v, 8, stride=TRACE), :] for j in range(4)]
                for i in range(4)
            ]
            grid = [[jnp.where(flip_first, grid[3 - i][j], grid[i][j]) for j in range(4)] for i in range(4)]
            grid = [[jnp.where(flip_second, grid[i][3 - j], grid[i][j]) for j in range(4)] for i in range(4)]
            for i in range(4):
                for j in range(4):
                    value = grid[i][j] if i == j else jnp.where(swapped, grid[j][i], grid[i][j])
                    at = ((i * 4 + j) * 5 + v) * 8
                    turned_ref[at : at + 8, :] = value
        normal = [side_ref[k * 24 + group * 8 : k * 24 + group * 8 + 8, :] for k in range(3)]
        length = jnp.sqrt(normal[0] * normal[0] + normal[1] * normal[1] + normal[2] * normal[2])
        first_nodes = face_nodes(2 * group)
        second_nodes = face_nodes(2 * group + 1)
        for node in range(16):
            own = [own_ref[pl.ds(start + node * 5 + v, 8, stride=TRACE), :] for v in range(5)]
            far = [turned_ref[(node * 5 + v) * 8 : (node * 5 + v) * 8 + 8, :] for v in range(5)]
            own_terms, own_wave = normal_flux(own, normal, length)
            far_terms, far_wave = normal_flux(far, normal, length)
            bound = jnp.maximum(own_wave, far_wave)
            viscous = bound + length
            for v in range(5):
                weight = bound if v == 0 else viscous
                surface = (0.5 * LIFT_FACTOR) * (
                    own_terms[v] - far_terms[v] + weight * (far[v] - own[v])
                )
                at = v * 256 + first_nodes[node] * 4
                rate_ref[at : at + 4, :] = rate_ref[at : at + 4, :] + surface[0:4]
                at = v * 256 + second_nodes[node] * 4
                rate_ref[at : at + 4, :] = rate_ref[at : at + 4, :] + surface[4:8]

    top = jnp.max(jnp.max(got_ref[:, MESSAGE:, :], axis=0))
    scale = CFL_NUMBER / top * SECTION_STEP

    def update(node, carry):
        for block in range(BLOCKS):
            lanes = slice(block * LANES, (block + 1) * LANES)
            rate = rate_ref[pl.ds(node * BLOCKS + block, 5, stride=64 * BLOCKS), :]
            section = SECTION_KEEP * register_ref[node, :, lanes] + rate
            section_ref[node, :, lanes] = section
            advanced_ref[node, :, lanes] = state_ref[node, :, lanes] + scale * section
        return carry

    lax.fori_loop(0, 64, update, 0)


def smem():
    return pl.BlockSpec(memory_space=pltpu.SMEM)


def vmem():
    return pl.BlockSpec(memory_space=pltpu.VMEM)


def params():
    return pltpu.CompilerParams(vmem_limit_bytes=VMEM_LIMIT)


def shape(*sizes):
    return jax.ShapeDtypeStruct(sizes, jnp.float32)


def scratch(*sizes):
    return pltpu.VMEM(sizes, jnp.float32)


def pack(rank, partner, state):
    return pl.pallas_call(
        pack_kernel,
        out_shape=(
            shape(COLUMNS // LANES * TRACE, LANES),
            shape(COLUMNS, LANES),
            shape(DEVICES, MESSAGE + 8, LANES),
        ),
        in_specs=[smem(), smem(), vmem()],
        out_specs=(vmem(), vmem(), vmem()),
        scratch_shapes=[scratch(1280, LANES), scratch(COLUMNS + DEVICES * SLOTS, LANES)],
        compiler_params=params(),
        name="pack",
    )(rank, partner, state)


def volume(state, metric):
    return pl.pallas_call(
        volume_kernel,
        out_shape=shape(1280, LANES),
        in_specs=[vmem(), vmem()],
        out_specs=vmem(),
        scratch_shapes=[scratch(1280, LANES), scratch(72, LANES), scratch(3, 1280, LANES)],
        compiler_params=params(),
        name="volume",
    )(state, metric)


def finish(rank, partner, table, own, got, code, normal, rate, state, register):
    return pl.pallas_call(
        finish_kernel,
        out_shape=(shape(64, 5, ELEMENTS), shape(64, 5, ELEMENTS)),
        in_specs=[smem(), smem()] + [vmem()] * 8,
        out_specs=(vmem(), vmem()),
        scratch_shapes=[
            scratch(COLUMNS + DEVICES * SLOTS, LANES),
            scratch(COLUMNS, LANES),
            scratch(COLUMNS // LANES * TRACE, LANES),
            scratch(16 * 5 * 8, LANES),
            scratch(72, LANES),
            scratch(1280, LANES),
        ],
        compiler_params=params(),
        name="finish",
    )(rank, partner, table, own, got, code, normal, rate, state, register)


def on_device(state, register, metric, face_normal, partner, flip_code, face_role, send_face):
    rank = lax.axis_index(AXES).astype(jnp.int32)[None]
    own, table, send = pack(rank, partner, state)
    rate = volume(state, metric)
    got = lax.all_to_all(send, AXES, 0, 0, tiled=True)
    code = flip_code.reshape(COLUMNS // LANES, LANES)
    return finish(rank, partner, table, own, got, code, face_normal, rate, state, register)


def solution(mesh):
    placed = (
        P(None, None, AXES),
        P(None, None, AXES),
        P(None, None, AXES),
        P(None, AXES),
        P(AXES),
        P(AXES),
        P(AXES),
        P(AXES, None, None),
    )
    return jax.shard_map(
        on_device,
        mesh=mesh,
        in_specs=placed,
        out_specs=(P(None, None, AXES), P(None, None, AXES)),
        check_vma=False,
    )
```

```python
import jax
import jax.numpy as jnp
import numpy as np
from jax import lax
from jax.experimental import pallas as pl
from jax.experimental.pallas import tpu as pltpu
from jax.sharding import Mesh
from jax.sharding import PartitionSpec as P

HEAT_RATIO = 1.4
LIFT_FACTOR = 6.0
CFL_NUMBER = 0.3
SECTION_KEEP = -0.4178904745
SECTION_STEP = 0.4432226
DEVICES = 128
ELEMENTS = 512
COLUMNS = 6 * ELEMENTS
SLOTS = 64
REACH = 24
LANES = 128
BLOCKS = ELEMENTS // LANES
TRACE = 80
MESSAGE = TRACE * SLOTS // LANES
UNROLL = 16
AXES = ("y", "r", "x")
PLANE = 32
NEAR = PLANE - REACH
CROSS = REACH
MARGIN = CROSS
VMEM_LIMIT = 24 * 1024 * 1024


def derivative_matrix():
    points = np.array([-1.0, -1.0 / np.sqrt(5.0), 1.0 / np.sqrt(5.0), 1.0])
    weights = np.array(
        [
            1.0
            / np.prod([points[target] - points[source] for source in range(4) if source != target])
            for target in range(4)
        ]
    )
    matrix = np.zeros((4, 4))
    for target in range(4):
        for source in range(4):
            if target != source:
                matrix[target, source] = (
                    weights[source] / weights[target] / (points[target] - points[source])
                )
        matrix[target, target] = -np.sum(matrix[target])
    return matrix


def face_nodes(face):
    side = 3 * (face % 2)
    if face < 2:
        return [side * 16 + i * 4 + j for i in range(4) for j in range(4)]
    if face < 4:
        return [i * 16 + side * 4 + j for i in range(4) for j in range(4)]
    return [i * 16 + j * 4 + side for i in range(4) for j in range(4)]


def tile_lanes(block):
    return slice(block * LANES, (block + 1) * LANES)


def spread_nodes(state_ref, rows_ref):
    for v in range(5):
        for tile in range(8):
            for block in range(BLOCKS):
                rows_ref[pl.ds(v * 256 + tile * 32 + block, 8, stride=BLOCKS), :] = state_ref[
                    v, tile * 8 : tile * 8 + 8, tile_lanes(block)
                ]


def face_rows(state_ref, flat_ref, v, face, block):
    side = 3 * (face % 2)
    lanes = tile_lanes(block)
    if face < 2:
        return state_ref[v, side * 16 : side * 16 + 16, lanes]
    if face < 4:
        return jnp.concatenate(
            [state_ref[v, i * 16 + side * 4 : i * 16 + side * 4 + 4, lanes] for i in range(4)], axis=0
        )
    return flat_ref[pl.ds(block * 320 + v * 64 + side, 16, stride=4), :]


def lane_index(shape):
    return lax.broadcasted_iota(jnp.int32, shape, 1)


def compact(rows):
    lane = lane_index((8, LANES))
    low = lane < 80
    mid = lane < 112

    def turn(value, shift):
        return pltpu.roll(value, shift, 1)

    first = [jnp.where(low, rows[k], turn(rows[5 + k], 80)) for k in range(3)]
    fourth = jnp.where(low, rows[3], jnp.where(mid, turn(rows[5], 32), turn(rows[7], 64)))
    fifth = jnp.where(low, rows[4], jnp.where(mid, turn(rows[6], 32), turn(rows[7], 48)))
    return first + [fourth, fifth]


def expand(parts):
    lane = lane_index((8, LANES))
    head = lane < 48
    body = lane < 64

    def turn(value, shift):
        return pltpu.roll(value, shift, 1)

    sixth = jnp.where(head, turn(parts[0], 48), turn(parts[3], 96))
    seventh = jnp.where(head, turn(parts[1], 48), turn(parts[4], 96))
    eighth = jnp.where(
        head, turn(parts[2], 48), jnp.where(body, turn(parts[3], 64), turn(parts[4], 80))
    )
    return list(parts) + [sixth, seventh, eighth]


def pack_kernel(
    place_ref, partner_ref, state_ref, own_ref, table_ref, plane_ref, up_ref, down_ref, best_ref, board_ref, flat_ref
):
    for block in range(BLOCKS):
        for v in range(5):
            flat_ref[block * 320 + v * 64 : block * 320 + v * 64 + 64, :] = state_ref[v, :, tile_lanes(block)]
    for face in range(6):
        for block in range(BLOCKS):
            pieces = [face_rows(state_ref, flat_ref, v, face, block) for v in range(5)]
            trace = jnp.concatenate(pieces, axis=0)
            place = face * BLOCKS + block
            own_ref[place * TRACE : (place + 1) * TRACE, :] = trace
            square = jnp.concatenate([trace, jnp.zeros((LANES - TRACE, LANES), jnp.float32)], axis=0)
            table_ref[place * LANES : (place + 1) * LANES, :] = square.T

    def scatter(step, carry):
        base = step * UNROLL
        for k in range(UNROLL):
            board_ref[pl.ds(partner_ref[base + k], 1), :] = table_ref[pl.ds(base + k, 1), :]
        return carry

    lax.fori_loop(0, COLUMNS // UNROLL, scatter, 0)

    def speeds(step, best):
        density, mom_x, mom_y, mom_z, energy = [
            state_ref[v, pl.ds(pl.multiple_of(step * 8, 8), 8), :] for v in range(5)
        ]
        inverse = 1.0 / density
        square = (mom_x * mom_x + mom_y * mom_y + mom_z * mom_z) * inverse
        pressure = (HEAT_RATIO - 1.0) * (energy - 0.5 * square)
        wave = jnp.sqrt(square * inverse) + jnp.sqrt(HEAT_RATIO * pressure * inverse)
        return jnp.maximum(best, wave)

    best = lax.fori_loop(0, 8, speeds, jnp.zeros((8, ELEMENTS), jnp.float32))
    best = jnp.maximum(
        jnp.maximum(best[:, tile_lanes(0)], best[:, tile_lanes(1)]),
        jnp.maximum(best[:, tile_lanes(2)], best[:, tile_lanes(3)]),
    )
    best_ref[...] = best
    up_ref[CROSS * MESSAGE :, :] = best
    down_ref[CROSS * MESSAGE :, :] = best
    plane, spot = place_ref[0], place_ref[1]

    def send(to_ref, peer, row):
        base = pl.multiple_of(COLUMNS + peer * SLOTS, SLOTS)
        parts = compact([board_ref[pl.ds(base + 8 * k, 8), :] for k in range(8)])
        for k in range(5):
            to_ref[pl.ds(pl.multiple_of(row + 8 * k, 8), 8), :] = parts[k]

    def send_plane(step, carry):
        for k in range(4):
            block = step * 4 + k
            send(plane_ref, plane * PLANE + block, block * MESSAGE)
        return carry

    def send_up(step, carry):
        for k in range(4):
            block = step * 4 + k
            send(up_ref, (plane + 1) * PLANE + block, block * MESSAGE)
        return carry

    def send_down(step, carry):
        for k in range(4):
            block = step * 4 + k
            send(down_ref, (plane - 1) * PLANE + NEAR + block, block * MESSAGE)
        return carry

    lax.fori_loop(0, (jnp.maximum(spot - NEAR + 1, 0) + 3) // 4, send_up, 0)
    lax.fori_loop(spot // 4, CROSS // 4, send_down, 0)
    lax.fori_loop(jnp.maximum(spot - REACH, 0) // 4, PLANE // 4, send_plane, 0)


def relay_kernel(place_ref, up_ref, down_ref, best_ref, far_ref, relay_ref):
    top = jnp.maximum(
        jnp.maximum(best_ref[...], far_ref[...]),
        jnp.maximum(up_ref[CROSS * MESSAGE :, :], down_ref[CROSS * MESSAGE :, :]),
    )
    spot = place_ref[1]
    for block in range(PLANE):
        relay_ref[block, MESSAGE:, :] = top

    def from_up(block, carry):
        for k in range(5):
            at = pl.multiple_of(block * MESSAGE + 8 * k, 8)
            relay_ref[block, 8 * k : 8 * k + 8, :] = up_ref[pl.ds(at, 8), :]
        return carry

    def from_down(block, carry):
        for k in range(5):
            at = pl.multiple_of(block * MESSAGE + 8 * k, 8)
            relay_ref[block + NEAR, 8 * k : 8 * k + 8, :] = down_ref[pl.ds(at, 8), :]
        return carry

    lax.fori_loop(0, jnp.maximum(spot - NEAR + 1, 0), from_up, 0)
    lax.fori_loop(spot, CROSS, from_down, 0)


def early_kernel(place_ref, partner_ref, table_ref, plane_ref, picked_ref, late_ref, board_ref):
    plane, spot = place_ref[0], place_ref[1]
    board_ref[0:COLUMNS, :] = table_ref[...]

    def receive(step, carry):
        for k in range(4):
            block = step * 4 + k
            start = pl.multiple_of(block * MESSAGE, 8)
            rows = expand([plane_ref[pl.ds(start + 8 * k, 8), :] for k in range(5)])
            base = pl.multiple_of(COLUMNS + (plane * PLANE + block) * SLOTS, SLOTS)
            for k in range(8):
                board_ref[pl.ds(base + 8 * k, 8), :] = rows[k]
        return carry

    lax.fori_loop(jnp.maximum(spot - REACH, 0) // 4, PLANE // 4, receive, 0)
    low = COLUMNS + plane * (PLANE * SLOTS)

    def gather(step, count):
        base = step * UNROLL
        for k in range(UNROLL):
            index = partner_ref[base + k]
            picked_ref[pl.ds(base + k, 1), :] = board_ref[pl.ds(index, 1), :]
            late_ref[1 + count] = base + k
            outside = (index < low) | (index >= low + PLANE * SLOTS)
            count = count + ((index >= COLUMNS) & outside).astype(jnp.int32)
        return count

    count = lax.fori_loop(0, COLUMNS // UNROLL, gather, jnp.int32(0))
    last = jnp.where(count > 0, late_ref[jnp.maximum(count, 1)], 0)
    for k in range(UNROLL):
        late_ref[1 + count + k] = last
    late_ref[0] = count


def volume_kernel(state_ref, metric_ref, rate_ref, rows_ref, tensor_ref, flux_ref):
    spread_nodes(state_ref, rows_ref)
    for direction in range(3):
        for half in range(2):
            for block in range(BLOCKS):
                tensor_ref[pl.ds(direction * 24 + half * 4 + block, 3, stride=8), :] = metric_ref[
                    direction, :, block * LANES : (block + 1) * LANES
                ]

    def fluxes(step, carry):
        at = pl.multiple_of(step * 8, 8)
        density, mom_x, mom_y, mom_z, energy = [
            rows_ref[pl.ds(v * 256 + at, 8), :] for v in range(5)
        ]
        inverse = 1.0 / density
        momentum = [mom_x, mom_y, mom_z]
        velocity = [m * inverse for m in momentum]
        pressure = (HEAT_RATIO - 1.0) * (
            energy
            - 0.5 * (mom_x * velocity[0] + mom_y * velocity[1] + mom_z * velocity[2])
        )
        enthalpy = energy + pressure
        for direction in range(3):
            tensor = [tensor_ref[direction * 24 + k * 8 : direction * 24 + k * 8 + 8, :] for k in range(3)]
            along = tensor[0] * velocity[0] + tensor[1] * velocity[1] + tensor[2] * velocity[2]
            values = [density * along]
            values += [momentum[k] * along + pressure * tensor[k] for k in range(3)]
            values += [enthalpy * along]
            for v in range(5):
                flux_ref[direction, pl.ds(v * 256 + at, 8), :] = values[v]
        return carry

    lax.fori_loop(0, 32, fluxes, 0)
    matrix = derivative_matrix()
    upper = lax.broadcasted_iota(jnp.int32, (8, LANES), 0) < 4

    def pair(first, second):
        return jnp.where(upper, jnp.float32(first), jnp.float32(second))

    straight = [[pair(matrix[2 * t, 2 * s], matrix[2 * t + 1, 2 * s + 1]) for s in range(2)] for t in range(2)]
    crossed = [[pair(matrix[2 * t, 2 * s + 1], matrix[2 * t + 1, 2 * s]) for s in range(2)] for t in range(2)]

    def combine(values, target):
        total = values[0] * float(matrix[target, 0])
        for source in range(1, 4):
            total = total + values[source] * float(matrix[target, source])
        return total

    def diverge(v, carry):
        base = pl.multiple_of(v * 256, 256)
        for rest in range(8):
            values = [flux_ref[0, pl.ds(base + a * 64 + rest * 8, 8), :] for a in range(4)]
            for a in range(4):
                rate_ref[pl.ds(base + a * 64 + rest * 8, 8), :] = -combine(values, a)
        for a in range(4):
            for half in range(2):
                values = [flux_ref[1, pl.ds(base + a * 64 + b * 16 + half * 8, 8), :] for b in range(4)]
                third = [flux_ref[2, pl.ds(base + a * 64 + b * 16 + half * 8, 8), :] for b in range(4)]
                other = [flux_ref[2, pl.ds(base + a * 64 + b * 16 + (1 - half) * 8, 8), :] for b in range(4)]
                for b in range(4):
                    at = pl.ds(base + a * 64 + b * 16 + half * 8, 8)
                    same, far = third[b], other[b]
                    total = combine(values, b)
                    total = total + straight[half][half] * same
                    total = total + crossed[half][half] * pltpu.roll(same, 4, 0)
                    total = total + straight[half][1 - half] * far
                    total = total + crossed[half][1 - half] * pltpu.roll(far, 4, 0)
                    rate_ref[at, :] = rate_ref[at, :] - total
        return carry

    lax.fori_loop(0, 5, diverge, 0)


def normal_flux(values, normal, length):
    density, momentum, energy = values[0], values[1:4], values[4]
    inverse = 1.0 / density
    velocity = [m * inverse for m in momentum]
    pressure = (HEAT_RATIO - 1.0) * (
        energy
        - 0.5 * (momentum[0] * velocity[0] + momentum[1] * velocity[1] + momentum[2] * velocity[2])
    )
    speed = velocity[0] * normal[0] + velocity[1] * normal[1] + velocity[2] * normal[2]
    terms = [density * speed]
    terms += [momentum[k] * speed + pressure * normal[k] for k in range(3)]
    terms += [(energy + pressure) * speed]
    wave = jnp.abs(speed) + jnp.sqrt(HEAT_RATIO * pressure * inverse) * length
    return terms, wave


def finish_kernel(
    place_ref,
    partner_ref,
    late_ref,
    early_ref,
    own_ref,
    relay_ref,
    code_ref,
    normal_ref,
    rate_in_ref,
    state_ref,
    register_ref,
    section_ref,
    advanced_ref,
    board_ref,
    picked_ref,
    other_ref,
    turned_ref,
    side_ref,
    rate_ref,
):
    plane, spot = place_ref[0], place_ref[1]
    picked_ref[0:COLUMNS, :] = early_ref[...]
    rate_ref[...] = rate_in_ref[...]

    def receive(block, peer):
        rows = expand([relay_ref[block, 8 * k : 8 * k + 8, :] for k in range(5)])
        base = pl.multiple_of(peer * SLOTS, SLOTS)
        for k in range(8):
            board_ref[pl.ds(base + 8 * k, 8), :] = rows[k]

    def receive_low(step, carry):
        for k in range(4):
            block = NEAR + step * 4 + k
            receive(block, (plane - 1) * PLANE + block + MARGIN)
        return carry

    def receive_high(step, carry):
        for k in range(4):
            block = step * 4 + k
            receive(block, (plane + 1) * PLANE + block + MARGIN)
        return carry

    lax.fori_loop(spot // 4, CROSS // 4, receive_low, 0)
    lax.fori_loop(0, (jnp.maximum(spot - NEAR + 1, 0) + 3) // 4, receive_high, 0)
    shift = MARGIN * SLOTS - COLUMNS

    def gather(step, carry):
        base = 1 + step * UNROLL
        for k in range(UNROLL):
            column = late_ref[base + k]
            picked_ref[pl.ds(column, 1), :] = board_ref[pl.ds(partner_ref[column] + shift, 1), :]
        return carry

    lax.fori_loop(0, (late_ref[0] + UNROLL - 1) // UNROLL, gather, 0)
    for place in range(COLUMNS // LANES):
        square = picked_ref[place * LANES : (place + 1) * LANES, :].T
        other_ref[place * TRACE : (place + 1) * TRACE, :] = square[0:TRACE]
        side_ref[pl.ds(place, 3, stride=24), :] = normal_ref[:, place * LANES : (place + 1) * LANES]

    for group in range(3):
        code = code_ref[group * 8 : group * 8 + 8, :]
        flip_first = code % 2 == 1
        flip_second = (code // 2) % 2 == 1
        swapped = code >= 4
        start = group * 8 * TRACE
        for v in range(5):
            grid = [
                [other_ref[pl.ds(start + v * 16 + i * 4 + j, 8, stride=TRACE), :] for j in range(4)]
                for i in range(4)
            ]
            grid = [[jnp.where(flip_first, grid[3 - i][j], grid[i][j]) for j in range(4)] for i in range(4)]
            grid = [[jnp.where(flip_second, grid[i][3 - j], grid[i][j]) for j in range(4)] for i in range(4)]
            for i in range(4):
                for j in range(4):
                    value = grid[i][j] if i == j else jnp.where(swapped, grid[j][i], grid[i][j])
                    at = ((i * 4 + j) * 5 + v) * 8
                    turned_ref[at : at + 8, :] = value
        normal = [side_ref[k * 24 + group * 8 : k * 24 + group * 8 + 8, :] for k in range(3)]
        length = jnp.sqrt(normal[0] * normal[0] + normal[1] * normal[1] + normal[2] * normal[2])
        first_nodes = face_nodes(2 * group)
        second_nodes = face_nodes(2 * group + 1)
        for node in range(16):
            own = [own_ref[pl.ds(start + v * 16 + node, 8, stride=TRACE), :] for v in range(5)]
            far = [turned_ref[(node * 5 + v) * 8 : (node * 5 + v) * 8 + 8, :] for v in range(5)]
            own_terms, own_wave = normal_flux(own, normal, length)
            far_terms, far_wave = normal_flux(far, normal, length)
            bound = jnp.maximum(own_wave, far_wave)
            viscous = bound + length
            for v in range(5):
                weight = bound if v == 0 else viscous
                surface = (0.5 * LIFT_FACTOR) * (
                    own_terms[v] - far_terms[v] + weight * (far[v] - own[v])
                )
                at = v * 256 + first_nodes[node] * 4
                rate_ref[at : at + 4, :] = rate_ref[at : at + 4, :] + surface[0:4]
                at = v * 256 + second_nodes[node] * 4
                rate_ref[at : at + 4, :] = rate_ref[at : at + 4, :] + surface[4:8]

    top = jnp.max(jnp.max(relay_ref[:, MESSAGE:, :], axis=0))
    scale = CFL_NUMBER / top * SECTION_STEP
    for v in range(5):
        for tile in range(8):
            for block in range(BLOCKS):
                nodes, lanes = slice(tile * 8, tile * 8 + 8), tile_lanes(block)
                rate = rate_ref[pl.ds(v * 256 + tile * 32 + block, 8, stride=BLOCKS), :]
                section = SECTION_KEEP * register_ref[v, nodes, lanes] + rate
                section_ref[v, nodes, lanes] = section
                advanced_ref[v, nodes, lanes] = state_ref[v, nodes, lanes] + scale * section


def smem():
    return pl.BlockSpec(memory_space=pltpu.SMEM)


def vmem():
    return pl.BlockSpec(memory_space=pltpu.VMEM)


def params():
    return pltpu.CompilerParams(vmem_limit_bytes=VMEM_LIMIT)


def shape(*sizes):
    return jax.ShapeDtypeStruct(sizes, jnp.float32)


def scratch(*sizes):
    return pltpu.VMEM(sizes, jnp.float32)


def pack(place, partner, state):
    return pl.pallas_call(
        pack_kernel,
        out_shape=(
            shape(COLUMNS // LANES * TRACE, LANES),
            shape(COLUMNS, LANES),
            shape(PLANE * MESSAGE, LANES),
            shape(CROSS * MESSAGE + 8, LANES),
            shape(CROSS * MESSAGE + 8, LANES),
            shape(8, LANES),
        ),
        in_specs=[smem(), smem(), vmem()],
        out_specs=(vmem(),) * 6,
        scratch_shapes=[scratch(COLUMNS + (DEVICES + CROSS) * SLOTS, LANES), scratch(1280, LANES)],
        compiler_params=params(),
        name="pack",
    )(place, partner, state)


def volume(state, metric):
    return pl.pallas_call(
        volume_kernel,
        out_shape=shape(1280, LANES),
        in_specs=[vmem(), vmem()],
        out_specs=vmem(),
        scratch_shapes=[scratch(1280, LANES), scratch(72, LANES), scratch(3, 1280, LANES)],
        compiler_params=params(),
        name="volume",
    )(state, metric)


def relay(place, up, down, best, far):
    return pl.pallas_call(
        relay_kernel,
        out_shape=shape(PLANE, MESSAGE + 8, LANES),
        in_specs=[smem()] + [vmem()] * 4,
        out_specs=vmem(),
        compiler_params=params(),
        name="relay",
    )(place, up, down, best, far)


def early(place, partner, table, plane):
    return pl.pallas_call(
        early_kernel,
        out_shape=(
            shape(COLUMNS, LANES),
            jax.ShapeDtypeStruct((COLUMNS + 1 + UNROLL,), jnp.int32),
        ),
        in_specs=[smem(), smem(), vmem(), vmem()],
        out_specs=(vmem(), smem()),
        scratch_shapes=[scratch(COLUMNS + DEVICES * SLOTS, LANES)],
        compiler_params=params(),
        name="early",
    )(place, partner, table, plane)


def finish(place, partner, late, picked, own, relayed, code, normal, rate, state, register):
    return pl.pallas_call(
        finish_kernel,
        out_shape=(shape(5, 64, ELEMENTS), shape(5, 64, ELEMENTS)),
        in_specs=[smem(), smem(), smem()] + [vmem()] * 8,
        out_specs=(vmem(), vmem()),
        scratch_shapes=[
            scratch((DEVICES + 2 * MARGIN) * SLOTS, LANES),
            scratch(COLUMNS, LANES),
            scratch(COLUMNS // LANES * TRACE, LANES),
            scratch(16 * 5 * 8, LANES),
            scratch(72, LANES),
            scratch(1280, LANES),
        ],
        compiler_params=params(),
        name="finish",
    )(place, partner, late, picked, own, relayed, code, normal, rate, state, register)


def along_y(value, steps):
    return lax.ppermute(value, "y", [(i, (i + steps) % 4) for i in range(4)])


def on_device(state, register, metric, face_normal, partner, flip_code, face_role, send_face):
    plane = lax.axis_index("y").astype(jnp.int32)
    spot = lax.axis_index(("r", "x")).astype(jnp.int32)
    place = jnp.stack([plane, spot])
    state = state.transpose(1, 0, 2)
    own, table, in_plane, up, down, best = pack(place, partner, state)
    from_below = along_y(up, 1)
    from_above = along_y(down, -1)
    far = along_y(best, 2)
    got = lax.all_to_all(in_plane, ("r", "x"), 0, 0, tiled=True)
    rate = volume(state, metric)
    relayed = relay(place, from_below, from_above, best, far)
    relayed = lax.all_to_all(relayed, ("r", "x"), 0, 0, tiled=True)
    picked, late = early(place, partner, table, got)
    code = flip_code.reshape(COLUMNS // LANES, LANES)
    section, advanced = finish(
        place, partner, late, picked, own, relayed, code, face_normal, rate, state, register.transpose(1, 0, 2)
    )
    return section.transpose(1, 0, 2), advanced.transpose(1, 0, 2)


def solution(mesh):
    placed = (
        P(None, None, AXES),
        P(None, None, AXES),
        P(None, None, AXES),
        P(None, AXES),
        P(AXES),
        P(AXES),
        P(AXES),
        P(AXES, None, None),
    )
    return jax.shard_map(
        on_device,
        mesh=Mesh(mesh.devices.reshape(4, 8, 4), AXES),
        in_specs=placed,
        out_specs=(P(None, None, AXES), P(None, None, AXES)),
        check_vma=False,
    )
```

```python
import jax
import jax.numpy as jnp
import numpy as np
from jax import lax
from jax.experimental import pallas as pl
from jax.experimental.pallas import tpu as pltpu
from jax.sharding import Mesh
from jax.sharding import PartitionSpec as P

HEAT_RATIO = 1.4
LIFT_FACTOR = 6.0
CFL_NUMBER = 0.3
SECTION_KEEP = -0.4178904745
SECTION_STEP = 0.4432226
DEVICES = 128
ELEMENTS = 512
COLUMNS = 6 * ELEMENTS
SLOTS = 64
REACH = 24
LANES = 128
BLOCKS = ELEMENTS // LANES
TRACE = 80
GROUP = COLUMNS // 3
MESSAGE = TRACE * SLOTS // LANES
UNROLL = 32
BATCH = 4
AXES = ("y", "r", "x")
PLANE = 32
NEAR = PLANE - REACH
CROSS = REACH
MARGIN = CROSS
VMEM_LIMIT = 24 * 1024 * 1024


def derivative_matrix():
    points = np.array([-1.0, -1.0 / np.sqrt(5.0), 1.0 / np.sqrt(5.0), 1.0])
    weights = np.array(
        [
            1.0
            / np.prod([points[target] - points[source] for source in range(4) if source != target])
            for target in range(4)
        ]
    )
    matrix = np.zeros((4, 4))
    for target in range(4):
        for source in range(4):
            if target != source:
                matrix[target, source] = (
                    weights[source] / weights[target] / (points[target] - points[source])
                )
        matrix[target, target] = -np.sum(matrix[target])
    return matrix


def face_nodes(face):
    side = 3 * (face % 2)
    if face < 2:
        return [side * 16 + i * 4 + j for i in range(4) for j in range(4)]
    if face < 4:
        return [i * 16 + side * 4 + j for i in range(4) for j in range(4)]
    return [i * 16 + j * 4 + side for i in range(4) for j in range(4)]


def tile_lanes(block):
    return slice(block * LANES, (block + 1) * LANES)


def spread_nodes(state_ref, rows_ref):
    for v in range(5):
        for tile in range(8):
            for block in range(BLOCKS):
                rows_ref[pl.ds(v * 256 + tile * 32 + block, 8, stride=BLOCKS), :] = state_ref[
                    v, tile * 8 : tile * 8 + 8, tile_lanes(block)
                ]


def face_rows(state_ref, flat_ref, v, face, block):
    side = 3 * (face % 2)
    lanes = tile_lanes(block)
    if face < 2:
        return state_ref[v, side * 16 : side * 16 + 16, lanes]
    if face < 4:
        return jnp.concatenate(
            [state_ref[v, i * 16 + side * 4 : i * 16 + side * 4 + 4, lanes] for i in range(4)], axis=0
        )
    return flat_ref[pl.ds(block * 320 + v * 64 + side, 16, stride=4), :]


def lane_index(shape):
    return lax.broadcasted_iota(jnp.int32, shape, 1)


def compact(rows):
    lane = lane_index((8, LANES))
    low = lane < 80
    mid = lane < 112

    def turn(value, shift):
        return pltpu.roll(value, shift, 1)

    first = [jnp.where(low, rows[k], turn(rows[5 + k], 80)) for k in range(3)]
    fourth = jnp.where(low, rows[3], jnp.where(mid, turn(rows[5], 32), turn(rows[7], 64)))
    fifth = jnp.where(low, rows[4], jnp.where(mid, turn(rows[6], 32), turn(rows[7], 48)))
    return first + [fourth, fifth]


def expand(parts):
    lane = lane_index((8, LANES))
    head = lane < 48
    body = lane < 64

    def turn(value, shift):
        return pltpu.roll(value, shift, 1)

    sixth = jnp.where(head, turn(parts[0], 48), turn(parts[3], 96))
    seventh = jnp.where(head, turn(parts[1], 48), turn(parts[4], 96))
    eighth = jnp.where(
        head, turn(parts[2], 48), jnp.where(body, turn(parts[3], 64), turn(parts[4], 80))
    )
    return list(parts) + [sixth, seventh, eighth]


def compact_into(board_ref, base, to_ref, at):
    rows = [board_ref[pl.ds(base + 8 * k, 8), :] for k in range(8 * BATCH)]
    parts = []
    for block in range(BATCH):
        parts += compact(rows[8 * block : 8 * block + 8])
    for k in range(5 * BATCH):
        to_ref[pl.ds(at + 8 * k, 8), :] = parts[k]


def expand_into(from_ref, start, board_ref, base):
    parts = [from_ref[pl.ds(start + 8 * k, 8), :] for k in range(5 * BATCH)]
    rows = []
    for block in range(BATCH):
        rows += expand(parts[5 * block : 5 * block + 5])
    for k in range(8 * BATCH):
        board_ref[pl.ds(base + 8 * k, 8), :] = rows[k]


def spread_flat(state_ref, flat_ref):
    for block in range(BLOCKS):
        for v in range(5):
            at = block * 320 + v * 64
            flat_ref[at : at + 64, :] = state_ref[v, :, tile_lanes(block)]


def face_trace(state_ref, flat_ref, face, block):
    return jnp.concatenate([face_rows(state_ref, flat_ref, v, face, block) for v in range(5)], axis=0)


def build_tables(state_ref, flat_ref, table_ref):
    spread_flat(state_ref, flat_ref)
    padding = jnp.zeros((LANES - TRACE, LANES), jnp.float32)
    for face in range(6):
        for block in range(BLOCKS):
            trace = face_trace(state_ref, flat_ref, face, block)
            place = face * BLOCKS + block
            square = jnp.concatenate([trace, padding], axis=0)
            table_ref[place * LANES : (place + 1) * LANES, :] = square.T


def pack_kernel(
    place_ref,
    partner_hbm,
    state_hbm,
    plane_ref,
    up_ref,
    down_ref,
    best_ref,
    partner_ref,
    state_ref,
    table_ref,
    board_ref,
    flat_ref,
    sems,
):
    copies = [pltpu.make_async_copy(partner_hbm, partner_ref, sems.at[0])]
    for a in range(4):
        nodes = pl.ds(a * 16, 16)
        copies.append(
            pltpu.make_async_copy(state_hbm.at[:, nodes, :], state_ref.at[:, nodes, :], sems.at[1 + a])
        )
    for copy in copies:
        copy.start()
    for copy in copies[1:]:
        copy.wait()
    build_tables(state_ref, flat_ref, table_ref)
    copies[0].wait()

    def scatter(step, carry):
        base = step * UNROLL
        targets = [partner_ref[base + k] for k in range(UNROLL)]
        rows = [table_ref[pl.ds(base + k, 1), :] for k in range(UNROLL)]
        for k in range(UNROLL):
            board_ref[pl.ds(targets[k], 1), :] = rows[k]
        return carry

    lax.fori_loop(0, COLUMNS // UNROLL, scatter, 0)

    def speeds(step, best):
        density, mom_x, mom_y, mom_z, energy = [
            state_ref[v, pl.ds(pl.multiple_of(step * 8, 8), 8), :] for v in range(5)
        ]
        inverse = 1.0 / density
        square = (mom_x * mom_x + mom_y * mom_y + mom_z * mom_z) * inverse
        pressure = (HEAT_RATIO - 1.0) * (energy - 0.5 * square)
        wave = jnp.sqrt(square * inverse) + jnp.sqrt(HEAT_RATIO * pressure * inverse)
        return jnp.maximum(best, wave)

    best = lax.fori_loop(0, 8, speeds, jnp.zeros((8, ELEMENTS), jnp.float32))
    best = jnp.maximum(
        jnp.maximum(best[:, tile_lanes(0)], best[:, tile_lanes(1)]),
        jnp.maximum(best[:, tile_lanes(2)], best[:, tile_lanes(3)]),
    )
    best_ref[...] = best
    up_ref[CROSS * MESSAGE :, :] = best
    down_ref[CROSS * MESSAGE :, :] = best
    plane, spot = place_ref[0], place_ref[1]

    def send(to_ref, peer, step):
        base = pl.multiple_of(COLUMNS + (peer + step * BATCH) * SLOTS, SLOTS)
        compact_into(board_ref, base, to_ref, pl.multiple_of(step * BATCH * MESSAGE, 8))

    def send_up(step, carry):
        send(up_ref, (plane + 1) * PLANE, step)
        return carry

    def send_down(step, carry):
        send(down_ref, (plane - 1) * PLANE + NEAR, step)
        return carry

    lax.fori_loop(0, (jnp.maximum(spot - NEAR + 1, 0) + BATCH - 1) // BATCH, send_up, 0)
    lax.fori_loop(spot // BATCH, CROSS // BATCH, send_down, 0)
    base = pl.multiple_of(COLUMNS + plane * (PLANE * SLOTS), SLOTS)
    plane_ref[...] = board_ref[pl.ds(base, PLANE * SLOTS), :]


def pack_plane_kernel(board_ref, plane_hbm, plane_ref, sems):
    copies = []
    for step in range(PLANE // BATCH):
        rows = BATCH * MESSAGE
        compact_into(board_ref, step * BATCH * SLOTS, plane_ref, step * rows)
        part = pl.ds(step * rows, rows)
        copies.append(
            pltpu.make_async_copy(plane_ref.at[part, :], plane_hbm.at[part, :], sems.at[step])
        )
        copies[-1].start()
    for copy in copies:
        copy.wait()


def relay_kernel(place_ref, up_ref, down_ref, best_ref, far_ref, rate_hbm, relay_ref):
    top = jnp.maximum(
        jnp.maximum(best_ref[...], far_ref[...]),
        jnp.maximum(up_ref[CROSS * MESSAGE :, :], down_ref[CROSS * MESSAGE :, :]),
    )
    spot = place_ref[1]
    for block in range(PLANE):
        relay_ref[block, MESSAGE:, :] = top

    def from_up(block, carry):
        for k in range(5):
            at = pl.multiple_of(block * MESSAGE + 8 * k, 8)
            relay_ref[block, 8 * k : 8 * k + 8, :] = up_ref[pl.ds(at, 8), :]
        return carry

    def from_down(block, carry):
        for k in range(5):
            at = pl.multiple_of(block * MESSAGE + 8 * k, 8)
            relay_ref[block + NEAR, 8 * k : 8 * k + 8, :] = down_ref[pl.ds(at, 8), :]
        return carry

    lax.fori_loop(0, jnp.maximum(spot - NEAR + 1, 0), from_up, 0)
    lax.fori_loop(spot, CROSS, from_down, 0)


def early_kernel(
    place_ref,
    partner_ref,
    blank_hbm,
    state_ref,
    plane_ref,
    picked_ref,
    owner_ref,
    board_ref,
    flat_ref,
    sem,
):
    plane, spot = place_ref[0], place_ref[1]
    blank = pltpu.make_async_copy(blank_hbm, owner_ref, sem)
    blank.start()
    build_tables(state_ref, flat_ref, board_ref)

    def receive(step, carry):
        start = pl.multiple_of(step * BATCH * MESSAGE, 8)
        base = pl.multiple_of(COLUMNS + (plane * PLANE + step * BATCH) * SLOTS, SLOTS)
        expand_into(plane_ref, start, board_ref, base)
        return carry

    lax.fori_loop(jnp.maximum(spot - REACH, 0) // BATCH, PLANE // BATCH, receive, 0)

    def gather(step, carry):
        base = step * UNROLL
        indices = [partner_ref[base + k] for k in range(UNROLL)]
        rows = [board_ref[pl.ds(index, 1), :] for index in indices]
        for k in range(UNROLL):
            picked_ref[pl.ds(base + k, 1), :] = rows[k]
            owner_ref[indices[k]] = base + k
        return carry

    blank.wait()
    lax.fori_loop(0, COLUMNS // UNROLL, gather, 0)


def spread_normals(normal_ref, side_ref):
    for place in range(COLUMNS // LANES):
        side_ref[pl.ds(place, 3, stride=24), :] = normal_ref[:, place * LANES : (place + 1) * LANES]


def group_normal(side_ref, group):
    normal = [side_ref[k * 24 + group * 8 : k * 24 + group * 8 + 8, :] for k in range(3)]
    length = jnp.sqrt(normal[0] * normal[0] + normal[1] * normal[1] + normal[2] * normal[2])
    return normal, length


def lift(rate_ref, group, node, terms):
    first, second = face_nodes(2 * group)[node], face_nodes(2 * group + 1)[node]
    for v in range(5):
        at = v * 256 + first * 4
        rate_ref[at : at + 4, :] = rate_ref[at : at + 4, :] + terms[v][0:4]
        at = v * 256 + second * 4
        rate_ref[at : at + 4, :] = rate_ref[at : at + 4, :] + terms[v][4:8]


def volume_kernel(
    state_ref,
    register_ref,
    metric_ref,
    normal_ref,
    rate_ref,
    own_ref,
    wave_ref,
    rows_ref,
    tensor_ref,
    flux_ref,
    flat_ref,
    side_ref,
):
    spread_nodes(state_ref, rows_ref)
    spread_flat(state_ref, flat_ref)
    spread_normals(normal_ref, side_ref)
    for face in range(6):
        for block in range(BLOCKS):
            place = face * BLOCKS + block
            own_ref[place * TRACE : (place + 1) * TRACE, :] = face_trace(state_ref, flat_ref, face, block)
    for direction in range(3):
        for half in range(2):
            for block in range(BLOCKS):
                tensor_ref[pl.ds(direction * 24 + half * 4 + block, 3, stride=8), :] = metric_ref[
                    direction, :, block * LANES : (block + 1) * LANES
                ]

    def fluxes(step, carry):
        at = pl.multiple_of(step * 8, 8)
        density, mom_x, mom_y, mom_z, energy = [
            rows_ref[pl.ds(v * 256 + at, 8), :] for v in range(5)
        ]
        inverse = 1.0 / density
        momentum = [mom_x, mom_y, mom_z]
        velocity = [m * inverse for m in momentum]
        pressure = (HEAT_RATIO - 1.0) * (
            energy
            - 0.5 * (mom_x * velocity[0] + mom_y * velocity[1] + mom_z * velocity[2])
        )
        enthalpy = energy + pressure
        for direction in range(3):
            tensor = [tensor_ref[direction * 24 + k * 8 : direction * 24 + k * 8 + 8, :] for k in range(3)]
            along = tensor[0] * velocity[0] + tensor[1] * velocity[1] + tensor[2] * velocity[2]
            values = [density * along]
            values += [momentum[k] * along + pressure * tensor[k] for k in range(3)]
            values += [enthalpy * along]
            for v in range(5):
                flux_ref[direction, pl.ds(v * 256 + at, 8), :] = values[v]
        return carry

    lax.fori_loop(0, 32, fluxes, 0)
    matrix = derivative_matrix()
    upper = lax.broadcasted_iota(jnp.int32, (8, LANES), 0) < 4

    def pair(first, second):
        return jnp.where(upper, jnp.float32(first), jnp.float32(second))

    straight = [[pair(matrix[2 * t, 2 * s], matrix[2 * t + 1, 2 * s + 1]) for s in range(2)] for t in range(2)]
    crossed = [[pair(matrix[2 * t, 2 * s + 1], matrix[2 * t + 1, 2 * s]) for s in range(2)] for t in range(2)]

    def combine(values, target):
        total = values[0] * float(matrix[target, 0])
        for source in range(1, 4):
            total = total + values[source] * float(matrix[target, source])
        return total

    def diverge(v, carry):
        base = pl.multiple_of(v * 256, 256)
        for rest in range(8):
            values = [flux_ref[0, pl.ds(base + a * 64 + rest * 8, 8), :] for a in range(4)]
            for a in range(4):
                rate_ref[pl.ds(base + a * 64 + rest * 8, 8), :] = -combine(values, a)
        for a in range(4):
            for half in range(2):
                values = [flux_ref[1, pl.ds(base + a * 64 + b * 16 + half * 8, 8), :] for b in range(4)]
                third = [flux_ref[2, pl.ds(base + a * 64 + b * 16 + half * 8, 8), :] for b in range(4)]
                other = [flux_ref[2, pl.ds(base + a * 64 + b * 16 + (1 - half) * 8, 8), :] for b in range(4)]
                for b in range(4):
                    at = pl.ds(base + a * 64 + b * 16 + half * 8, 8)
                    same, far = third[b], other[b]
                    total = combine(values, b)
                    total = total + straight[half][half] * same
                    total = total + crossed[half][half] * pltpu.roll(same, 4, 0)
                    total = total + straight[half][1 - half] * far
                    total = total + crossed[half][1 - half] * pltpu.roll(far, 4, 0)
                    rate_ref[at, :] = rate_ref[at, :] - total
        return carry

    lax.fori_loop(0, 5, diverge, 0)
    for group in range(3):
        normal, length = group_normal(side_ref, group)
        start = group * 8 * TRACE
        for node in range(16):
            own = [own_ref[pl.ds(start + v * 16 + node, 8, stride=TRACE), :] for v in range(5)]
            terms, wave = normal_flux(own, normal, length)
            lift(rate_ref, group, node, [(0.5 * LIFT_FACTOR) * term for term in terms])
            at = (group * 16 + node) * 8
            wave_ref[at : at + 8, :] = wave
    for v in range(5):
        for tile in range(8):
            for block in range(BLOCKS):
                at = pl.ds(v * 256 + tile * 32 + block, 8, stride=BLOCKS)
                old = register_ref[v, tile * 8 : tile * 8 + 8, tile_lanes(block)]
                rate_ref[at, :] = rate_ref[at, :] + SECTION_KEEP * old


def normal_flux(values, normal, length):
    density, momentum, energy = values[0], values[1:4], values[4]
    inverse = 1.0 / density
    velocity = [m * inverse for m in momentum]
    pressure = (HEAT_RATIO - 1.0) * (
        energy
        - 0.5 * (momentum[0] * velocity[0] + momentum[1] * velocity[1] + momentum[2] * velocity[2])
    )
    speed = velocity[0] * normal[0] + velocity[1] * normal[1] + velocity[2] * normal[2]
    terms = [density * speed]
    terms += [momentum[k] * speed + pressure * normal[k] for k in range(3)]
    terms += [(energy + pressure) * speed]
    wave = jnp.abs(speed) + jnp.sqrt(HEAT_RATIO * pressure * inverse) * length
    return terms, wave


def finish_kernel(
    place_ref,
    owner_hbm,
    early_hbm,
    own_hbm,
    wave_hbm,
    relay_ref,
    code_ref,
    normal_ref,
    rate_hbm,
    state_hbm,
    section_hbm,
    advanced_hbm,
    owner_ref,
    section_ref,
    advanced_ref,
    board_ref,
    picked_ref,
    other_ref,
    turned_ref,
    side_ref,
    rate_ref,
    own_ref,
    wave_ref,
    state_ref,
    sems,
):
    plane, spot = place_ref[0], place_ref[1]
    window = CROSS * SLOTS
    low_slot = jnp.maximum(COLUMNS + ((plane - 1) * PLANE + NEAR) * SLOTS, 0)
    high_slot = jnp.minimum(COLUMNS + (plane + 1) * PLANE * SLOTS, COLUMNS + DEVICES * SLOTS - window)
    sources = [
        (owner_hbm.at[pl.ds(pl.multiple_of(low_slot, 512), window)], owner_ref.at[0]),
        (owner_hbm.at[pl.ds(pl.multiple_of(high_slot, 512), window)], owner_ref.at[1]),
    ]
    for part in range(3):
        rows = pl.ds(part * GROUP, GROUP)
        sources.append((early_hbm.at[rows, :], picked_ref.at[rows, :]))
    for part in range(3):
        rows = pl.ds(part * 8 * TRACE, 8 * TRACE)
        sources.append((own_hbm.at[rows, :], own_ref.at[rows, :]))
    sources += [(wave_hbm, wave_ref), (rate_hbm, rate_ref), (state_hbm, state_ref)]
    copies = [
        pltpu.make_async_copy(source, target, sems.at[k])
        for k, (source, target) in enumerate(sources)
    ]
    for copy in copies:
        copy.start()
    spread_normals(normal_ref, side_ref)

    def receive(peer, block):
        parts = [relay_ref[block + k // 5, 8 * (k % 5) : 8 * (k % 5) + 8, :] for k in range(5 * BATCH)]
        rows = []
        for k in range(BATCH):
            rows += expand(parts[5 * k : 5 * k + 5])
        base = pl.multiple_of((peer + block + MARGIN) * SLOTS, SLOTS)
        for k in range(8 * BATCH):
            board_ref[pl.ds(base + 8 * k, 8), :] = rows[k]

    def receive_low(step, carry):
        receive((plane - 1) * PLANE, NEAR + step * BATCH)
        return carry

    def receive_high(step, carry):
        receive((plane + 1) * PLANE, step * BATCH)
        return carry

    lax.fori_loop(spot // BATCH, CROSS // BATCH, receive_low, 0)
    high = (jnp.maximum(spot - NEAR + 1, 0) + BATCH - 1) // BATCH
    lax.fori_loop(0, high, receive_high, 0)

    def place_rows(side, base, step):
        at = step * UNROLL
        columns = [owner_ref[side, at + k] for k in range(UNROLL)]
        rows = [board_ref[pl.ds(base * SLOTS + at + k, 1), :] for k in range(UNROLL)]
        for k in range(UNROLL):
            picked_ref[pl.ds(columns[k], 1), :] = rows[k]

    def place_low(step, carry):
        place_rows(0, (plane - 1) * PLANE + NEAR + MARGIN, step)
        return carry

    def place_high(step, carry):
        place_rows(1, (plane + 1) * PLANE + MARGIN, step)
        return carry

    chunk = SLOTS // UNROLL
    for copy in copies[:5]:
        copy.wait()

    @pl.when(plane > 0)
    def _():
        lax.fori_loop(spot * chunk, CROSS * chunk, place_low, 0)

    @pl.when(plane < 3)
    def _():
        lax.fori_loop(0, jnp.maximum(spot - NEAR + 1, 0) * chunk, place_high, 0)

    for place in range(COLUMNS // LANES):
        square = picked_ref[place * LANES : (place + 1) * LANES, :].T
        other_ref[place * TRACE : (place + 1) * TRACE, :] = square[0:TRACE]
    for copy in copies[5:]:
        copy.wait()
    for group in range(3):
        code = code_ref[group * 8 : group * 8 + 8, :]
        flip_first = code % 2 == 1
        flip_second = (code // 2) % 2 == 1
        swapped = code >= 4
        start = group * 8 * TRACE
        for v in range(5):
            grid = [
                [other_ref[pl.ds(start + v * 16 + i * 4 + j, 8, stride=TRACE), :] for j in range(4)]
                for i in range(4)
            ]
            grid = [[jnp.where(flip_first, grid[3 - i][j], grid[i][j]) for j in range(4)] for i in range(4)]
            grid = [[jnp.where(flip_second, grid[i][3 - j], grid[i][j]) for j in range(4)] for i in range(4)]
            for i in range(4):
                for j in range(4):
                    value = grid[i][j] if i == j else jnp.where(swapped, grid[j][i], grid[i][j])
                    at = ((i * 4 + j) * 5 + v) * 8
                    turned_ref[at : at + 8, :] = value
        normal, length = group_normal(side_ref, group)
        for node in range(16):
            own = [own_ref[pl.ds(start + v * 16 + node, 8, stride=TRACE), :] for v in range(5)]
            far = [turned_ref[(node * 5 + v) * 8 : (node * 5 + v) * 8 + 8, :] for v in range(5)]
            far_terms, far_wave = normal_flux(far, normal, length)
            at = (group * 16 + node) * 8
            bound = jnp.maximum(wave_ref[at : at + 8, :], far_wave)
            viscous = bound + length
            terms = [
                (0.5 * LIFT_FACTOR)
                * ((bound if v == 0 else viscous) * (far[v] - own[v]) - far_terms[v])
                for v in range(5)
            ]
            lift(rate_ref, group, node, terms)

    top = jnp.max(jnp.max(relay_ref[:, MESSAGE:, :], axis=0))
    scale = CFL_NUMBER / top * SECTION_STEP
    results = []
    for v in range(5):
        for tile in range(8):
            for block in range(BLOCKS):
                nodes, lanes = slice(tile * 8, tile * 8 + 8), tile_lanes(block)
                section = rate_ref[pl.ds(v * 256 + tile * 32 + block, 8, stride=BLOCKS), :]
                section_ref[v, nodes, lanes] = section
                advanced_ref[v, nodes, lanes] = state_ref[v, nodes, lanes] + scale * section
        for source, target in ((section_ref, section_hbm), (advanced_ref, advanced_hbm)):
            results.append(pltpu.make_async_copy(source.at[v], target.at[v], sems.at[len(results)]))
            results[-1].start()
    for copy in results:
        copy.wait()


def smem():
    return pl.BlockSpec(memory_space=pltpu.SMEM)


def vmem():
    return pl.BlockSpec(memory_space=pltpu.VMEM)


def params():
    return pltpu.CompilerParams(vmem_limit_bytes=VMEM_LIMIT)


def shape(*sizes):
    return jax.ShapeDtypeStruct(sizes, jnp.float32)


def scratch(*sizes):
    return pltpu.VMEM(sizes, jnp.float32)


def hbm():
    return pl.BlockSpec(memory_space=pltpu.HBM)


def anywhere():
    return pl.BlockSpec(memory_space=pl.ANY)


def pack(place, partner, state):
    return pl.pallas_call(
        pack_kernel,
        out_shape=(
            scratch(PLANE * SLOTS, LANES),
            shape(CROSS * MESSAGE + 8, LANES),
            shape(CROSS * MESSAGE + 8, LANES),
            shape(8, LANES),
        ),
        in_specs=[smem(), hbm(), hbm()],
        out_specs=(vmem(),) * 4,
        scratch_shapes=[
            pltpu.SMEM((COLUMNS,), jnp.int32),
            scratch(5, 64, ELEMENTS),
            scratch(COLUMNS, LANES),
            scratch(COLUMNS + (DEVICES + CROSS) * SLOTS, LANES),
            scratch(1280, LANES),
            pltpu.SemaphoreType.DMA((5,)),
        ],
        compiler_params=params(),
        name="pack",
    )(place, partner, state)


def pack_plane(board):
    return pl.pallas_call(
        pack_plane_kernel,
        out_shape=pltpu.HBM((PLANE * MESSAGE, LANES), jnp.float32),
        in_specs=[vmem()],
        out_specs=hbm(),
        scratch_shapes=[
            scratch(PLANE * MESSAGE, LANES),
            pltpu.SemaphoreType.DMA((PLANE // BATCH,)),
        ],
        compiler_params=params(),
        name="pack_plane",
    )(board)


def volume(state, register, metric, normal):
    return pl.pallas_call(
        volume_kernel,
        out_shape=(
            shape(1280, LANES),
            pltpu.HBM((COLUMNS // LANES * TRACE, LANES), jnp.float32),
            shape(COLUMNS // LANES * 16, LANES),
        ),
        in_specs=[vmem()] * 4,
        out_specs=(vmem(),) * 3,
        scratch_shapes=[
            scratch(1280, LANES),
            scratch(72, LANES),
            scratch(3, 1280, LANES),
            scratch(1280, LANES),
            scratch(72, LANES),
        ],
        compiler_params=params(),
        name="volume",
    )(state, register, metric, normal)


def relay(place, up, down, best, far, rate):
    return pl.pallas_call(
        relay_kernel,
        out_shape=shape(PLANE, MESSAGE + 8, LANES),
        in_specs=[smem()] + [vmem()] * 4 + [anywhere()],
        out_specs=vmem(),
        compiler_params=params(),
        cost_estimate=pl.CostEstimate(flops=100000000000, bytes_accessed=100000000, transcendentals=0),
        name="relay",
    )(place, up, down, best, far, rate)


def early(place, partner, blank, state, plane):
    return pl.pallas_call(
        early_kernel,
        out_shape=(
            pltpu.HBM((COLUMNS, LANES), jnp.float32),
            jax.ShapeDtypeStruct((COLUMNS + DEVICES * SLOTS,), jnp.int32),
        ),
        in_specs=[smem(), smem(), anywhere(), vmem(), vmem()],
        out_specs=(vmem(), smem()),
        scratch_shapes=[
            scratch(COLUMNS + DEVICES * SLOTS, LANES),
            scratch(1280, LANES),
            pltpu.SemaphoreType.DMA,
        ],
        compiler_params=params(),
        name="early",
    )(place, partner, blank, state, plane)


def finish(place, owner, picked, own, wave, relayed, code, normal, rate, state):
    return pl.pallas_call(
        finish_kernel,
        out_shape=(pltpu.HBM((5, 64, ELEMENTS), jnp.float32),) * 2,
        in_specs=[smem(), hbm(), hbm(), hbm(), anywhere(), vmem(), vmem(), vmem(), anywhere(), anywhere()],
        out_specs=(hbm(), hbm()),
        scratch_shapes=[
            pltpu.SMEM((2, CROSS * SLOTS), jnp.int32),
            scratch(5, 64, ELEMENTS),
            scratch(5, 64, ELEMENTS),
            scratch((DEVICES + 2 * MARGIN) * SLOTS, LANES),
            scratch(COLUMNS + 8, LANES),
            scratch(COLUMNS // LANES * TRACE, LANES),
            scratch(16 * 5 * 8, LANES),
            scratch(72, LANES),
            scratch(1280, LANES),
            scratch(COLUMNS // LANES * TRACE, LANES),
            scratch(COLUMNS // LANES * 16, LANES),
            scratch(5, 64, ELEMENTS),
            pltpu.SemaphoreType.DMA((11,)),
        ],
        compiler_params=params(),
        name="finish",
    )(place, owner, picked, own, wave, relayed, code, normal, rate, state)


def in_hbm(value):
    return pltpu.with_memory_space_constraint(value, pltpu.HBM)


def in_vmem(value):
    return pltpu.with_memory_space_constraint(value, pltpu.VMEM)


def along_y(value, steps):
    return lax.ppermute(value, "y", [(i, (i + steps) % 4) for i in range(4)])


def on_device(state, register, metric, face_normal, partner, flip_code, face_role, send_face):
    plane = lax.axis_index("y").astype(jnp.int32)
    spot = lax.axis_index(("r", "x")).astype(jnp.int32)
    place = jnp.stack([plane, spot])
    state = state.transpose(1, 0, 2)
    board, up, down, best = pack(place, in_hbm(partner), in_hbm(state))
    from_below = along_y(up, 1)
    from_above = along_y(down, -1)
    far = along_y(best, 2)
    in_plane = pack_plane(in_vmem(board))
    got = lax.all_to_all(in_plane, ("r", "x"), 0, 0, tiled=True)
    rate, own, wave = volume(state, register.transpose(1, 0, 2), metric, face_normal)
    relayed = relay(place, from_below, from_above, best, far, rate)
    relayed = lax.all_to_all(relayed, ("r", "x"), 0, 0, tiled=True)
    blank = jnp.full((COLUMNS + DEVICES * SLOTS,), COLUMNS, jnp.int32)
    picked, owner = early(place, partner, blank, state, got)
    code = flip_code.reshape(COLUMNS // LANES, LANES)
    section, advanced = finish(
        place, in_hbm(owner), in_hbm(picked), in_hbm(own), wave, relayed, code, face_normal, rate, state
    )
    return section.transpose(1, 0, 2), advanced.transpose(1, 0, 2)


def solution(mesh):
    placed = (
        P(None, None, AXES),
        P(None, None, AXES),
        P(None, None, AXES),
        P(None, AXES),
        P(AXES),
        P(AXES),
        P(AXES),
        P(AXES, None, None),
    )
    return jax.shard_map(
        on_device,
        mesh=Mesh(mesh.devices.reshape(4, 8, 4), AXES),
        in_specs=placed,
        out_specs=(P(None, None, AXES), P(None, None, AXES)),
        check_vma=False,
    )
```

```python
import jax
import jax.numpy as jnp
import numpy as np
from jax import lax
from jax.experimental import pallas as pl
from jax.experimental.pallas import tpu as pltpu
from jax.sharding import Mesh
from jax.sharding import PartitionSpec as P

HEAT_RATIO = 1.4
LIFT_FACTOR = 6.0
CFL_NUMBER = 0.3
SECTION_KEEP = -0.4178904745
SECTION_STEP = 0.4432226
DEVICES = 128
ELEMENTS = 512
COLUMNS = 6 * ELEMENTS
SLOTS = 64
REACH = 24
LANES = 128
BLOCKS = ELEMENTS // LANES
TRACE = 80
GROUP = COLUMNS // 3
MESSAGE = TRACE * SLOTS // LANES
UNROLL = 32
SIDE = 48
BATCH = 4
AXES = ("y", "r", "x")
PLANE = 32
NEAR = PLANE - REACH
CROSS = REACH
MARGIN = CROSS
VMEM_LIMIT = 24 * 1024 * 1024


def derivative_matrix():
    points = np.array([-1.0, -1.0 / np.sqrt(5.0), 1.0 / np.sqrt(5.0), 1.0])
    weights = np.array(
        [
            1.0
            / np.prod([points[target] - points[source] for source in range(4) if source != target])
            for target in range(4)
        ]
    )
    matrix = np.zeros((4, 4))
    for target in range(4):
        for source in range(4):
            if target != source:
                matrix[target, source] = (
                    weights[source] / weights[target] / (points[target] - points[source])
                )
        matrix[target, target] = -np.sum(matrix[target])
    return matrix


def face_nodes(face):
    side = 3 * (face % 2)
    if face < 2:
        return [side * 16 + i * 4 + j for i in range(4) for j in range(4)]
    if face < 4:
        return [i * 16 + side * 4 + j for i in range(4) for j in range(4)]
    return [i * 16 + j * 4 + side for i in range(4) for j in range(4)]


def tile_lanes(block):
    return slice(block * LANES, (block + 1) * LANES)


def spread_nodes(state_ref, rows_ref):
    for v in range(5):
        for tile in range(8):
            for block in range(BLOCKS):
                rows_ref[pl.ds(v * 256 + tile * 32 + block, 8, stride=BLOCKS), :] = state_ref[
                    v, tile * 8 : tile * 8 + 8, tile_lanes(block)
                ]


def face_rows(state_ref, flat_ref, v, face, block):
    side = 3 * (face % 2)
    lanes = tile_lanes(block)
    if face < 2:
        return state_ref[v, side * 16 : side * 16 + 16, lanes]
    if face < 4:
        return jnp.concatenate(
            [state_ref[v, i * 16 + side * 4 : i * 16 + side * 4 + 4, lanes] for i in range(4)], axis=0
        )
    return flat_ref[pl.ds(block * 320 + v * 64 + side, 16, stride=4), :]


def aligned(row):
    return row if isinstance(row, int) else pl.multiple_of(row, 8)


def lane_index(shape):
    return lax.broadcasted_iota(jnp.int32, shape, 1)


def compact(rows):
    lane = lane_index((8, LANES))
    low = lane < 80
    mid = lane < 112

    def turn(value, shift):
        return pltpu.roll(value, shift, 1)

    first = [jnp.where(low, rows[k], turn(rows[5 + k], 80)) for k in range(3)]
    fourth = jnp.where(low, rows[3], jnp.where(mid, turn(rows[5], 32), turn(rows[7], 64)))
    fifth = jnp.where(low, rows[4], jnp.where(mid, turn(rows[6], 32), turn(rows[7], 48)))
    return first + [fourth, fifth]


def expand(parts):
    lane = lane_index((8, LANES))
    head = lane < 48
    body = lane < 64

    def turn(value, shift):
        return pltpu.roll(value, shift, 1)

    sixth = jnp.where(head, turn(parts[0], 48), turn(parts[3], 96))
    seventh = jnp.where(head, turn(parts[1], 48), turn(parts[4], 96))
    eighth = jnp.where(
        head, turn(parts[2], 48), jnp.where(body, turn(parts[3], 64), turn(parts[4], 80))
    )
    return list(parts) + [sixth, seventh, eighth]


def compact_into(board_ref, base, to_ref, at):
    rows = [board_ref[pl.ds(base + 8 * k, 8), :] for k in range(8 * BATCH)]
    parts = []
    for block in range(BATCH):
        parts += compact(rows[8 * block : 8 * block + 8])
    for k in range(5 * BATCH):
        to_ref[pl.ds(at + 8 * k, 8), :] = parts[k]


def expand_into(from_ref, start, board_ref, base):
    parts = [from_ref[pl.ds(start + 8 * k, 8), :] for k in range(5 * BATCH)]
    rows = []
    for block in range(BATCH):
        rows += expand(parts[5 * block : 5 * block + 5])
    for k in range(8 * BATCH):
        board_ref[pl.ds(base + 8 * k, 8), :] = rows[k]


def spread_flat(state_ref, flat_ref):
    for block in range(BLOCKS):
        for v in range(5):
            at = block * 320 + v * 64
            flat_ref[at : at + 64, :] = state_ref[v, :, tile_lanes(block)]


def face_trace(state_ref, flat_ref, face, block):
    return jnp.concatenate([face_rows(state_ref, flat_ref, v, face, block) for v in range(5)], axis=0)


def build_tables(state_ref, flat_ref, table_ref):
    spread_flat(state_ref, flat_ref)
    padding = jnp.zeros((LANES - TRACE, LANES), jnp.float32)
    for face in range(6):
        for block in range(BLOCKS):
            trace = face_trace(state_ref, flat_ref, face, block)
            place = face * BLOCKS + block
            square = jnp.concatenate([trace, padding], axis=0)
            table_ref[place * LANES : (place + 1) * LANES, :] = square.T


def pack_kernel(
    place_ref,
    partner_hbm,
    state_hbm,
    plane_hbm,
    up_ref,
    down_ref,
    best_ref,
    plane_ref,
    partner_ref,
    state_ref,
    table_ref,
    board_ref,
    flat_ref,
    sems,
):
    copies = [pltpu.make_async_copy(partner_hbm, partner_ref, sems.at[0])]
    for a in range(4):
        nodes = pl.ds(a * 16, 16)
        copies.append(
            pltpu.make_async_copy(state_hbm.at[:, nodes, :], state_ref.at[:, nodes, :], sems.at[1 + a])
        )
    for copy in copies:
        copy.start()
    for copy in copies[1:]:
        copy.wait()
    build_tables(state_ref, flat_ref, table_ref)
    copies[0].wait()

    def scatter(step, carry):
        base = step * UNROLL
        targets = [partner_ref[base + k] for k in range(UNROLL)]
        rows = [table_ref[pl.ds(base + k, 1), :] for k in range(UNROLL)]
        for k in range(UNROLL):
            board_ref[pl.ds(targets[k], 1), :] = rows[k]
        return carry

    lax.fori_loop(0, COLUMNS // UNROLL, scatter, 0)

    def speeds(step, best):
        density, mom_x, mom_y, mom_z, energy = [
            state_ref[v, pl.ds(pl.multiple_of(step * 8, 8), 8), :] for v in range(5)
        ]
        inverse = 1.0 / density
        square = (mom_x * mom_x + mom_y * mom_y + mom_z * mom_z) * inverse
        pressure = (HEAT_RATIO - 1.0) * (energy - 0.5 * square)
        wave = jnp.sqrt(square * inverse) + jnp.sqrt(HEAT_RATIO * pressure * inverse)
        return jnp.maximum(best, wave)

    best = lax.fori_loop(0, 8, speeds, jnp.zeros((8, ELEMENTS), jnp.float32))
    best = jnp.maximum(
        jnp.maximum(best[:, tile_lanes(0)], best[:, tile_lanes(1)]),
        jnp.maximum(best[:, tile_lanes(2)], best[:, tile_lanes(3)]),
    )
    best_ref[...] = best
    up_ref[CROSS * MESSAGE :, :] = best
    down_ref[CROSS * MESSAGE :, :] = best
    plane, spot = place_ref[0], place_ref[1]

    def send(to_ref, peer, step):
        base = pl.multiple_of(COLUMNS + (peer + step * BATCH) * SLOTS, SLOTS)
        compact_into(board_ref, base, to_ref, aligned(step * BATCH * MESSAGE))

    def send_up(step, carry):
        send(up_ref, (plane + 1) * PLANE, step)
        return carry

    def send_down(step, carry):
        send(down_ref, (plane - 1) * PLANE + NEAR, step)
        return carry

    sent = []
    for step in range(PLANE // BATCH):
        send(plane_ref, plane * PLANE, step)
        part = pl.ds(step * BATCH * MESSAGE, BATCH * MESSAGE)
        sent.append(
            pltpu.make_async_copy(plane_ref.at[part, :], plane_hbm.at[part, :], sems.at[5 + step])
        )
        sent[-1].start()
    lax.fori_loop(0, (jnp.maximum(spot - NEAR + 1, 0) + BATCH - 1) // BATCH, send_up, 0)
    lax.fori_loop(spot // BATCH, CROSS // BATCH, send_down, 0)
    for copy in sent:
        copy.wait()


def relay_kernel(place_ref, up_ref, down_ref, best_ref, rate_hbm, relay_ref, three_ref):
    three_ref[...] = jnp.maximum(
        best_ref[...], jnp.maximum(up_ref[CROSS * MESSAGE :, :], down_ref[CROSS * MESSAGE :, :])
    )
    spot = place_ref[1]

    def from_up(block, carry):
        for k in range(5):
            at = pl.multiple_of(block * MESSAGE + 8 * k, 8)
            relay_ref[block, 8 * k : 8 * k + 8, :] = up_ref[pl.ds(at, 8), :]
        return carry

    def from_down(block, carry):
        for k in range(5):
            at = pl.multiple_of(block * MESSAGE + 8 * k, 8)
            relay_ref[block + NEAR, 8 * k : 8 * k + 8, :] = down_ref[pl.ds(at, 8), :]
        return carry

    lax.fori_loop(0, jnp.maximum(spot - NEAR + 1, 0), from_up, 0)
    lax.fori_loop(spot, CROSS, from_down, 0)


def top_kernel(three_ref, far_ref, relay_in, relay_hbm, top_ref, sem):
    top = jnp.maximum(three_ref[...], far_ref[...])
    for block in range(PLANE):
        top_ref[block] = top
    copy = pltpu.make_async_copy(top_ref, relay_hbm.at[:, pl.ds(MESSAGE, 8), :], sem)
    copy.start()
    copy.wait()


def early_kernel(
    place_ref,
    partner_ref,
    blank_hbm,
    state_ref,
    plane_ref,
    other_ref,
    owner_ref,
    board_ref,
    flat_ref,
    picked_ref,
    sem,
):
    plane, spot = place_ref[0], place_ref[1]
    blank = pltpu.make_async_copy(blank_hbm, owner_ref, sem)
    blank.start()
    build_tables(state_ref, flat_ref, board_ref)

    def receive(step, carry):
        start = pl.multiple_of(step * BATCH * MESSAGE, 8)
        base = pl.multiple_of(COLUMNS + (plane * PLANE + step * BATCH) * SLOTS, SLOTS)
        expand_into(plane_ref, start, board_ref, base)
        return carry

    lax.fori_loop(jnp.maximum(spot - REACH, 0) // BATCH, PLANE // BATCH, receive, 0)

    def gather(step, carry):
        base = step * UNROLL
        indices = [partner_ref[base + k] for k in range(UNROLL)]
        rows = [board_ref[pl.ds(index, 1), :] for index in indices]
        for k in range(UNROLL):
            picked_ref[pl.ds(base + k, 1), :] = rows[k]
            owner_ref[indices[k]] = base + k
        return carry

    blank.wait()
    lax.fori_loop(0, COLUMNS // UNROLL, gather, 0)
    for place in range(COLUMNS // LANES):
        square = picked_ref[place * LANES : (place + 1) * LANES, :].T
        other_ref[place * TRACE : (place + 1) * TRACE, :] = square[0:TRACE]


def sublane_index():
    return lax.broadcasted_iota(jnp.int32, (8, LANES), 0)


def wide(row):
    return jnp.broadcast_to(row, (8, LANES))


def face_normals(normal_ref, place):
    lanes = pl.ds(pl.multiple_of(place * LANES, LANES), LANES)
    normal = [wide(normal_ref[k : k + 1, lanes]) for k in range(3)]
    length = jnp.sqrt(normal[0] * normal[0] + normal[1] * normal[1] + normal[2] * normal[2])
    return normal, length


def lift(tiles, flux_ref, field_ref, v, block):
    first = sublane_index() < 4
    start = pl.multiple_of(v * 16, 16)

    def piece(face, half):
        return flux_ref[pl.ds((face * BLOCKS + block) * TRACE + half * 8 + start, 8), :]

    tiles = list(tiles)
    for half in range(2):
        tiles[half] = tiles[half] + piece(0, half)
        tiles[6 + half] = tiles[6 + half] + piece(1, half)
        low, high = piece(2, half), piece(3, half)
        tiles[4 * half] = tiles[4 * half] + jnp.where(first, low, 0.0)
        tiles[4 * half + 2] = tiles[4 * half + 2] + jnp.where(first, pltpu.roll(low, 4, 0), 0.0)
        tiles[4 * half + 1] = tiles[4 * half + 1] + jnp.where(first, 0.0, pltpu.roll(high, 4, 0))
        tiles[4 * half + 3] = tiles[4 * half + 3] + jnp.where(first, 0.0, high)
    base = pl.multiple_of(v * 64, 64) + block * 320
    for tile in range(8):
        field_ref[pl.ds(base + tile * 8, 8), :] = tiles[tile]
    for half in range(2):
        for face in (4, 5):
            nodes = pl.ds(base + half * 32 + 3 * (face - 4), 8, stride=4)
            field_ref[nodes, :] = field_ref[nodes, :] + piece(face, half)


def turn_indices(code):
    flip_first = jnp.where(code % 2 == 1, 3, 0)
    flip_second = jnp.where((code // 2) % 2 == 1, 3, 0)
    swapped = code >= 4
    sublane = sublane_index()
    result = []
    for half in range(2):
        i, j = 2 * half + sublane // 4, sublane % 4
        first = jnp.where(swapped, j, i) ^ flip_first
        second = jnp.where(swapped, i, j) ^ flip_second
        result.append(first * 4 + second)
    return result


def volume_kernel(
    place_ref,
    state_ref,
    register_ref,
    metric_ref,
    normal_ref,
    code_ref,
    partner_ref,
    field_ref,
    own_ref,
    side_ref,
    turn_ref,
    rows_ref,
    tensor_ref,
    flux_ref,
    flat_ref,
    rate_ref,
    term_ref,
):
    low = COLUMNS + place_ref[0] * (PLANE * SLOTS)
    spread_nodes(state_ref, rows_ref)
    spread_flat(state_ref, flat_ref)
    for face in range(6):
        for block in range(BLOCKS):
            place = face * BLOCKS + block
            own_ref[place * TRACE : (place + 1) * TRACE, :] = face_trace(state_ref, flat_ref, face, block)

    def own_fluxes(face, carry):
        for block in range(BLOCKS):
            place = face * BLOCKS + block
            normal, length = face_normals(normal_ref, place)
            start = pl.multiple_of(place * TRACE, TRACE)
            side = pl.multiple_of(place * SIDE, 16)
            for k, value in enumerate(normal + [length]):
                side_ref[pl.ds(side + 16 + 8 * k, 8), :] = value
            partner = wide(partner_ref[pl.ds(place, 1), :])
            late = (partner >= COLUMNS) & ((partner < low) | (partner >= low + PLANE * SLOTS))
            late = jnp.where(late, 16, 0)
            for half, turn in enumerate(turn_indices(wide(code_ref[pl.ds(place, 1), :]))):
                turn_ref[pl.ds(pl.multiple_of(place * 16, 16) + half * 8, 8), :] = turn + late
            for half in range(2):
                at = start + half * 8
                own = [own_ref[pl.ds(at + v * 16, 8), :] for v in range(5)]
                terms, wave = normal_flux(own, normal, length)
                for v in range(5):
                    term_ref[pl.ds(at + v * 16, 8), :] = (0.5 * LIFT_FACTOR) * terms[v]
                side_ref[pl.ds(side + half * 8, 8), :] = wave
        return carry

    lax.fori_loop(0, 6, own_fluxes, 0)
    for direction in range(3):
        for half in range(2):
            for block in range(BLOCKS):
                tensor_ref[pl.ds(direction * 24 + half * 4 + block, 3, stride=8), :] = metric_ref[
                    direction, :, block * LANES : (block + 1) * LANES
                ]

    def fluxes(step, carry):
        at = pl.multiple_of(step * 8, 8)
        density, mom_x, mom_y, mom_z, energy = [
            rows_ref[pl.ds(v * 256 + at, 8), :] for v in range(5)
        ]
        inverse = 1.0 / density
        momentum = [mom_x, mom_y, mom_z]
        velocity = [m * inverse for m in momentum]
        pressure = (HEAT_RATIO - 1.0) * (
            energy
            - 0.5 * (mom_x * velocity[0] + mom_y * velocity[1] + mom_z * velocity[2])
        )
        enthalpy = energy + pressure
        for direction in range(3):
            tensor = [tensor_ref[direction * 24 + k * 8 : direction * 24 + k * 8 + 8, :] for k in range(3)]
            along = tensor[0] * velocity[0] + tensor[1] * velocity[1] + tensor[2] * velocity[2]
            values = [density * along]
            values += [momentum[k] * along + pressure * tensor[k] for k in range(3)]
            values += [enthalpy * along]
            for v in range(5):
                flux_ref[direction, pl.ds(v * 256 + at, 8), :] = values[v]
        return carry

    lax.fori_loop(0, 32, fluxes, 0)
    matrix = derivative_matrix()
    upper = lax.broadcasted_iota(jnp.int32, (8, LANES), 0) < 4

    def pair(first, second):
        return jnp.where(upper, jnp.float32(first), jnp.float32(second))

    straight = [[pair(matrix[2 * t, 2 * s], matrix[2 * t + 1, 2 * s + 1]) for s in range(2)] for t in range(2)]
    crossed = [[pair(matrix[2 * t, 2 * s + 1], matrix[2 * t + 1, 2 * s]) for s in range(2)] for t in range(2)]

    def combine(values, target):
        total = values[0] * float(matrix[target, 0])
        for source in range(1, 4):
            total = total + values[source] * float(matrix[target, source])
        return total

    def diverge(v, carry):
        base = pl.multiple_of(v * 256, 256)
        for rest in range(8):
            values = [flux_ref[0, pl.ds(base + a * 64 + rest * 8, 8), :] for a in range(4)]
            for a in range(4):
                rate_ref[pl.ds(base + a * 64 + rest * 8, 8), :] = -combine(values, a)
        for a in range(4):
            for half in range(2):
                values = [flux_ref[1, pl.ds(base + a * 64 + b * 16 + half * 8, 8), :] for b in range(4)]
                third = [flux_ref[2, pl.ds(base + a * 64 + b * 16 + half * 8, 8), :] for b in range(4)]
                other = [flux_ref[2, pl.ds(base + a * 64 + b * 16 + (1 - half) * 8, 8), :] for b in range(4)]
                for b in range(4):
                    at = pl.ds(base + a * 64 + b * 16 + half * 8, 8)
                    same, far = third[b], other[b]
                    total = combine(values, b)
                    total = total + straight[half][half] * same
                    total = total + crossed[half][half] * pltpu.roll(same, 4, 0)
                    total = total + straight[half][1 - half] * far
                    total = total + crossed[half][1 - half] * pltpu.roll(far, 4, 0)
                    rate_ref[at, :] = rate_ref[at, :] - total
        return carry

    lax.fori_loop(0, 5, diverge, 0)

    def gather_terms(v, carry):
        base = pl.multiple_of(v * 256, 256)
        for block in range(BLOCKS):
            tiles = []
            for tile in range(8):
                old = register_ref[v, tile * 8 : tile * 8 + 8, tile_lanes(block)]
                rate = rate_ref[pl.ds(base + tile * 32 + block, 8, stride=BLOCKS), :]
                tiles.append(rate + SECTION_KEEP * old)
            lift(tiles, term_ref, field_ref, v, block)
        return carry

    lax.fori_loop(0, 5, gather_terms, 0)


def normal_flux(values, normal, length):
    density, momentum, energy = values[0], values[1:4], values[4]
    inverse = 1.0 / density
    velocity = [m * inverse for m in momentum]
    pressure = (HEAT_RATIO - 1.0) * (
        energy
        - 0.5 * (momentum[0] * velocity[0] + momentum[1] * velocity[1] + momentum[2] * velocity[2])
    )
    speed = velocity[0] * normal[0] + velocity[1] * normal[1] + velocity[2] * normal[2]
    terms = [density * speed]
    terms += [momentum[k] * speed + pressure * normal[k] for k in range(3)]
    terms += [(energy + pressure) * speed]
    wave = jnp.abs(speed) + jnp.sqrt(HEAT_RATIO * pressure * inverse) * length
    return terms, wave


def finish_kernel(
    place_ref,
    owner_hbm,
    other_hbm,
    own_hbm,
    side_hbm,
    turn_hbm,
    rate_hbm,
    state_hbm,
    relay_ref,
    section_hbm,
    advanced_hbm,
    low_ref,
    high_ref,
    section_ref,
    advanced_ref,
    board_ref,
    picked_ref,
    other_ref,
    own_ref,
    side_ref,
    turn_ref,
    rate_ref,
    state_ref,
    term_ref,
    field_ref,
    sems,
):
    plane, spot = place_ref[0], place_ref[1]
    window = CROSS * SLOTS
    low_slot = jnp.maximum(COLUMNS + ((plane - 1) * PLANE + NEAR) * SLOTS, 0)
    high_slot = jnp.minimum(COLUMNS + (plane + 1) * PLANE * SLOTS, COLUMNS + DEVICES * SLOTS - window)
    sources = [
        (owner_hbm.at[pl.ds(pl.multiple_of(low_slot, 512), window)], low_ref),
        (owner_hbm.at[pl.ds(pl.multiple_of(high_slot, 512), window)], high_ref),
        (other_hbm, other_ref),
        (own_hbm, own_ref),
        (turn_hbm, turn_ref),
        (side_hbm, side_ref),
        (rate_hbm, rate_ref),
        (state_hbm, state_ref),
    ]
    copies = [
        pltpu.make_async_copy(source, target, sems.at[k])
        for k, (source, target) in enumerate(sources)
    ]
    for copy in copies:
        copy.start()

    def receive(peer, block):
        parts = [relay_ref[block + k // 5, 8 * (k % 5) : 8 * (k % 5) + 8, :] for k in range(5 * BATCH)]
        rows = []
        for k in range(BATCH):
            rows += expand(parts[5 * k : 5 * k + 5])
        base = pl.multiple_of((peer + block + MARGIN) * SLOTS, SLOTS)
        for k in range(8 * BATCH):
            board_ref[pl.ds(base + 8 * k, 8), :] = rows[k]

    def receive_low(step, carry):
        receive((plane - 1) * PLANE, NEAR + step * BATCH)
        return carry

    def receive_high(step, carry):
        receive((plane + 1) * PLANE, step * BATCH)
        return carry

    lax.fori_loop(spot // BATCH, CROSS // BATCH, receive_low, 0)
    high = (jnp.maximum(spot - NEAR + 1, 0) + BATCH - 1) // BATCH
    lax.fori_loop(0, high, receive_high, 0)

    def place_rows(columns_ref, base, step):
        at = step * UNROLL
        columns = [columns_ref[at + k] for k in range(UNROLL)]
        rows = [board_ref[pl.ds(base * SLOTS + at + k, 1), :] for k in range(UNROLL)]
        for k in range(UNROLL):
            picked_ref[pl.ds(columns[k], 1), :] = rows[k]

    def place_low(step, carry):
        place_rows(low_ref, (plane - 1) * PLANE + NEAR + MARGIN, step)
        return carry

    def place_high(step, carry):
        place_rows(high_ref, (plane + 1) * PLANE + MARGIN, step)
        return carry

    chunk = SLOTS // UNROLL
    for copy in copies[:2]:
        copy.wait()

    @pl.when(plane > 0)
    def _():
        lax.fori_loop(spot * chunk, CROSS * chunk, place_low, 0)

    @pl.when(plane < 3)
    def _():
        lax.fori_loop(0, jnp.maximum(spot - NEAR + 1, 0) * chunk, place_high, 0)

    for copy in copies[2:]:
        copy.wait()

    def far_fluxes(face, carry):
        for block in range(BLOCKS):
            place = face * BLOCKS + block
            square = picked_ref[pl.ds(pl.multiple_of(place * LANES, LANES), LANES), :].T
            start = pl.multiple_of(place * TRACE, TRACE)
            side = pl.multiple_of(place * SIDE, 16)
            at = pl.multiple_of(place * 16, 16)
            turns = [turn_ref[pl.ds(at + half * 8, 8), :] for half in range(2)]
            late = turns[0] >= 16
            known = [
                jnp.where(late, square[8 * k : 8 * k + 8], other_ref[pl.ds(start + 8 * k, 8), :])
                for k in range(10)
            ]
            normal = [side_ref[pl.ds(side + 16 + 8 * k, 8), :] for k in range(3)]
            length = side_ref[pl.ds(side + 40, 8), :]
            for half in range(2):
                upper = turns[half] % 16 >= 8
                sublane = turns[half] % 8
                far = []
                for v in range(5):
                    parts = [
                        jnp.take_along_axis(known[2 * v + k], sublane, axis=0, mode="promise_in_bounds")
                        for k in range(2)
                    ]
                    far.append(jnp.where(upper, parts[1], parts[0]))
                far_terms, far_wave = normal_flux(far, normal, length)
                bound = jnp.maximum(side_ref[pl.ds(side + half * 8, 8), :], far_wave)
                viscous = bound + length
                for v in range(5):
                    rows = pl.ds(start + v * 16 + half * 8, 8)
                    weight = bound if v == 0 else viscous
                    term_ref[rows, :] = (0.5 * LIFT_FACTOR) * (
                        weight * (far[v] - own_ref[rows, :]) - far_terms[v]
                    )
        return carry

    lax.fori_loop(0, 6, far_fluxes, 0)
    top = jnp.max(jnp.max(relay_ref[:, MESSAGE:, :], axis=0))
    scale = CFL_NUMBER / top * SECTION_STEP

    def results(v):
        return [
            pltpu.make_async_copy(section_ref.at[v], section_hbm.at[v], sems.at[2 * v]),
            pltpu.make_async_copy(advanced_ref.at[v], advanced_hbm.at[v], sems.at[2 * v + 1]),
        ]

    def update(v, carry):
        for block in range(BLOCKS):
            lanes = tile_lanes(block)
            base = pl.multiple_of(v * 64, 64) + block * 320
            tiles = [rate_ref[pl.ds(base + tile * 8, 8), :] for tile in range(8)]
            lift(tiles, term_ref, field_ref, v, block)
            for tile in range(8):
                nodes = slice(tile * 8, tile * 8 + 8)
                section = field_ref[pl.ds(base + tile * 8, 8), :]
                section_ref[v, nodes, lanes] = section
                advanced_ref[v, nodes, lanes] = state_ref[v, nodes, lanes] + scale * section
        for copy in results(v):
            copy.start()
        return carry

    lax.fori_loop(0, 5, update, 0)
    for v in range(5):
        for copy in results(v):
            copy.wait()


def smem():
    return pl.BlockSpec(memory_space=pltpu.SMEM)


def vmem():
    return pl.BlockSpec(memory_space=pltpu.VMEM)


def params():
    return pltpu.CompilerParams(vmem_limit_bytes=VMEM_LIMIT)


def shape(*sizes):
    return jax.ShapeDtypeStruct(sizes, jnp.float32)


def scratch(*sizes):
    return pltpu.VMEM(sizes, jnp.float32)


def hbm():
    return pl.BlockSpec(memory_space=pltpu.HBM)


def anywhere():
    return pl.BlockSpec(memory_space=pl.ANY)


def in_hbm_shape(*sizes):
    return pltpu.HBM(sizes, jnp.float32)


def pack(place, partner, state):
    return pl.pallas_call(
        pack_kernel,
        out_shape=(
            in_hbm_shape(PLANE * MESSAGE, LANES),
            shape(CROSS * MESSAGE + 8, LANES),
            shape(CROSS * MESSAGE + 8, LANES),
            shape(8, LANES),
        ),
        in_specs=[smem(), hbm(), hbm()],
        out_specs=(hbm(), vmem(), vmem(), vmem()),
        scratch_shapes=[
            scratch(PLANE * MESSAGE, LANES),
            pltpu.SMEM((COLUMNS,), jnp.int32),
            scratch(5, 64, ELEMENTS),
            scratch(COLUMNS, LANES),
            scratch(COLUMNS + (DEVICES + CROSS) * SLOTS, LANES),
            scratch(1280, LANES),
            pltpu.SemaphoreType.DMA((5 + PLANE // BATCH,)),
        ],
        compiler_params=params(),
        name="pack",
    )(place, partner, state)


def volume(place, state, register, metric, normal, code, partner):
    return pl.pallas_call(
        volume_kernel,
        out_shape=(
            in_hbm_shape(1280, LANES),
            in_hbm_shape(24 * TRACE, LANES),
            in_hbm_shape(24 * SIDE, LANES),
            pltpu.HBM((24 * 16, LANES), jnp.int32),
        ),
        in_specs=[smem()] + [vmem()] * 6,
        out_specs=(vmem(),) * 4,
        scratch_shapes=[
            scratch(1280, LANES),
            scratch(72, LANES),
            scratch(3, 1280, LANES),
            scratch(1280, LANES),
            scratch(1280, LANES),
            scratch(24 * TRACE, LANES),
        ],
        compiler_params=params(),
        name="volume",
    )(place, state, register, metric, normal, code, partner)


def relay(place, up, down, best, rate):
    return pl.pallas_call(
        relay_kernel,
        out_shape=(in_hbm_shape(PLANE, MESSAGE + 8, LANES), shape(8, LANES)),
        in_specs=[smem()] + [vmem()] * 3 + [hbm()],
        out_specs=(vmem(), vmem()),
        compiler_params=params(),
        cost_estimate=pl.CostEstimate(flops=10**11, bytes_accessed=10**8, transcendentals=0),
        name="relay",
    )(place, up, down, best, rate)


def spread_top(three, far, relayed):
    return pl.pallas_call(
        top_kernel,
        out_shape=in_hbm_shape(PLANE, MESSAGE + 8, LANES),
        in_specs=[vmem(), vmem(), hbm()],
        out_specs=hbm(),
        scratch_shapes=[scratch(PLANE, 8, LANES), pltpu.SemaphoreType.DMA],
        input_output_aliases={2: 0},
        compiler_params=params(),
        name="top",
    )(three, far, relayed)


def early(place, partner, blank, state, plane):
    return pl.pallas_call(
        early_kernel,
        out_shape=(
            in_hbm_shape(24 * TRACE, LANES),
            pltpu.HBM((COLUMNS + DEVICES * SLOTS,), jnp.int32),
        ),
        in_specs=[smem(), smem(), anywhere(), vmem(), vmem()],
        out_specs=(vmem(), smem()),
        scratch_shapes=[
            scratch(COLUMNS + DEVICES * SLOTS, LANES),
            scratch(1280, LANES),
            scratch(COLUMNS, LANES),
            pltpu.SemaphoreType.DMA,
        ],
        compiler_params=params(),
        name="early",
    )(place, partner, blank, state, plane)


def finish(place, owner, other, own, side, turn, rate, state, relayed):
    held = [in_hbm(value) for value in (owner, other, own, side, turn, rate, state)]
    return pl.pallas_call(
        finish_kernel,
        out_shape=(in_hbm_shape(5, 64, ELEMENTS),) * 2,
        in_specs=[smem()] + [hbm()] * 7 + [vmem()],
        out_specs=(hbm(), hbm()),
        scratch_shapes=[
            pltpu.SMEM((CROSS * SLOTS,), jnp.int32),
            pltpu.SMEM((CROSS * SLOTS,), jnp.int32),
            scratch(5, 64, ELEMENTS),
            scratch(5, 64, ELEMENTS),
            scratch((DEVICES + 2 * MARGIN) * SLOTS, LANES),
            scratch(COLUMNS + 8, LANES),
            scratch(24 * TRACE, LANES),
            scratch(24 * TRACE, LANES),
            scratch(24 * SIDE, LANES),
            pltpu.VMEM((24 * 16, LANES), jnp.int32),
            scratch(1280, LANES),
            scratch(5, 64, ELEMENTS),
            scratch(24 * TRACE, LANES),
            scratch(1280, LANES),
            pltpu.SemaphoreType.DMA((10,)),
        ],
        compiler_params=params(),
        name="finish",
    )(place, *held, relayed)


def in_hbm(value):
    return pltpu.with_memory_space_constraint(value, pltpu.HBM)


def in_vmem(value):
    return pltpu.with_memory_space_constraint(value, pltpu.VMEM)


def along_y(value, steps):
    return lax.ppermute(value, "y", [(i, (i + steps) % 4) for i in range(4)])


def on_device(state, register, metric, face_normal, partner, flip_code, face_role, send_face):
    plane = lax.axis_index("y").astype(jnp.int32)
    spot = lax.axis_index(("r", "x")).astype(jnp.int32)
    place = jnp.stack([plane, spot])
    state = state.transpose(1, 0, 2)
    rows = (COLUMNS // LANES, LANES)
    in_plane, up, down, best = pack(place, in_hbm(partner), in_hbm(state))
    from_below = along_y(up, 1)
    from_above = along_y(down, -1)
    far = along_y(best, 2)
    got = lax.all_to_all(in_plane, ("r", "x"), 0, 0, tiled=True)
    rate, own, side, turn = volume(
        place,
        state,
        register.transpose(1, 0, 2),
        metric,
        face_normal,
        flip_code.reshape(rows),
        partner.reshape(rows),
    )
    relayed, three = relay(place, from_below, from_above, best, in_hbm(rate))
    relayed = spread_top(three, far, in_hbm(relayed))
    relayed = lax.all_to_all(relayed, ("r", "x"), 0, 0, tiled=True)
    blank = jnp.full((COLUMNS + DEVICES * SLOTS,), COLUMNS, jnp.int32)
    other, owner = early(place, partner, blank, state, got)
    section, advanced = finish(place, owner, other, own, side, turn, rate, state, relayed)
    return section.transpose(1, 0, 2), advanced.transpose(1, 0, 2)


def solution(mesh):
    placed = (
        P(None, None, AXES),
        P(None, None, AXES),
        P(None, None, AXES),
        P(None, AXES),
        P(AXES),
        P(AXES),
        P(AXES),
        P(AXES, None, None),
    )
    return jax.shard_map(
        on_device,
        mesh=Mesh(mesh.devices.reshape(4, 8, 4), AXES),
        in_specs=placed,
        out_specs=(P(None, None, AXES), P(None, None, AXES)),
        check_vma=False,
    )
```

```python
import jax
import jax.numpy as jnp
import numpy as np
from jax import lax
from jax.experimental import pallas as pl
from jax.experimental.pallas import tpu as pltpu
from jax.sharding import Mesh
from jax.sharding import PartitionSpec as P

HEAT_RATIO = 1.4
LIFT_FACTOR = 6.0
CFL_NUMBER = 0.3
SECTION_KEEP = -0.4178904745
SECTION_STEP = 0.4432226
DEVICES = 128
ELEMENTS = 512
COLUMNS = 6 * ELEMENTS
SLOTS = 64
REACH = 24
LANES = 128
BLOCKS = ELEMENTS // LANES
TRACE = 80
GROUP = COLUMNS // 3
MESSAGE = TRACE * SLOTS // LANES
UNROLL = 32
SIDE = 24
BATCH = 4
AXES = ("y", "r", "x")
PLANE = 32
NEAR = PLANE - REACH
CROSS = REACH
MARGIN = CROSS
VMEM_LIMIT = 24 * 1024 * 1024


def derivative_matrix():
    points = np.array([-1.0, -1.0 / np.sqrt(5.0), 1.0 / np.sqrt(5.0), 1.0])
    weights = np.array(
        [
            1.0
            / np.prod([points[target] - points[source] for source in range(4) if source != target])
            for target in range(4)
        ]
    )
    matrix = np.zeros((4, 4))
    for target in range(4):
        for source in range(4):
            if target != source:
                matrix[target, source] = (
                    weights[source] / weights[target] / (points[target] - points[source])
                )
        matrix[target, target] = -np.sum(matrix[target])
    return matrix


def face_nodes(face):
    side = 3 * (face % 2)
    if face < 2:
        return [side * 16 + i * 4 + j for i in range(4) for j in range(4)]
    if face < 4:
        return [i * 16 + side * 4 + j for i in range(4) for j in range(4)]
    return [i * 16 + j * 4 + side for i in range(4) for j in range(4)]


def tile_lanes(block):
    return pl.ds(aligned(block * LANES, LANES), LANES)


def spread_nodes(state_ref, rows_ref):
    for v in range(5):
        for tile in range(8):
            for block in range(BLOCKS):
                rows_ref[pl.ds(v * 256 + tile * 32 + block, 8, stride=BLOCKS), :] = state_ref[
                    v, tile * 8 : tile * 8 + 8, tile_lanes(block)
                ]


def face_rows(state_ref, flat_ref, v, face, block):
    side = 3 * (face % 2)
    lanes = tile_lanes(block)
    if face < 2:
        return state_ref[v, side * 16 : side * 16 + 16, lanes]
    if face < 4:
        return jnp.concatenate(
            [state_ref[v, i * 16 + side * 4 : i * 16 + side * 4 + 4, lanes] for i in range(4)], axis=0
        )
    return flat_ref[pl.ds(aligned(block * 320, 64) + v * 64 + side, 16, stride=4), :]


def aligned(row, step=8):
    return row if isinstance(row, int) else pl.multiple_of(row, step)


def lane_index(shape):
    return lax.broadcasted_iota(jnp.int32, shape, 1)


def compact(rows):
    lane = lane_index((8, LANES))
    low = lane < 80
    mid = lane < 112

    def turn(value, shift):
        return pltpu.roll(value, shift, 1)

    first = [jnp.where(low, rows[k], turn(rows[5 + k], 80)) for k in range(3)]
    fourth = jnp.where(low, rows[3], jnp.where(mid, turn(rows[5], 32), turn(rows[7], 64)))
    fifth = jnp.where(low, rows[4], jnp.where(mid, turn(rows[6], 32), turn(rows[7], 48)))
    return first + [fourth, fifth]


def expand(parts):
    lane = lane_index((8, LANES))
    head = lane < 48
    body = lane < 64

    def turn(value, shift):
        return pltpu.roll(value, shift, 1)

    sixth = jnp.where(head, turn(parts[0], 48), turn(parts[3], 96))
    seventh = jnp.where(head, turn(parts[1], 48), turn(parts[4], 96))
    eighth = jnp.where(
        head, turn(parts[2], 48), jnp.where(body, turn(parts[3], 64), turn(parts[4], 80))
    )
    return list(parts) + [sixth, seventh, eighth]


def compact_into(board_ref, base, to_ref, at):
    rows = [board_ref[pl.ds(base + 8 * k, 8), :] for k in range(8 * BATCH)]
    parts = []
    for block in range(BATCH):
        parts += compact(rows[8 * block : 8 * block + 8])
    for k in range(5 * BATCH):
        to_ref[pl.ds(at + 8 * k, 8), :] = parts[k]


def expand_into(from_ref, start, board_ref, base):
    parts = [from_ref[pl.ds(start + 8 * k, 8), :] for k in range(5 * BATCH)]
    rows = []
    for block in range(BATCH):
        rows += expand(parts[5 * block : 5 * block + 5])
    for k in range(8 * BATCH):
        board_ref[pl.ds(base + 8 * k, 8), :] = rows[k]


def spread_flat(state_ref, flat_ref):
    for block in range(BLOCKS):
        for v in range(5):
            at = block * 320 + v * 64
            flat_ref[at : at + 64, :] = state_ref[v, :, tile_lanes(block)]


def face_trace(state_ref, flat_ref, face, block):
    return jnp.concatenate([face_rows(state_ref, flat_ref, v, face, block) for v in range(5)], axis=0)


def build_tables(state_ref, flat_ref, table_ref):
    spread_flat(state_ref, flat_ref)
    padding = jnp.zeros((LANES - TRACE, LANES), jnp.float32)
    for face in range(6):
        for block in range(BLOCKS):
            trace = face_trace(state_ref, flat_ref, face, block)
            place = face * BLOCKS + block
            square = jnp.concatenate([trace, padding], axis=0)
            table_ref[place * LANES : (place + 1) * LANES, :] = square.T


def pack_kernel(
    place_ref,
    partner_hbm,
    state_hbm,
    plane_hbm,
    up_ref,
    down_ref,
    best_ref,
    plane_ref,
    partner_ref,
    state_ref,
    table_ref,
    board_ref,
    flat_ref,
    sems,
):
    copies = [pltpu.make_async_copy(partner_hbm, partner_ref, sems.at[0])]
    for a in range(4):
        nodes = pl.ds(a * 16, 16)
        copies.append(
            pltpu.make_async_copy(state_hbm.at[:, nodes, :], state_ref.at[:, nodes, :], sems.at[1 + a])
        )
    for copy in copies:
        copy.start()
    for copy in copies[1:]:
        copy.wait()
    spread_flat(state_ref, flat_ref)
    copies[0].wait()
    padding = jnp.zeros((LANES - TRACE, LANES), jnp.float32)

    def build(face, block, slot):
        square = jnp.concatenate([face_trace(state_ref, flat_ref, face, block), padding], axis=0)
        table_ref[slot] = square.T

    def scatter(block, carry):
        for face in range(6):
            build(face, block, face)
            base = face * ELEMENTS + block * LANES
            for start in range(0, LANES, UNROLL):
                targets = [partner_ref[base + start + k] for k in range(UNROLL)]
                rows = [table_ref[face, start + k : start + k + 1, :] for k in range(UNROLL)]
                for k in range(UNROLL):
                    board_ref[pl.ds(targets[k], 1), :] = rows[k]
        return carry

    lax.fori_loop(0, BLOCKS, scatter, 0)

    def speeds(step, best):
        density, mom_x, mom_y, mom_z, energy = [
            state_ref[v, pl.ds(pl.multiple_of(step * 8, 8), 8), :] for v in range(5)
        ]
        inverse = 1.0 / density
        square = (mom_x * mom_x + mom_y * mom_y + mom_z * mom_z) * inverse
        pressure = (HEAT_RATIO - 1.0) * (energy - 0.5 * square)
        wave = jnp.sqrt(square * inverse) + jnp.sqrt(HEAT_RATIO * pressure * inverse)
        return jnp.maximum(best, wave)

    best = lax.fori_loop(0, 8, speeds, jnp.zeros((8, ELEMENTS), jnp.float32))
    best = jnp.maximum(
        jnp.maximum(best[:, tile_lanes(0)], best[:, tile_lanes(1)]),
        jnp.maximum(best[:, tile_lanes(2)], best[:, tile_lanes(3)]),
    )
    best_ref[...] = best
    up_ref[CROSS * MESSAGE :, :] = best
    down_ref[CROSS * MESSAGE :, :] = best
    plane, spot = place_ref[0], place_ref[1]

    def send(to_ref, peer, step):
        base = pl.multiple_of(COLUMNS + (peer + step * BATCH) * SLOTS, SLOTS)
        compact_into(board_ref, base, to_ref, aligned(step * BATCH * MESSAGE))

    def send_up(step, carry):
        send(up_ref, (plane + 1) * PLANE, step)
        return carry

    def send_down(step, carry):
        send(down_ref, (plane - 1) * PLANE + NEAR, step)
        return carry

    sent = []
    for step in range(PLANE // BATCH):
        send(plane_ref, plane * PLANE, step)
        part = pl.ds(step * BATCH * MESSAGE, BATCH * MESSAGE)
        sent.append(
            pltpu.make_async_copy(plane_ref.at[part, :], plane_hbm.at[part, :], sems.at[5 + step])
        )
        sent[-1].start()
    lax.fori_loop(0, (jnp.maximum(spot - NEAR + 1, 0) + BATCH - 1) // BATCH, send_up, 0)
    lax.fori_loop(spot // BATCH, CROSS // BATCH, send_down, 0)
    for copy in sent:
        copy.wait()


def relay_kernel(place_ref, up_ref, down_ref, best_ref, rate_hbm, relay_ref, three_ref):
    three_ref[...] = jnp.maximum(
        best_ref[...], jnp.maximum(up_ref[CROSS * MESSAGE :, :], down_ref[CROSS * MESSAGE :, :])
    )
    spot = place_ref[1]

    def from_up(block, carry):
        for k in range(5):
            at = pl.multiple_of(block * MESSAGE + 8 * k, 8)
            relay_ref[block, 8 * k : 8 * k + 8, :] = up_ref[pl.ds(at, 8), :]
        return carry

    def from_down(block, carry):
        for k in range(5):
            at = pl.multiple_of(block * MESSAGE + 8 * k, 8)
            relay_ref[block + NEAR, 8 * k : 8 * k + 8, :] = down_ref[pl.ds(at, 8), :]
        return carry

    lax.fori_loop(0, jnp.maximum(spot - NEAR + 1, 0), from_up, 0)
    lax.fori_loop(spot, CROSS, from_down, 0)


def top_kernel(three_ref, far_ref, relay_in, relay_hbm, top_ref, sem):
    top = jnp.maximum(three_ref[...], far_ref[...])
    for block in range(PLANE):
        top_ref[block] = top
    copy = pltpu.make_async_copy(top_ref, relay_hbm.at[:, pl.ds(MESSAGE, 8), :], sem)
    copy.start()
    copy.wait()


def early_kernel(
    place_ref,
    partner_ref,
    blank_hbm,
    state_ref,
    plane_ref,
    other_ref,
    owner_ref,
    board_ref,
    flat_ref,
    picked_ref,
    sem,
):
    plane, spot = place_ref[0], place_ref[1]
    blank = pltpu.make_async_copy(blank_hbm, owner_ref, sem)
    blank.start()
    build_tables(state_ref, flat_ref, board_ref)

    def receive(step, carry):
        start = pl.multiple_of(step * BATCH * MESSAGE, 8)
        base = pl.multiple_of(COLUMNS + (plane * PLANE + step * BATCH) * SLOTS, SLOTS)
        expand_into(plane_ref, start, board_ref, base)
        return carry

    lax.fori_loop(jnp.maximum(spot - REACH, 0) // BATCH, PLANE // BATCH, receive, 0)

    def gather(step, carry):
        base = step * UNROLL
        indices = [partner_ref[base + k] for k in range(UNROLL)]
        rows = [board_ref[pl.ds(index, 1), :] for index in indices]
        for k in range(UNROLL):
            picked_ref[pl.ds(base + k, 1), :] = rows[k]
            owner_ref[indices[k]] = base + k
        return carry

    blank.wait()
    lax.fori_loop(0, COLUMNS // UNROLL, gather, 0)
    for place in range(COLUMNS // LANES):
        square = picked_ref[place * LANES : (place + 1) * LANES, :].T
        other_ref[place * TRACE : (place + 1) * TRACE, :] = square[0:TRACE]


def sublane_index():
    return lax.broadcasted_iota(jnp.int32, (8, LANES), 0)


def wide(row):
    return jnp.broadcast_to(row, (8, LANES))


def face_normals(normal_ref, place):
    lanes = pl.ds(pl.multiple_of(place * LANES, LANES), LANES)
    normal = [wide(normal_ref[k : k + 1, lanes]) for k in range(3)]
    length = jnp.sqrt(normal[0] * normal[0] + normal[1] * normal[1] + normal[2] * normal[2])
    return normal, length


def lift(tiles, flux_ref, field_ref, v, block):
    first = sublane_index() < 4

    def piece(face, half):
        start = aligned((face * BLOCKS + block) * TRACE + v * 16)
        return flux_ref[pl.ds(start + half * 8, 8), :]

    tiles = list(tiles)
    for half in range(2):
        tiles[half] = tiles[half] + piece(0, half)
        tiles[6 + half] = tiles[6 + half] + piece(1, half)
        low, high = piece(2, half), piece(3, half)
        tiles[4 * half] = tiles[4 * half] + jnp.where(first, low, 0.0)
        tiles[4 * half + 2] = tiles[4 * half + 2] + jnp.where(first, pltpu.roll(low, 4, 0), 0.0)
        tiles[4 * half + 1] = tiles[4 * half + 1] + jnp.where(first, 0.0, pltpu.roll(high, 4, 0))
        tiles[4 * half + 3] = tiles[4 * half + 3] + jnp.where(first, 0.0, high)
    base = aligned(v * 64 + block * 320)
    for tile in range(8):
        field_ref[pl.ds(base + tile * 8, 8), :] = tiles[tile]
    for half in range(2):
        for face in (4, 5):
            nodes = pl.ds(base + half * 32 + 3 * (face - 4), 8, stride=4)
            field_ref[nodes, :] = field_ref[nodes, :] + piece(face, half)


def turn_indices(code):
    flip_first = jnp.where(code % 2 == 1, 3, 0)
    flip_second = jnp.where((code // 2) % 2 == 1, 3, 0)
    swapped = code >= 4
    sublane = sublane_index()
    result = []
    for half in range(2):
        i, j = 2 * half + sublane // 4, sublane % 4
        first = jnp.where(swapped, j, i) ^ flip_first
        second = jnp.where(swapped, i, j) ^ flip_second
        result.append(first * 4 + second)
    return result


def volume_kernel(
    place_ref,
    state_ref,
    register_ref,
    metric_ref,
    normal_ref,
    code_ref,
    partner_ref,
    field_ref,
    own_ref,
    side_ref,
    turn_ref,
    rows_ref,
    tensor_ref,
    flux_ref,
    flat_ref,
    rate_ref,
    term_ref,
):
    low = COLUMNS + place_ref[0] * (PLANE * SLOTS)
    spread_nodes(state_ref, rows_ref)
    spread_flat(state_ref, flat_ref)
    for face in range(6):
        for block in range(BLOCKS):
            place = face * BLOCKS + block
            own_ref[place * TRACE : (place + 1) * TRACE, :] = face_trace(state_ref, flat_ref, face, block)

    def own_fluxes(face, carry):
        for block in range(BLOCKS):
            place = face * BLOCKS + block
            normal, length = face_normals(normal_ref, place)
            start = pl.multiple_of(place * TRACE, TRACE)
            side = pl.multiple_of(place * SIDE, 8)
            rows = [value[0:1] for value in normal + [length]]
            side_ref[pl.ds(side + 16, 8), :] = jnp.concatenate(rows + rows, axis=0)
            partner = wide(partner_ref[pl.ds(place, 1), :])
            late = (partner >= COLUMNS) & ((partner < low) | (partner >= low + PLANE * SLOTS))
            late = jnp.where(late, 16, 0)
            for half, turn in enumerate(turn_indices(wide(code_ref[pl.ds(place, 1), :]))):
                turn_ref[pl.ds(pl.multiple_of(place * 16, 16) + half * 8, 8), :] = turn + late
            for half in range(2):
                at = start + half * 8
                own = [own_ref[pl.ds(at + v * 16, 8), :] for v in range(5)]
                terms, wave = normal_flux(own, normal, length)
                for v in range(5):
                    term_ref[pl.ds(at + v * 16, 8), :] = (0.5 * LIFT_FACTOR) * terms[v]
                side_ref[pl.ds(side + half * 8, 8), :] = wave
        return carry

    lax.fori_loop(0, 6, own_fluxes, 0)
    for direction in range(3):
        for half in range(2):
            for block in range(BLOCKS):
                tensor_ref[pl.ds(direction * 24 + half * 4 + block, 3, stride=8), :] = metric_ref[
                    direction, :, block * LANES : (block + 1) * LANES
                ]

    def fluxes(step, carry):
        at = pl.multiple_of(step * 8, 8)
        density, mom_x, mom_y, mom_z, energy = [
            rows_ref[pl.ds(v * 256 + at, 8), :] for v in range(5)
        ]
        inverse = 1.0 / density
        momentum = [mom_x, mom_y, mom_z]
        velocity = [m * inverse for m in momentum]
        pressure = (HEAT_RATIO - 1.0) * (
            energy
            - 0.5 * (mom_x * velocity[0] + mom_y * velocity[1] + mom_z * velocity[2])
        )
        enthalpy = energy + pressure
        for direction in range(3):
            tensor = [tensor_ref[direction * 24 + k * 8 : direction * 24 + k * 8 + 8, :] for k in range(3)]
            along = tensor[0] * velocity[0] + tensor[1] * velocity[1] + tensor[2] * velocity[2]
            values = [density * along]
            values += [momentum[k] * along + pressure * tensor[k] for k in range(3)]
            values += [enthalpy * along]
            for v in range(5):
                flux_ref[direction, pl.ds(v * 256 + at, 8), :] = values[v]
        return carry

    lax.fori_loop(0, 32, fluxes, 0)
    matrix = derivative_matrix()
    upper = lax.broadcasted_iota(jnp.int32, (8, LANES), 0) < 4

    def pair(first, second):
        return jnp.where(upper, jnp.float32(first), jnp.float32(second))

    straight = [[pair(matrix[2 * t, 2 * s], matrix[2 * t + 1, 2 * s + 1]) for s in range(2)] for t in range(2)]
    crossed = [[pair(matrix[2 * t, 2 * s + 1], matrix[2 * t + 1, 2 * s]) for s in range(2)] for t in range(2)]

    def combine(values, target):
        total = values[0] * float(matrix[target, 0])
        for source in range(1, 4):
            total = total + values[source] * float(matrix[target, source])
        return total

    def diverge(v, carry):
        base = pl.multiple_of(v * 256, 256)
        for rest in range(8):
            values = [flux_ref[0, pl.ds(base + a * 64 + rest * 8, 8), :] for a in range(4)]
            for a in range(4):
                rate_ref[pl.ds(base + a * 64 + rest * 8, 8), :] = -combine(values, a)
        for a in range(4):
            for half in range(2):
                values = [flux_ref[1, pl.ds(base + a * 64 + b * 16 + half * 8, 8), :] for b in range(4)]
                third = [flux_ref[2, pl.ds(base + a * 64 + b * 16 + half * 8, 8), :] for b in range(4)]
                other = [flux_ref[2, pl.ds(base + a * 64 + b * 16 + (1 - half) * 8, 8), :] for b in range(4)]
                for b in range(4):
                    at = pl.ds(base + a * 64 + b * 16 + half * 8, 8)
                    same, far = third[b], other[b]
                    total = combine(values, b)
                    total = total + straight[half][half] * same
                    total = total + crossed[half][half] * pltpu.roll(same, 4, 0)
                    total = total + straight[half][1 - half] * far
                    total = total + crossed[half][1 - half] * pltpu.roll(far, 4, 0)
                    rate_ref[at, :] = rate_ref[at, :] - total
        return carry

    lax.fori_loop(0, 5, diverge, 0)

    def gather_terms(v, carry):
        base = pl.multiple_of(v * 256, 256)
        for block in range(BLOCKS):
            tiles = []
            for tile in range(8):
                old = register_ref[v, tile * 8 : tile * 8 + 8, tile_lanes(block)]
                rate = rate_ref[pl.ds(base + tile * 32 + block, 8, stride=BLOCKS), :]
                tiles.append(rate + SECTION_KEEP * old)
            lift(tiles, term_ref, field_ref, v, block)
        return carry

    lax.fori_loop(0, 5, gather_terms, 0)


def normal_flux(values, normal, length):
    density, momentum, energy = values[0], values[1:4], values[4]
    inverse = 1.0 / density
    velocity = [m * inverse for m in momentum]
    pressure = (HEAT_RATIO - 1.0) * (
        energy
        - 0.5 * (momentum[0] * velocity[0] + momentum[1] * velocity[1] + momentum[2] * velocity[2])
    )
    speed = velocity[0] * normal[0] + velocity[1] * normal[1] + velocity[2] * normal[2]
    terms = [density * speed]
    terms += [momentum[k] * speed + pressure * normal[k] for k in range(3)]
    terms += [(energy + pressure) * speed]
    wave = jnp.abs(speed) + jnp.sqrt(HEAT_RATIO * pressure * inverse) * length
    return terms, wave


def finish_kernel(
    place_ref,
    owner_hbm,
    other_hbm,
    own_hbm,
    side_ref,
    turn_ref,
    rate_ref,
    state_ref,
    relay_ref,
    section_hbm,
    advanced_hbm,
    low_ref,
    high_ref,
    section_ref,
    advanced_ref,
    board_ref,
    picked_ref,
    other_ref,
    own_ref,
    term_ref,
    field_ref,
    sems,
):
    plane, spot = place_ref[0], place_ref[1]
    window = CROSS * SLOTS
    low_slot = jnp.maximum(COLUMNS + ((plane - 1) * PLANE + NEAR) * SLOTS, 0)
    high_slot = jnp.minimum(COLUMNS + (plane + 1) * PLANE * SLOTS, COLUMNS + DEVICES * SLOTS - window)
    sources = [
        (owner_hbm.at[pl.ds(pl.multiple_of(low_slot, 512), window)], low_ref),
        (owner_hbm.at[pl.ds(pl.multiple_of(high_slot, 512), window)], high_ref),
        (other_hbm, other_ref),
        (own_hbm, own_ref),
    ]
    copies = [
        pltpu.make_async_copy(source, target, sems.at[k])
        for k, (source, target) in enumerate(sources)
    ]
    for copy in copies:
        copy.start()

    def receive(peer, block):
        parts = [relay_ref[block + k // 5, 8 * (k % 5) : 8 * (k % 5) + 8, :] for k in range(5 * BATCH)]
        rows = []
        for k in range(BATCH):
            rows += expand(parts[5 * k : 5 * k + 5])
        base = pl.multiple_of((peer + block + MARGIN) * SLOTS, SLOTS)
        for k in range(8 * BATCH):
            board_ref[pl.ds(base + 8 * k, 8), :] = rows[k]

    def receive_low(step, carry):
        receive((plane - 1) * PLANE, NEAR + step * BATCH)
        return carry

    def receive_high(step, carry):
        receive((plane + 1) * PLANE, step * BATCH)
        return carry

    lax.fori_loop(spot // BATCH, CROSS // BATCH, receive_low, 0)
    high = (jnp.maximum(spot - NEAR + 1, 0) + BATCH - 1) // BATCH
    lax.fori_loop(0, high, receive_high, 0)

    def place_rows(columns_ref, base, step):
        at = step * UNROLL
        columns = [columns_ref[at + k] for k in range(UNROLL)]
        rows = [board_ref[pl.ds(base * SLOTS + at + k, 1), :] for k in range(UNROLL)]
        for k in range(UNROLL):
            picked_ref[pl.ds(columns[k], 1), :] = rows[k]

    def place_low(step, carry):
        place_rows(low_ref, (plane - 1) * PLANE + NEAR + MARGIN, step)
        return carry

    def place_high(step, carry):
        place_rows(high_ref, (plane + 1) * PLANE + MARGIN, step)
        return carry

    chunk = SLOTS // UNROLL
    for copy in copies[:2]:
        copy.wait()

    @pl.when(plane > 0)
    def _():
        lax.fori_loop(spot * chunk, CROSS * chunk, place_low, 0)

    @pl.when(plane < 3)
    def _():
        lax.fori_loop(0, jnp.maximum(spot - NEAR + 1, 0) * chunk, place_high, 0)

    for copy in copies[2:]:
        copy.wait()

    top = jnp.max(jnp.max(relay_ref[:, MESSAGE:, :], axis=0))
    scale = CFL_NUMBER / top * SECTION_STEP

    def results(block):
        lanes = tile_lanes(block)
        pairs = ((section_ref, section_hbm), (advanced_ref, advanced_hbm))
        return [
            pltpu.make_async_copy(source.at[:, :, lanes], target.at[:, :, lanes], sems.at[2 * block + k])
            for k, (source, target) in enumerate(pairs)
        ]

    def element_block(block):
        for face in range(6):
            place = face * BLOCKS + block
            square = picked_ref[pl.ds(pl.multiple_of(place * LANES, LANES), LANES), :].T
            start = pl.multiple_of(place * TRACE, TRACE)
            side = pl.multiple_of(place * SIDE, 8)
            at = pl.multiple_of(place * 16, 16)
            turns = [turn_ref[pl.ds(at + half * 8, 8), :] for half in range(2)]
            late = turns[0] >= 16
            known = [
                jnp.where(late, square[8 * k : 8 * k + 8], other_ref[pl.ds(start + 8 * k, 8), :])
                for k in range(10)
            ]
            rows = side_ref[pl.ds(side + 16, 8), :]
            normal = [wide(rows[k : k + 1]) for k in range(3)]
            length = wide(rows[3:4])
            for half in range(2):
                upper = turns[half] % 16 >= 8
                sublane = turns[half] % 8
                far = []
                for v in range(5):
                    parts = [
                        jnp.take_along_axis(known[2 * v + k], sublane, axis=0, mode="promise_in_bounds")
                        for k in range(2)
                    ]
                    far.append(jnp.where(upper, parts[1], parts[0]))
                far_terms, far_wave = normal_flux(far, normal, length)
                bound = jnp.maximum(side_ref[pl.ds(side + half * 8, 8), :], far_wave)
                viscous = bound + length
                for v in range(5):
                    rows = pl.ds(start + v * 16 + half * 8, 8)
                    weight = bound if v == 0 else viscous
                    term_ref[rows, :] = (0.5 * LIFT_FACTOR) * (
                        weight * (far[v] - own_ref[rows, :]) - far_terms[v]
                    )
        lanes = tile_lanes(block)
        for v in range(5):
            base = block * 320 + v * 64
            tiles = [rate_ref[pl.ds(base + tile * 8, 8), :] for tile in range(8)]
            lift(tiles, term_ref, field_ref, v, block)
            for tile in range(8):
                nodes = slice(tile * 8, tile * 8 + 8)
                section = field_ref[pl.ds(base + tile * 8, 8), :]
                section_ref[v, nodes, lanes] = section
                advanced_ref[v, nodes, lanes] = state_ref[v, nodes, lanes] + scale * section
        for copy in results(block):
            copy.start()

    for block in range(BLOCKS):
        element_block(block)
    for block in range(BLOCKS):
        for copy in results(block):
            copy.wait()


def smem():
    return pl.BlockSpec(memory_space=pltpu.SMEM)


def vmem():
    return pl.BlockSpec(memory_space=pltpu.VMEM)


def params():
    return pltpu.CompilerParams(vmem_limit_bytes=VMEM_LIMIT)


def shape(*sizes):
    return jax.ShapeDtypeStruct(sizes, jnp.float32)


def scratch(*sizes):
    return pltpu.VMEM(sizes, jnp.float32)


def hbm():
    return pl.BlockSpec(memory_space=pltpu.HBM)


def anywhere():
    return pl.BlockSpec(memory_space=pl.ANY)


def in_hbm_shape(*sizes):
    return pltpu.HBM(sizes, jnp.float32)


def pack(place, partner, state):
    return pl.pallas_call(
        pack_kernel,
        out_shape=(
            in_hbm_shape(PLANE * MESSAGE, LANES),
            shape(CROSS * MESSAGE + 8, LANES),
            shape(CROSS * MESSAGE + 8, LANES),
            shape(8, LANES),
        ),
        in_specs=[smem(), hbm(), hbm()],
        out_specs=(hbm(), vmem(), vmem(), vmem()),
        scratch_shapes=[
            scratch(PLANE * MESSAGE, LANES),
            pltpu.SMEM((COLUMNS,), jnp.int32),
            scratch(5, 64, ELEMENTS),
            scratch(6, LANES, LANES),
            scratch(COLUMNS + (DEVICES + CROSS) * SLOTS, LANES),
            scratch(1280, LANES),
            pltpu.SemaphoreType.DMA((5 + PLANE // BATCH,)),
        ],
        compiler_params=params(),
        name="pack",
    )(place, partner, state)


def volume(place, state, register, metric, normal, code, partner):
    return pl.pallas_call(
        volume_kernel,
        out_shape=(
            shape(1280, LANES),
            in_hbm_shape(24 * TRACE, LANES),
            shape(24 * SIDE, LANES),
            jax.ShapeDtypeStruct((24 * 16, LANES), jnp.int32),
        ),
        in_specs=[smem()] + [vmem()] * 6,
        out_specs=(vmem(),) * 4,
        scratch_shapes=[
            scratch(1280, LANES),
            scratch(72, LANES),
            scratch(3, 1280, LANES),
            scratch(1280, LANES),
            scratch(1280, LANES),
            scratch(24 * TRACE, LANES),
        ],
        compiler_params=params(),
        name="volume",
    )(place, state, register, metric, normal, code, partner)


def relay(place, up, down, best, rate):
    return pl.pallas_call(
        relay_kernel,
        out_shape=(in_hbm_shape(PLANE, MESSAGE + 8, LANES), shape(8, LANES)),
        in_specs=[smem()] + [vmem()] * 3 + [anywhere()],
        out_specs=(vmem(), vmem()),
        compiler_params=params(),
        cost_estimate=pl.CostEstimate(flops=10**11, bytes_accessed=10**8, transcendentals=0),
        name="relay",
    )(place, up, down, best, rate)


def spread_top(three, far, relayed):
    return pl.pallas_call(
        top_kernel,
        out_shape=in_hbm_shape(PLANE, MESSAGE + 8, LANES),
        in_specs=[vmem(), vmem(), hbm()],
        out_specs=hbm(),
        scratch_shapes=[scratch(PLANE, 8, LANES), pltpu.SemaphoreType.DMA],
        input_output_aliases={2: 0},
        compiler_params=params(),
        name="top",
    )(three, far, relayed)


def early(place, partner, blank, state, plane):
    return pl.pallas_call(
        early_kernel,
        out_shape=(
            in_hbm_shape(24 * TRACE, LANES),
            pltpu.HBM((COLUMNS + DEVICES * SLOTS,), jnp.int32),
        ),
        in_specs=[smem(), smem(), anywhere(), vmem(), vmem()],
        out_specs=(vmem(), smem()),
        scratch_shapes=[
            scratch(COLUMNS + DEVICES * SLOTS, LANES),
            scratch(1280, LANES),
            scratch(COLUMNS, LANES),
            pltpu.SemaphoreType.DMA,
        ],
        compiler_params=params(),
        name="early",
    )(place, partner, blank, state, plane)


def finish(place, owner, other, own, side, turn, rate, state, relayed):
    held = [in_hbm(value) for value in (owner, other, own)]
    return pl.pallas_call(
        finish_kernel,
        out_shape=(in_hbm_shape(5, 64, ELEMENTS),) * 2,
        in_specs=[smem()] + [hbm()] * 3 + [vmem()] * 5,
        out_specs=(hbm(), hbm()),
        scratch_shapes=[
            pltpu.SMEM((CROSS * SLOTS,), jnp.int32),
            pltpu.SMEM((CROSS * SLOTS,), jnp.int32),
            scratch(5, 64, ELEMENTS),
            scratch(5, 64, ELEMENTS),
            scratch((DEVICES + 2 * MARGIN) * SLOTS, LANES),
            scratch(COLUMNS + 8, LANES),
            scratch(24 * TRACE, LANES),
            scratch(24 * TRACE, LANES),
            scratch(24 * TRACE, LANES),
            scratch(1280, LANES),
            pltpu.SemaphoreType.DMA((10,)),
        ],
        compiler_params=params(),
        name="finish",
    )(place, *held, side, turn, rate, state, relayed)


def in_hbm(value):
    return pltpu.with_memory_space_constraint(value, pltpu.HBM)


def in_vmem(value):
    return pltpu.with_memory_space_constraint(value, pltpu.VMEM)


def along_y(value, steps):
    return lax.ppermute(value, "y", [(i, (i + steps) % 4) for i in range(4)])


def on_device(state, register, metric, face_normal, partner, flip_code, face_role, send_face):
    plane = lax.axis_index("y").astype(jnp.int32)
    spot = lax.axis_index(("r", "x")).astype(jnp.int32)
    place = jnp.stack([plane, spot])
    state = state.transpose(1, 0, 2)
    rows = (COLUMNS // LANES, LANES)
    in_plane, up, down, best = pack(place, in_hbm(partner), in_hbm(state))
    from_below = along_y(up, 1)
    from_above = along_y(down, -1)
    far = along_y(best, 2)
    got = lax.all_to_all(in_plane, ("r", "x"), 0, 0, tiled=True)
    rate, own, side, turn = volume(
        place,
        state,
        register.transpose(1, 0, 2),
        metric,
        face_normal,
        flip_code.reshape(rows),
        partner.reshape(rows),
    )
    relayed, three = relay(place, from_below, from_above, best, rate)
    relayed = spread_top(three, far, in_hbm(relayed))
    relayed = lax.all_to_all(relayed, ("r", "x"), 0, 0, tiled=True)
    blank = jnp.full((COLUMNS + DEVICES * SLOTS,), COLUMNS, jnp.int32)
    other, owner = early(place, partner, blank, state, got)
    section, advanced = finish(place, owner, other, own, side, turn, rate, state, relayed)
    return section.transpose(1, 0, 2), advanced.transpose(1, 0, 2)


def solution(mesh):
    placed = (
        P(None, None, AXES),
        P(None, None, AXES),
        P(None, None, AXES),
        P(None, AXES),
        P(AXES),
        P(AXES),
        P(AXES),
        P(AXES, None, None),
    )
    return jax.shard_map(
        on_device,
        mesh=Mesh(mesh.devices.reshape(4, 8, 4), AXES),
        in_specs=placed,
        out_specs=(P(None, None, AXES), P(None, None, AXES)),
        check_vma=False,
    )
```

```python
import functools

import jax
import jax.numpy as jnp
import numpy as np
from jax import lax
from jax.experimental import pallas as pl
from jax.experimental.pallas import tpu as pltpu
from jax.sharding import Mesh
from jax.sharding import PartitionSpec as P

HEAT_RATIO = 1.4
LIFT_FACTOR = 6.0
CFL_NUMBER = 0.3
SECTION_KEEP = -0.4178904745
SECTION_STEP = 0.4432226
DEVICES = 128
ELEMENTS = 512
COLUMNS = 6 * ELEMENTS
SLOTS = 64
REACH = 24
LANES = 128
BLOCKS = ELEMENTS // LANES
TRACE = 80
GROUP = COLUMNS // 3
MESSAGE = TRACE * SLOTS // LANES
LONG = MESSAGE + 1
UNROLL = 32
SIDE = 24
BATCH = 4
AXES = ("y", "r", "x")
PLANE = 32
NEAR = PLANE - REACH
CROSS = REACH
MARGIN = PLANE
VMEM_LIMIT = 24 * 1024 * 1024


def derivative_matrix():
    points = np.array([-1.0, -1.0 / np.sqrt(5.0), 1.0 / np.sqrt(5.0), 1.0])
    weights = np.array(
        [
            1.0
            / np.prod([points[target] - points[source] for source in range(4) if source != target])
            for target in range(4)
        ]
    )
    matrix = np.zeros((4, 4))
    for target in range(4):
        for source in range(4):
            if target != source:
                matrix[target, source] = (
                    weights[source] / weights[target] / (points[target] - points[source])
                )
        matrix[target, target] = -np.sum(matrix[target])
    return matrix


def face_nodes(face):
    side = 3 * (face % 2)
    if face < 2:
        return [side * 16 + i * 4 + j for i in range(4) for j in range(4)]
    if face < 4:
        return [i * 16 + side * 4 + j for i in range(4) for j in range(4)]
    return [i * 16 + j * 4 + side for i in range(4) for j in range(4)]


def tile_lanes(block):
    return pl.ds(aligned(block * LANES, LANES), LANES)


def spread_nodes(state_ref, rows_ref):
    for v in range(5):
        for tile in range(8):
            for block in range(BLOCKS):
                rows_ref[pl.ds(v * 256 + tile * 32 + block, 8, stride=BLOCKS), :] = state_ref[
                    v, tile * 8 : tile * 8 + 8, tile_lanes(block)
                ]


def face_rows(state_ref, flat_ref, v, face, block):
    side = 3 * (face % 2)
    lanes = tile_lanes(block)
    if face < 2:
        return state_ref[v, side * 16 : side * 16 + 16, lanes]
    if face < 4:
        return jnp.concatenate(
            [state_ref[v, i * 16 + side * 4 : i * 16 + side * 4 + 4, lanes] for i in range(4)], axis=0
        )
    return flat_ref[pl.ds(aligned(block * 320, 64) + v * 64 + side, 16, stride=4), :]


def aligned(row, step=8):
    return row if isinstance(row, int) else pl.multiple_of(row, step)


def lane_index(shape):
    return lax.broadcasted_iota(jnp.int32, shape, 1)


def compact(rows):
    lane = lane_index((8, LANES))
    low = lane < 80
    mid = lane < 112

    def turn(value, shift):
        return pltpu.roll(value, shift, 1)

    first = [jnp.where(low, rows[k], turn(rows[5 + k], 80)) for k in range(3)]
    fourth = jnp.where(low, rows[3], jnp.where(mid, turn(rows[5], 32), turn(rows[7], 64)))
    fifth = jnp.where(low, rows[4], jnp.where(mid, turn(rows[6], 32), turn(rows[7], 48)))
    return first + [fourth, fifth]


def expand(parts):
    lane = lane_index((8, LANES))
    head = lane < 48
    body = lane < 64

    def turn(value, shift):
        return pltpu.roll(value, shift, 1)

    sixth = jnp.where(head, turn(parts[0], 48), turn(parts[3], 96))
    seventh = jnp.where(head, turn(parts[1], 48), turn(parts[4], 96))
    eighth = jnp.where(
        head, turn(parts[2], 48), jnp.where(body, turn(parts[3], 64), turn(parts[4], 80))
    )
    return list(parts) + [sixth, seventh, eighth]


def compact_into(board_ref, base, to_ref, at):
    rows = [board_ref[pl.ds(base + 8 * k, 8), :] for k in range(8 * BATCH)]
    parts = []
    for block in range(BATCH):
        parts += compact(rows[8 * block : 8 * block + 8])
    for k in range(5 * BATCH):
        to_ref[pl.ds(at + 8 * k, 8), :] = parts[k]


def expand_into(from_ref, start, board_ref, base):
    parts = [from_ref[pl.ds(start + 8 * k, 8), :] for k in range(5 * BATCH)]
    rows = []
    for block in range(BATCH):
        rows += expand(parts[5 * block : 5 * block + 5])
    for k in range(8 * BATCH):
        board_ref[pl.ds(base + 8 * k, 8), :] = rows[k]


def spread_flat(state_ref, flat_ref):
    for block in range(BLOCKS):
        for v in range(5):
            at = block * 320 + v * 64
            flat_ref[at : at + 64, :] = state_ref[v, :, tile_lanes(block)]


def face_trace(state_ref, flat_ref, face, block):
    return jnp.concatenate([face_rows(state_ref, flat_ref, v, face, block) for v in range(5)], axis=0)


def build_tables(state_ref, flat_ref, table_ref):
    spread_flat(state_ref, flat_ref)
    padding = jnp.zeros((LANES - TRACE, LANES), jnp.float32)
    for face in range(6):
        for block in range(BLOCKS):
            trace = face_trace(state_ref, flat_ref, face, block)
            place = face * BLOCKS + block
            square = jnp.concatenate([trace, padding], axis=0)
            table_ref[place * LANES : (place + 1) * LANES, :] = square.T


def pack_kernel(
    place_ref,
    partner_hbm,
    state_hbm,
    plane_hbm,
    up_ref,
    down_ref,
    best_ref,
    plane_ref,
    partner_ref,
    state_ref,
    table_ref,
    board_ref,
    flat_ref,
    sems,
):
    copies = [pltpu.make_async_copy(partner_hbm, partner_ref, sems.at[0])]
    for a in range(4):
        nodes = pl.ds(a * 16, 16)
        copies.append(
            pltpu.make_async_copy(state_hbm.at[:, nodes, :], state_ref.at[:, nodes, :], sems.at[1 + a])
        )
    for copy in copies:
        copy.start()
    for copy in copies[1:]:
        copy.wait()
    spread_flat(state_ref, flat_ref)
    copies[0].wait()
    padding = jnp.zeros((LANES - TRACE, LANES), jnp.float32)

    def build(face, block, slot):
        square = jnp.concatenate([face_trace(state_ref, flat_ref, face, block), padding], axis=0)
        table_ref[slot] = square.T

    def scatter(block):
        for face in range(6):
            build(face, block, face)
            base = face * ELEMENTS + block * LANES
            for start in range(0, LANES, UNROLL):
                targets = [partner_ref[base + start + k] for k in range(UNROLL)]
                rows = [table_ref[face, start + k : start + k + 1, :] for k in range(UNROLL)]
                for k in range(UNROLL):
                    board_ref[pl.ds(targets[k], 1), :] = rows[k]

    for block in range(BLOCKS):
        scatter(block)

    def speeds(step, best):
        density, mom_x, mom_y, mom_z, energy = [
            state_ref[v, pl.ds(pl.multiple_of(step * 8, 8), 8), :] for v in range(5)
        ]
        inverse = 1.0 / density
        square = (mom_x * mom_x + mom_y * mom_y + mom_z * mom_z) * inverse
        pressure = (HEAT_RATIO - 1.0) * (energy - 0.5 * square)
        wave = jnp.sqrt(square * inverse) + jnp.sqrt(HEAT_RATIO * pressure * inverse)
        return jnp.maximum(best, wave)

    best = lax.fori_loop(0, 8, speeds, jnp.zeros((8, ELEMENTS), jnp.float32))
    best = jnp.maximum(
        jnp.maximum(best[:, tile_lanes(0)], best[:, tile_lanes(1)]),
        jnp.maximum(best[:, tile_lanes(2)], best[:, tile_lanes(3)]),
    )
    best_ref[...] = best
    up_ref[CROSS * MESSAGE :, :] = best
    down_ref[CROSS * MESSAGE :, :] = best
    plane, spot = place_ref[0], place_ref[1]

    def send(to_ref, peer, step):
        base = pl.multiple_of(COLUMNS + (peer + step * BATCH) * SLOTS, SLOTS)
        compact_into(board_ref, base, to_ref, aligned(step * BATCH * MESSAGE))

    def send_up(step, carry):
        send(up_ref, (plane + 1) * PLANE, step)
        return carry

    def send_down(step, carry):
        send(down_ref, (plane - 1) * PLANE + NEAR, step)
        return carry

    sent = []
    for step in range(PLANE // BATCH):
        send(plane_ref, plane * PLANE, step)
        part = pl.ds(step * BATCH * MESSAGE, BATCH * MESSAGE)
        sent.append(
            pltpu.make_async_copy(plane_ref.at[part, :], plane_hbm.at[part, :], sems.at[5 + step])
        )
        sent[-1].start()
    upward = (jnp.maximum(spot - NEAR + 1, 0) + BATCH - 1) // BATCH
    lax.fori_loop(0, jnp.where(plane < 3, upward, 0), send_up, 0)
    lax.fori_loop(jnp.where(plane > 0, spot // BATCH, CROSS // BATCH), CROSS // BATCH, send_down, 0)
    for copy in sent:
        copy.wait()


def relay_kernel(place_ref, up_ref, down_ref, best_ref, rate_hbm, relay_ref, three_ref):
    spot = place_ref[1]
    for block in range(PLANE):
        for k in range(5):
            if block < CROSS:
                value = up_ref[block * MESSAGE + 8 * k : block * MESSAGE + 8 * k + 8, :]
            if block >= NEAR:
                at = (block - NEAR) * MESSAGE + 8 * k
                other = down_ref[at : at + 8, :]
                value = other if block >= CROSS else jnp.where(block <= spot - NEAR, value, other)
            relay_ref[block * LONG + 8 * k : block * LONG + 8 * k + 8, :] = value
    three_ref[...] = jnp.maximum(
        best_ref[...], jnp.maximum(up_ref[CROSS * MESSAGE :, :], down_ref[CROSS * MESSAGE :, :])
    )


def top_kernel(three_ref, far_ref, relay_in, relay_hbm, top_ref, sems):
    top = jnp.max(jnp.maximum(three_ref[...], far_ref[...]), axis=0, keepdims=True)
    top_ref[0] = top
    copies = [
        pltpu.make_async_copy(top_ref, relay_hbm.at[pl.ds(block * LONG + MESSAGE, 1)], sems.at[block])
        for block in range(PLANE)
    ]
    for copy in copies:
        copy.start()
    for copy in copies:
        copy.wait()


def early_kernel(
    place_ref,
    partner_ref,
    blank_hbm,
    state_ref,
    plane_ref,
    other_ref,
    owner_ref,
    board_ref,
    flat_ref,
    picked_ref,
    sem,
):
    plane, spot = place_ref[0], place_ref[1]
    blank = pltpu.make_async_copy(blank_hbm, owner_ref, sem)
    blank.start()
    build_tables(state_ref, flat_ref, board_ref)

    def receive(step, carry):
        start = pl.multiple_of(step * BATCH * MESSAGE, 8)
        base = pl.multiple_of(COLUMNS + (plane * PLANE + step * BATCH) * SLOTS, SLOTS)
        expand_into(plane_ref, start, board_ref, base)
        return carry

    lax.fori_loop(jnp.maximum(spot - REACH, 0) // BATCH, PLANE // BATCH, receive, 0)

    def gather(step, carry):
        base = step * UNROLL
        indices = [partner_ref[base + k] for k in range(UNROLL)]
        rows = [board_ref[pl.ds(index, 1), :] for index in indices]
        for k in range(UNROLL):
            picked_ref[pl.ds(base + k, 1), :] = rows[k]
            owner_ref[indices[k]] = base + k
        return carry

    blank.wait()
    lax.fori_loop(0, COLUMNS // UNROLL, gather, 0)
    for place in range(COLUMNS // LANES):
        square = picked_ref[place * LANES : (place + 1) * LANES, :].T
        other_ref[place * TRACE : (place + 1) * TRACE, :] = square[0:TRACE]


def sublane_index():
    return lax.broadcasted_iota(jnp.int32, (8, LANES), 0)


def wide(row):
    return jnp.broadcast_to(row, (8, LANES))


def face_normals(normal_ref, place):
    lanes = pl.ds(pl.multiple_of(place * LANES, LANES), LANES)
    normal = [wide(normal_ref[k : k + 1, lanes]) for k in range(3)]
    length = jnp.sqrt(normal[0] * normal[0] + normal[1] * normal[1] + normal[2] * normal[2])
    return normal, length


def lift(tiles, flux_ref, field_ref, v, block):
    first = sublane_index() < 4

    def piece(face, half):
        start = aligned((face * BLOCKS + block) * TRACE + v * 16)
        return flux_ref[pl.ds(start + half * 8, 8), :]

    tiles = list(tiles)
    for half in range(2):
        tiles[half] = tiles[half] + piece(0, half)
        tiles[6 + half] = tiles[6 + half] + piece(1, half)
        low, high = piece(2, half), piece(3, half)
        tiles[4 * half] = tiles[4 * half] + jnp.where(first, low, 0.0)
        tiles[4 * half + 2] = tiles[4 * half + 2] + jnp.where(first, pltpu.roll(low, 4, 0), 0.0)
        tiles[4 * half + 1] = tiles[4 * half + 1] + jnp.where(first, 0.0, pltpu.roll(high, 4, 0))
        tiles[4 * half + 3] = tiles[4 * half + 3] + jnp.where(first, 0.0, high)
    base = aligned(v * 64 + block * 320)
    for tile in range(8):
        field_ref[pl.ds(base + tile * 8, 8), :] = tiles[tile]
    for half in range(2):
        for face in (4, 5):
            nodes = pl.ds(base + half * 32 + 3 * (face - 4), 8, stride=4)
            field_ref[nodes, :] = field_ref[nodes, :] + piece(face, half)


def turn_indices(code):
    flip_first = jnp.where(code % 2 == 1, 3, 0)
    flip_second = jnp.where((code // 2) % 2 == 1, 3, 0)
    swapped = code >= 4
    sublane = sublane_index()
    result = []
    for half in range(2):
        i, j = 2 * half + sublane // 4, sublane % 4
        first = jnp.where(swapped, j, i) ^ flip_first
        second = jnp.where(swapped, i, j) ^ flip_second
        result.append(first * 4 + second)
    return result


def volume_kernel(
    place_ref,
    state_ref,
    register_ref,
    metric_ref,
    normal_ref,
    code_ref,
    partner_ref,
    field_ref,
    own_ref,
    side_ref,
    turn_ref,
    rows_ref,
    tensor_ref,
    flux_ref,
    flat_ref,
    rate_ref,
    term_ref,
):
    low = COLUMNS + place_ref[0] * (PLANE * SLOTS)
    spread_nodes(state_ref, rows_ref)
    spread_flat(state_ref, flat_ref)
    for face in range(6):
        for block in range(BLOCKS):
            place = face * BLOCKS + block
            own_ref[place * TRACE : (place + 1) * TRACE, :] = face_trace(state_ref, flat_ref, face, block)

    def own_fluxes(face, carry):
        for block in range(BLOCKS):
            place = face * BLOCKS + block
            normal, length = face_normals(normal_ref, place)
            start = pl.multiple_of(place * TRACE, TRACE)
            side = pl.multiple_of(place * SIDE, 8)
            rows = [value[0:1] for value in normal + [length]]
            side_ref[pl.ds(side + 16, 8), :] = jnp.concatenate(rows + rows, axis=0)
            partner = wide(partner_ref[pl.ds(place, 1), :])
            late = (partner >= COLUMNS) & ((partner < low) | (partner >= low + PLANE * SLOTS))
            late = jnp.where(late, 16, 0)
            for half, turn in enumerate(turn_indices(wide(code_ref[pl.ds(place, 1), :]))):
                turn_ref[pl.ds(pl.multiple_of(place * 16, 16) + half * 8, 8), :] = turn + late
            for half in range(2):
                at = start + half * 8
                own = [own_ref[pl.ds(at + v * 16, 8), :] for v in range(5)]
                terms, wave = normal_flux(own, normal, length)
                for v in range(5):
                    term_ref[pl.ds(at + v * 16, 8), :] = (0.5 * LIFT_FACTOR) * terms[v]
                side_ref[pl.ds(side + half * 8, 8), :] = wave
        return carry

    lax.fori_loop(0, 6, own_fluxes, 0)
    for direction in range(3):
        for half in range(2):
            for block in range(BLOCKS):
                tensor_ref[pl.ds(direction * 24 + half * 4 + block, 3, stride=8), :] = metric_ref[
                    direction, :, block * LANES : (block + 1) * LANES
                ]

    def fluxes(step, carry):
        at = pl.multiple_of(step * 8, 8)
        density, mom_x, mom_y, mom_z, energy = [
            rows_ref[pl.ds(v * 256 + at, 8), :] for v in range(5)
        ]
        inverse = 1.0 / density
        momentum = [mom_x, mom_y, mom_z]
        velocity = [m * inverse for m in momentum]
        pressure = (HEAT_RATIO - 1.0) * (
            energy
            - 0.5 * (mom_x * velocity[0] + mom_y * velocity[1] + mom_z * velocity[2])
        )
        enthalpy = energy + pressure
        for direction in range(3):
            tensor = [tensor_ref[direction * 24 + k * 8 : direction * 24 + k * 8 + 8, :] for k in range(3)]
            along = tensor[0] * velocity[0] + tensor[1] * velocity[1] + tensor[2] * velocity[2]
            values = [density * along]
            values += [momentum[k] * along + pressure * tensor[k] for k in range(3)]
            values += [enthalpy * along]
            for v in range(5):
                flux_ref[direction, pl.ds(v * 256 + at, 8), :] = values[v]
        return carry

    lax.fori_loop(0, 32, fluxes, 0)
    matrix = derivative_matrix()
    upper = lax.broadcasted_iota(jnp.int32, (8, LANES), 0) < 4

    def pair(first, second):
        return jnp.where(upper, jnp.float32(first), jnp.float32(second))

    straight = [[pair(matrix[2 * t, 2 * s], matrix[2 * t + 1, 2 * s + 1]) for s in range(2)] for t in range(2)]
    crossed = [[pair(matrix[2 * t, 2 * s + 1], matrix[2 * t + 1, 2 * s]) for s in range(2)] for t in range(2)]

    def combine(values, target):
        total = values[0] * float(matrix[target, 0])
        for source in range(1, 4):
            total = total + values[source] * float(matrix[target, source])
        return total

    def diverge(v, carry):
        base = pl.multiple_of(v * 256, 256)
        for rest in range(8):
            values = [flux_ref[0, pl.ds(base + a * 64 + rest * 8, 8), :] for a in range(4)]
            for a in range(4):
                rate_ref[pl.ds(base + a * 64 + rest * 8, 8), :] = -combine(values, a)
        for a in range(4):
            for half in range(2):
                values = [flux_ref[1, pl.ds(base + a * 64 + b * 16 + half * 8, 8), :] for b in range(4)]
                third = [flux_ref[2, pl.ds(base + a * 64 + b * 16 + half * 8, 8), :] for b in range(4)]
                other = [flux_ref[2, pl.ds(base + a * 64 + b * 16 + (1 - half) * 8, 8), :] for b in range(4)]
                for b in range(4):
                    at = pl.ds(base + a * 64 + b * 16 + half * 8, 8)
                    same, far = third[b], other[b]
                    total = combine(values, b)
                    total = total + straight[half][half] * same
                    total = total + crossed[half][half] * pltpu.roll(same, 4, 0)
                    total = total + straight[half][1 - half] * far
                    total = total + crossed[half][1 - half] * pltpu.roll(far, 4, 0)
                    rate_ref[at, :] = rate_ref[at, :] - total
        return carry

    lax.fori_loop(0, 5, diverge, 0)

    def gather_terms(v, carry):
        base = pl.multiple_of(v * 256, 256)
        for block in range(BLOCKS):
            tiles = []
            for tile in range(8):
                old = register_ref[v, tile * 8 : tile * 8 + 8, tile_lanes(block)]
                rate = rate_ref[pl.ds(base + tile * 32 + block, 8, stride=BLOCKS), :]
                tiles.append(rate + SECTION_KEEP * old)
            lift(tiles, term_ref, field_ref, v, block)
        return carry

    lax.fori_loop(0, 5, gather_terms, 0)


def normal_flux(values, normal, length):
    density, momentum, energy = values[0], values[1:4], values[4]
    inverse = 1.0 / density
    velocity = [m * inverse for m in momentum]
    pressure = (HEAT_RATIO - 1.0) * (
        energy
        - 0.5 * (momentum[0] * velocity[0] + momentum[1] * velocity[1] + momentum[2] * velocity[2])
    )
    speed = velocity[0] * normal[0] + velocity[1] * normal[1] + velocity[2] * normal[2]
    terms = [density * speed]
    terms += [momentum[k] * speed + pressure * normal[k] for k in range(3)]
    terms += [(energy + pressure) * speed]
    wave = jnp.abs(speed) + jnp.sqrt(HEAT_RATIO * pressure * inverse) * length
    return terms, wave


def finish_kernel(
    place_ref,
    owner_hbm,
    other_hbm,
    own_hbm,
    side_ref,
    turn_ref,
    rate_ref,
    state_ref,
    relay_ref,
    section_hbm,
    advanced_hbm,
    low_ref,
    high_ref,
    section_ref,
    advanced_ref,
    board_ref,
    picked_ref,
    other_ref,
    own_ref,
    term_ref,
    field_ref,
    sems,
):
    plane, spot = place_ref[0], place_ref[1]
    window = CROSS * SLOTS
    low_slot = jnp.maximum(COLUMNS + ((plane - 1) * PLANE + NEAR) * SLOTS, 0)
    high_slot = jnp.minimum(COLUMNS + (plane + 1) * PLANE * SLOTS, COLUMNS + DEVICES * SLOTS - window)
    sources = [
        (owner_hbm.at[pl.ds(pl.multiple_of(low_slot, 512), window)], low_ref),
        (owner_hbm.at[pl.ds(pl.multiple_of(high_slot, 512), window)], high_ref),
        (other_hbm, other_ref),
        (own_hbm, own_ref),
    ]
    copies = [
        pltpu.make_async_copy(source, target, sems.at[k])
        for k, (source, target) in enumerate(sources)
    ]
    for copy in copies:
        copy.start()

    def receive(blocks):
        parts = [relay_ref[b * LONG + 8 * k : b * LONG + 8 * k + 8, :] for b in blocks for k in range(5)]
        rows = []
        for k in range(BATCH):
            rows += expand(parts[5 * k : 5 * k + 5])
        for k, block in enumerate(blocks):
            side = jnp.where(block >= spot + NEAR, plane - 1, plane + 1)
            base = pl.multiple_of((side * PLANE + block + MARGIN) * SLOTS, SLOTS)
            for j in range(8):
                board_ref[pl.ds(base + 8 * j, 8), :] = rows[8 * k + j]

    for first in range(0, PLANE, BATCH):
        last = first + BATCH - 1

        @pl.when((first <= spot - NEAR) | (last >= spot + NEAR))
        def _(first=first):
            receive(range(first, first + BATCH))

    def place_rows(columns_ref, base, step):
        at = step * UNROLL
        columns = [columns_ref[at + k] for k in range(UNROLL)]
        rows = [board_ref[pl.ds(base * SLOTS + at + k, 1), :] for k in range(UNROLL)]
        for k in range(UNROLL):
            picked_ref[pl.ds(columns[k], 1), :] = rows[k]

    def place_low(step, carry):
        place_rows(low_ref, (plane - 1) * PLANE + NEAR + MARGIN, step)
        return carry

    def place_high(step, carry):
        place_rows(high_ref, (plane + 1) * PLANE + MARGIN, step)
        return carry

    chunk = SLOTS // UNROLL
    for copy in copies[:2]:
        copy.wait()

    @pl.when(plane > 0)
    def _():
        lax.fori_loop(spot * chunk, CROSS * chunk, place_low, 0)

    @pl.when(plane < 3)
    def _():
        lax.fori_loop(0, jnp.maximum(spot - NEAR + 1, 0) * chunk, place_high, 0)

    for copy in copies[2:]:
        copy.wait()

    tops = [relay_ref[b * LONG + MESSAGE : (b + 1) * LONG, :] for b in range(PLANE)]
    top = jnp.max(functools.reduce(jnp.maximum, tops))
    scale = CFL_NUMBER / top * SECTION_STEP

    def results(block):
        lanes = tile_lanes(block)
        pairs = ((section_ref, section_hbm), (advanced_ref, advanced_hbm))
        return [
            pltpu.make_async_copy(source.at[:, :, lanes], target.at[:, :, lanes], sems.at[2 * block + k])
            for k, (source, target) in enumerate(pairs)
        ]

    def element_block(block):
        for face in range(6):
            place = face * BLOCKS + block
            square = picked_ref[pl.ds(pl.multiple_of(place * LANES, LANES), LANES), :].T
            start = pl.multiple_of(place * TRACE, TRACE)
            side = pl.multiple_of(place * SIDE, 8)
            at = pl.multiple_of(place * 16, 16)
            turns = [turn_ref[pl.ds(at + half * 8, 8), :] for half in range(2)]
            late = turns[0] >= 16
            known = [
                jnp.where(late, square[8 * k : 8 * k + 8], other_ref[pl.ds(start + 8 * k, 8), :])
                for k in range(10)
            ]
            rows = side_ref[pl.ds(side + 16, 8), :]
            normal = [wide(rows[k : k + 1]) for k in range(3)]
            length = wide(rows[3:4])
            for half in range(2):
                upper = turns[half] % 16 >= 8
                sublane = turns[half] % 8
                far = []
                for v in range(5):
                    parts = [
                        jnp.take_along_axis(known[2 * v + k], sublane, axis=0, mode="promise_in_bounds")
                        for k in range(2)
                    ]
                    far.append(jnp.where(upper, parts[1], parts[0]))
                far_terms, far_wave = normal_flux(far, normal, length)
                bound = jnp.maximum(side_ref[pl.ds(side + half * 8, 8), :], far_wave)
                viscous = bound + length
                for v in range(5):
                    rows = pl.ds(start + v * 16 + half * 8, 8)
                    weight = bound if v == 0 else viscous
                    term_ref[rows, :] = (0.5 * LIFT_FACTOR) * (
                        weight * (far[v] - own_ref[rows, :]) - far_terms[v]
                    )
        lanes = tile_lanes(block)
        for v in range(5):
            base = block * 320 + v * 64
            tiles = [rate_ref[pl.ds(base + tile * 8, 8), :] for tile in range(8)]
            lift(tiles, term_ref, field_ref, v, block)
            for tile in range(8):
                nodes = slice(tile * 8, tile * 8 + 8)
                section = field_ref[pl.ds(base + tile * 8, 8), :]
                section_ref[v, nodes, lanes] = section
                advanced_ref[v, nodes, lanes] = state_ref[v, nodes, lanes] + scale * section
        for copy in results(block):
            copy.start()

    for block in range(BLOCKS):
        element_block(block)
    for block in range(BLOCKS):
        for copy in results(block):
            copy.wait()


def smem():
    return pl.BlockSpec(memory_space=pltpu.SMEM)


def vmem():
    return pl.BlockSpec(memory_space=pltpu.VMEM)


def params():
    return pltpu.CompilerParams(vmem_limit_bytes=VMEM_LIMIT)


def shape(*sizes):
    return jax.ShapeDtypeStruct(sizes, jnp.float32)


def scratch(*sizes):
    return pltpu.VMEM(sizes, jnp.float32)


def hbm():
    return pl.BlockSpec(memory_space=pltpu.HBM)


def anywhere():
    return pl.BlockSpec(memory_space=pl.ANY)


def in_hbm_shape(*sizes):
    return pltpu.HBM(sizes, jnp.float32)


def pack(place, partner, state):
    return pl.pallas_call(
        pack_kernel,
        out_shape=(
            in_hbm_shape(PLANE * MESSAGE, LANES),
            shape(CROSS * MESSAGE + 8, LANES),
            shape(CROSS * MESSAGE + 8, LANES),
            shape(8, LANES),
        ),
        in_specs=[smem(), hbm(), hbm()],
        out_specs=(hbm(), vmem(), vmem(), vmem()),
        scratch_shapes=[
            scratch(PLANE * MESSAGE, LANES),
            pltpu.SMEM((COLUMNS,), jnp.int32),
            scratch(5, 64, ELEMENTS),
            scratch(6, LANES, LANES),
            scratch(COLUMNS + (DEVICES + CROSS) * SLOTS, LANES),
            scratch(1280, LANES),
            pltpu.SemaphoreType.DMA((5 + PLANE // BATCH,)),
        ],
        compiler_params=params(),
        name="pack",
    )(place, partner, state)


def volume(place, state, register, metric, normal, code, partner):
    return pl.pallas_call(
        volume_kernel,
        out_shape=(
            shape(1280, LANES),
            in_hbm_shape(24 * TRACE, LANES),
            shape(24 * SIDE, LANES),
            jax.ShapeDtypeStruct((24 * 16, LANES), jnp.int32),
        ),
        in_specs=[smem()] + [vmem()] * 6,
        out_specs=(vmem(),) * 4,
        scratch_shapes=[
            scratch(1280, LANES),
            scratch(72, LANES),
            scratch(3, 1280, LANES),
            scratch(1280, LANES),
            scratch(1280, LANES),
            scratch(24 * TRACE, LANES),
        ],
        compiler_params=params(),
        name="volume",
    )(place, state, register, metric, normal, code, partner)


def relay(place, up, down, best, rate):
    return pl.pallas_call(
        relay_kernel,
        out_shape=(in_hbm_shape(PLANE * LONG, LANES), shape(8, LANES)),
        in_specs=[smem()] + [vmem()] * 3 + [anywhere()],
        out_specs=(vmem(), vmem()),
        compiler_params=params(),
        cost_estimate=pl.CostEstimate(flops=10**11, bytes_accessed=10**8, transcendentals=0),
        name="relay",
    )(place, up, down, best, rate)


def spread_top(three, far, relayed):
    return pl.pallas_call(
        top_kernel,
        out_shape=in_hbm_shape(PLANE * LONG, 1, LANES),
        in_specs=[vmem(), vmem(), hbm()],
        out_specs=hbm(),
        scratch_shapes=[scratch(1, 1, LANES), pltpu.SemaphoreType.DMA((PLANE,))],
        input_output_aliases={2: 0},
        compiler_params=params(),
        name="top",
    )(three, far, relayed)


def early(place, partner, blank, state, plane):
    return pl.pallas_call(
        early_kernel,
        out_shape=(
            in_hbm_shape(24 * TRACE, LANES),
            pltpu.HBM((COLUMNS + DEVICES * SLOTS,), jnp.int32),
        ),
        in_specs=[smem(), smem(), anywhere(), vmem(), vmem()],
        out_specs=(vmem(), smem()),
        scratch_shapes=[
            scratch(COLUMNS + DEVICES * SLOTS, LANES),
            scratch(1280, LANES),
            scratch(COLUMNS, LANES),
            pltpu.SemaphoreType.DMA,
        ],
        compiler_params=params(),
        name="early",
    )(place, partner, blank, state, plane)


def finish(place, owner, other, own, side, turn, rate, state, relayed):
    held = [in_hbm(value) for value in (owner, other, own)]
    return pl.pallas_call(
        finish_kernel,
        out_shape=(in_hbm_shape(5, 64, ELEMENTS),) * 2,
        in_specs=[smem()] + [hbm()] * 3 + [vmem()] * 5,
        out_specs=(hbm(), hbm()),
        scratch_shapes=[
            pltpu.SMEM((CROSS * SLOTS,), jnp.int32),
            pltpu.SMEM((CROSS * SLOTS,), jnp.int32),
            scratch(5, 64, ELEMENTS),
            scratch(5, 64, ELEMENTS),
            scratch((DEVICES + 2 * MARGIN) * SLOTS, LANES),
            scratch(COLUMNS + 8, LANES),
            scratch(24 * TRACE, LANES),
            scratch(24 * TRACE, LANES),
            scratch(24 * TRACE, LANES),
            scratch(1280, LANES),
            pltpu.SemaphoreType.DMA((10,)),
        ],
        compiler_params=params(),
        name="finish",
    )(place, *held, side, turn, rate, state, relayed)


def in_hbm(value):
    return pltpu.with_memory_space_constraint(value, pltpu.HBM)


def in_vmem(value):
    return pltpu.with_memory_space_constraint(value, pltpu.VMEM)


def along_y(value, steps):
    return lax.ppermute(value, "y", [(i, (i + steps) % 4) for i in range(4)])


def on_device(state, register, metric, face_normal, partner, flip_code, face_role, send_face):
    plane = lax.axis_index("y").astype(jnp.int32)
    spot = lax.axis_index(("r", "x")).astype(jnp.int32)
    place = jnp.stack([plane, spot])
    state = state.transpose(1, 0, 2)
    rows = (COLUMNS // LANES, LANES)
    in_plane, up, down, best = pack(place, in_hbm(partner), in_hbm(state))
    from_below = along_y(up, 1)
    from_above = along_y(down, -1)
    far = along_y(best, 2)
    got = lax.all_to_all(in_plane, ("r", "x"), 0, 0, tiled=True)
    rate, own, side, turn = volume(
        place,
        state,
        register.transpose(1, 0, 2),
        metric,
        face_normal,
        flip_code.reshape(rows),
        partner.reshape(rows),
    )
    relayed, three = relay(place, from_below, from_above, best, rate)
    relayed = spread_top(three, far, in_hbm(relayed.reshape(PLANE * LONG, 1, LANES))).reshape(PLANE, LONG, 1, LANES)
    relayed = lax.all_to_all(relayed, ("r", "x"), 0, 0, tiled=True).reshape(PLANE * LONG, LANES)
    blank = jnp.full((COLUMNS + DEVICES * SLOTS,), COLUMNS, jnp.int32)
    other, owner = early(place, partner, blank, state, got)
    section, advanced = finish(place, owner, other, own, side, turn, rate, state, relayed)
    return section.transpose(1, 0, 2), advanced.transpose(1, 0, 2)


def solution(mesh):
    placed = (
        P(None, None, AXES),
        P(None, None, AXES),
        P(None, None, AXES),
        P(None, AXES),
        P(AXES),
        P(AXES),
        P(AXES),
        P(AXES, None, None),
    )
    return jax.shard_map(
        on_device,
        mesh=Mesh(mesh.devices.reshape(4, 8, 4), AXES),
        in_specs=placed,
        out_specs=(P(None, None, AXES), P(None, None, AXES)),
        check_vma=False,
    )
```

```python
import functools

import jax
import jax.numpy as jnp
import numpy as np
from jax import lax
from jax.experimental import pallas as pl
from jax.experimental.pallas import tpu as pltpu
from jax.sharding import Mesh
from jax.sharding import PartitionSpec as P

HEAT_RATIO = 1.4
LIFT_FACTOR = 6.0
CFL_NUMBER = 0.3
SECTION_KEEP = -0.4178904745
SECTION_STEP = 0.4432226
DEVICES = 128
ELEMENTS = 512
COLUMNS = 6 * ELEMENTS
SLOTS = 64
REACH = 24
LANES = 128
BLOCKS = ELEMENTS // LANES
TRACE = 80
GROUP = COLUMNS // 3
MESSAGE = TRACE * SLOTS // LANES
LONG = MESSAGE + 1
UNROLL = 32
SIDE = 24
BATCH = 4
AXES = ("y", "r", "x")
PLANE = 32
NEAR = PLANE - REACH
CROSS = REACH
MARGIN = PLANE
VMEM_LIMIT = 24 * 1024 * 1024


def derivative_matrix():
    points = np.array([-1.0, -1.0 / np.sqrt(5.0), 1.0 / np.sqrt(5.0), 1.0])
    weights = np.array(
        [
            1.0
            / np.prod([points[target] - points[source] for source in range(4) if source != target])
            for target in range(4)
        ]
    )
    matrix = np.zeros((4, 4))
    for target in range(4):
        for source in range(4):
            if target != source:
                matrix[target, source] = (
                    weights[source] / weights[target] / (points[target] - points[source])
                )
        matrix[target, target] = -np.sum(matrix[target])
    return matrix


def face_nodes(face):
    side = 3 * (face % 2)
    if face < 2:
        return [side * 16 + i * 4 + j for i in range(4) for j in range(4)]
    if face < 4:
        return [i * 16 + side * 4 + j for i in range(4) for j in range(4)]
    return [i * 16 + j * 4 + side for i in range(4) for j in range(4)]


def tile_lanes(block):
    return pl.ds(aligned(block * LANES, LANES), LANES)


def spread_nodes(state_ref, rows_ref):
    for v in range(5):
        for tile in range(8):
            for block in range(BLOCKS):
                rows_ref[pl.ds(v * 256 + tile * 32 + block, 8, stride=BLOCKS), :] = state_ref[
                    v, tile * 8 : tile * 8 + 8, tile_lanes(block)
                ]


def face_rows(state_ref, flat_ref, v, face, block):
    side = 3 * (face % 2)
    lanes = tile_lanes(block)
    if face < 2:
        return state_ref[v, side * 16 : side * 16 + 16, lanes]
    if face < 4:
        return jnp.concatenate(
            [state_ref[v, i * 16 + side * 4 : i * 16 + side * 4 + 4, lanes] for i in range(4)], axis=0
        )
    return flat_ref[pl.ds(aligned(block * 320, 64) + v * 64 + side, 16, stride=4), :]


def aligned(row, step=8):
    return row if isinstance(row, int) else pl.multiple_of(row, step)


def lane_index(shape):
    return lax.broadcasted_iota(jnp.int32, shape, 1)


def compact(rows):
    lane = lane_index((8, LANES))
    low = lane < 80
    mid = lane < 112

    def turn(value, shift):
        return pltpu.roll(value, shift, 1)

    first = [jnp.where(low, rows[k], turn(rows[5 + k], 80)) for k in range(3)]
    fourth = jnp.where(low, rows[3], jnp.where(mid, turn(rows[5], 32), turn(rows[7], 64)))
    fifth = jnp.where(low, rows[4], jnp.where(mid, turn(rows[6], 32), turn(rows[7], 48)))
    return first + [fourth, fifth]


def expand(parts):
    lane = lane_index((8, LANES))
    head = lane < 48
    body = lane < 64

    def turn(value, shift):
        return pltpu.roll(value, shift, 1)

    sixth = jnp.where(head, turn(parts[0], 48), turn(parts[3], 96))
    seventh = jnp.where(head, turn(parts[1], 48), turn(parts[4], 96))
    eighth = jnp.where(
        head, turn(parts[2], 48), jnp.where(body, turn(parts[3], 64), turn(parts[4], 80))
    )
    return list(parts) + [sixth, seventh, eighth]


def compact_into(board_ref, base, to_ref, at):
    rows = [board_ref[pl.ds(base + 8 * k, 8), :] for k in range(8 * BATCH)]
    parts = []
    for block in range(BATCH):
        parts += compact(rows[8 * block : 8 * block + 8])
    for k in range(5 * BATCH):
        to_ref[pl.ds(at + 8 * k, 8), :] = parts[k]


def expand_into(from_ref, start, board_ref, base):
    parts = [from_ref[pl.ds(start + 8 * k, 8), :] for k in range(5 * BATCH)]
    rows = []
    for block in range(BATCH):
        rows += expand(parts[5 * block : 5 * block + 5])
    for k in range(8 * BATCH):
        board_ref[pl.ds(base + 8 * k, 8), :] = rows[k]


def spread_flat(state_ref, flat_ref):
    for block in range(BLOCKS):
        for v in range(5):
            at = block * 320 + v * 64
            flat_ref[at : at + 64, :] = state_ref[v, :, tile_lanes(block)]


def face_trace(state_ref, flat_ref, face, block):
    return jnp.concatenate([face_rows(state_ref, flat_ref, v, face, block) for v in range(5)], axis=0)


def build_tables(state_ref, flat_ref, table_ref):
    spread_flat(state_ref, flat_ref)
    padding = jnp.zeros((LANES - TRACE, LANES), jnp.float32)
    for face in range(6):
        for block in range(BLOCKS):
            trace = face_trace(state_ref, flat_ref, face, block)
            place = face * BLOCKS + block
            square = jnp.concatenate([trace, padding], axis=0)
            table_ref[place * LANES : (place + 1) * LANES, :] = square.T


def pack_kernel(
    place_ref,
    partner_hbm,
    state_hbm,
    plane_hbm,
    up_ref,
    down_ref,
    best_ref,
    plane_ref,
    partner_ref,
    state_ref,
    table_ref,
    board_ref,
    flat_ref,
    sems,
):
    copies = [pltpu.make_async_copy(partner_hbm, partner_ref, sems.at[0])]
    for a in range(4):
        nodes = pl.ds(a * 16, 16)
        copies.append(
            pltpu.make_async_copy(state_hbm.at[:, nodes, :], state_ref.at[:, nodes, :], sems.at[1 + a])
        )
    for copy in copies:
        copy.start()
    for copy in copies[1:]:
        copy.wait()
    spread_flat(state_ref, flat_ref)
    copies[0].wait()
    padding = jnp.zeros((LANES - TRACE, LANES), jnp.float32)

    def build(face, block, slot):
        square = jnp.concatenate([face_trace(state_ref, flat_ref, face, block), padding], axis=0)
        table_ref[slot] = square.T

    def scatter(block):
        for face in range(6):
            build(face, block, face)
            base = face * ELEMENTS + block * LANES
            for start in range(0, LANES, UNROLL):
                targets = [partner_ref[base + start + k] for k in range(UNROLL)]
                rows = [table_ref[face, start + k : start + k + 1, :] for k in range(UNROLL)]
                for k in range(UNROLL):
                    board_ref[pl.ds(targets[k], 1), :] = rows[k]

    for block in range(BLOCKS):
        scatter(block)

    def speeds(step, best):
        density, mom_x, mom_y, mom_z, energy = [
            state_ref[v, pl.ds(pl.multiple_of(step * 8, 8), 8), :] for v in range(5)
        ]
        inverse = 1.0 / density
        square = (mom_x * mom_x + mom_y * mom_y + mom_z * mom_z) * inverse
        pressure = (HEAT_RATIO - 1.0) * (energy - 0.5 * square)
        wave = jnp.sqrt(square * inverse) + jnp.sqrt(HEAT_RATIO * pressure * inverse)
        return jnp.maximum(best, wave)

    best = lax.fori_loop(0, 8, speeds, jnp.zeros((8, ELEMENTS), jnp.float32))
    best = jnp.maximum(
        jnp.maximum(best[:, tile_lanes(0)], best[:, tile_lanes(1)]),
        jnp.maximum(best[:, tile_lanes(2)], best[:, tile_lanes(3)]),
    )
    best_ref[...] = best
    up_ref[CROSS * MESSAGE :, :] = best
    down_ref[CROSS * MESSAGE :, :] = best
    plane, spot = place_ref[0], place_ref[1]

    def send(to_ref, peer, step):
        base = pl.multiple_of(COLUMNS + (peer + step * BATCH) * SLOTS, SLOTS)
        compact_into(board_ref, base, to_ref, aligned(step * BATCH * MESSAGE))

    def send_up(step, carry):
        send(up_ref, (plane + 1) * PLANE, step)
        return carry

    def send_down(step, carry):
        send(down_ref, (plane - 1) * PLANE + NEAR, step)
        return carry

    sent = []
    for step in range(PLANE // BATCH):
        send(plane_ref, plane * PLANE, step)
        part = pl.ds(step * BATCH * MESSAGE, BATCH * MESSAGE)
        sent.append(
            pltpu.make_async_copy(plane_ref.at[part, :], plane_hbm.at[part, :], sems.at[5 + step])
        )
        sent[-1].start()
    upward = (jnp.maximum(spot - NEAR + 1, 0) + BATCH - 1) // BATCH
    lax.fori_loop(0, jnp.where(plane < 3, upward, 0), send_up, 0)
    lax.fori_loop(jnp.where(plane > 0, spot // BATCH, CROSS // BATCH), CROSS // BATCH, send_down, 0)
    for copy in sent:
        copy.wait()


def relay_kernel(place_ref, up_ref, down_ref, best_ref, rate_hbm, relay_ref, three_ref):
    spot = place_ref[1]
    for block in range(PLANE):
        for k in range(5):
            if block < CROSS:
                value = up_ref[block * MESSAGE + 8 * k : block * MESSAGE + 8 * k + 8, :]
            if block >= NEAR:
                at = (block - NEAR) * MESSAGE + 8 * k
                other = down_ref[at : at + 8, :]
                value = other if block >= CROSS else jnp.where(block <= spot - NEAR, value, other)
            relay_ref[block * LONG + 8 * k : block * LONG + 8 * k + 8, :] = value
    three_ref[...] = jnp.maximum(
        best_ref[...], jnp.maximum(up_ref[CROSS * MESSAGE :, :], down_ref[CROSS * MESSAGE :, :])
    )


def top_kernel(three_ref, far_ref, relay_in, relay_hbm, top_ref, sems):
    top = jnp.max(jnp.maximum(three_ref[...], far_ref[...]), axis=0, keepdims=True)
    top_ref[0] = top
    copies = [
        pltpu.make_async_copy(top_ref, relay_hbm.at[pl.ds(block * LONG + MESSAGE, 1)], sems.at[block])
        for block in range(PLANE)
    ]
    for copy in copies:
        copy.start()
    for copy in copies:
        copy.wait()


def early_kernel(
    place_ref,
    partner_ref,
    blank_hbm,
    state_ref,
    plane_ref,
    other_ref,
    owner_ref,
    board_ref,
    flat_ref,
    picked_ref,
    sem,
):
    plane, spot = place_ref[0], place_ref[1]
    blank = pltpu.make_async_copy(blank_hbm, owner_ref, sem)
    blank.start()
    build_tables(state_ref, flat_ref, board_ref)

    def receive(step, carry):
        start = pl.multiple_of(step * BATCH * MESSAGE, 8)
        base = pl.multiple_of(COLUMNS + (plane * PLANE + step * BATCH) * SLOTS, SLOTS)
        expand_into(plane_ref, start, board_ref, base)
        return carry

    lax.fori_loop(jnp.maximum(spot - REACH, 0) // BATCH, PLANE // BATCH, receive, 0)

    def gather(step, carry):
        base = step * UNROLL
        indices = [partner_ref[base + k] for k in range(UNROLL)]
        rows = [board_ref[pl.ds(index, 1), :] for index in indices]
        for k in range(UNROLL):
            picked_ref[pl.ds(base + k, 1), :] = rows[k]
            owner_ref[indices[k]] = base + k
        return carry

    blank.wait()
    lax.fori_loop(0, COLUMNS // UNROLL, gather, 0)
    for place in range(COLUMNS // LANES):
        square = picked_ref[place * LANES : (place + 1) * LANES, :].T
        other_ref[place * TRACE : (place + 1) * TRACE, :] = square[0:TRACE]


def sublane_index():
    return lax.broadcasted_iota(jnp.int32, (8, LANES), 0)


def wide(row):
    return jnp.broadcast_to(row, (8, LANES))


def face_normals(normal_ref, place):
    lanes = pl.ds(pl.multiple_of(place * LANES, LANES), LANES)
    normal = [wide(normal_ref[k : k + 1, lanes]) for k in range(3)]
    length = jnp.sqrt(normal[0] * normal[0] + normal[1] * normal[1] + normal[2] * normal[2])
    return normal, length


def lift(tiles, flux_ref, field_ref, v, block):
    first = sublane_index() < 4

    def piece(face, half):
        start = aligned((face * BLOCKS + block) * TRACE + v * 16)
        return flux_ref[pl.ds(start + half * 8, 8), :]

    tiles = list(tiles)
    for half in range(2):
        tiles[half] = tiles[half] + piece(0, half)
        tiles[6 + half] = tiles[6 + half] + piece(1, half)
        low, high = piece(2, half), piece(3, half)
        tiles[4 * half] = tiles[4 * half] + jnp.where(first, low, 0.0)
        tiles[4 * half + 2] = tiles[4 * half + 2] + jnp.where(first, pltpu.roll(low, 4, 0), 0.0)
        tiles[4 * half + 1] = tiles[4 * half + 1] + jnp.where(first, 0.0, pltpu.roll(high, 4, 0))
        tiles[4 * half + 3] = tiles[4 * half + 3] + jnp.where(first, 0.0, high)
    base = aligned(v * 64 + block * 320)
    for tile in range(8):
        field_ref[pl.ds(base + tile * 8, 8), :] = tiles[tile]
    for half in range(2):
        for face in (4, 5):
            nodes = pl.ds(base + half * 32 + 3 * (face - 4), 8, stride=4)
            field_ref[nodes, :] = field_ref[nodes, :] + piece(face, half)


def turn_indices(code):
    flip_first = jnp.where(code % 2 == 1, 3, 0)
    flip_second = jnp.where((code // 2) % 2 == 1, 3, 0)
    swapped = code >= 4
    sublane = sublane_index()
    result = []
    for half in range(2):
        i, j = 2 * half + sublane // 4, sublane % 4
        first = jnp.where(swapped, j, i) ^ flip_first
        second = jnp.where(swapped, i, j) ^ flip_second
        result.append(first * 4 + second)
    return result


def volume_kernel(
    place_ref,
    state_ref,
    register_ref,
    metric_ref,
    normal_ref,
    code_ref,
    partner_ref,
    field_ref,
    side_ref,
    turn_ref,
    own_ref,
    rows_ref,
    tensor_ref,
    flux_ref,
    flat_ref,
    rate_ref,
    term_ref,
):
    low = COLUMNS + place_ref[0] * (PLANE * SLOTS)
    spread_nodes(state_ref, rows_ref)
    spread_flat(state_ref, flat_ref)
    for face in range(6):
        for block in range(BLOCKS):
            place = face * BLOCKS + block
            own_ref[place * TRACE : (place + 1) * TRACE, :] = face_trace(state_ref, flat_ref, face, block)

    def own_fluxes(face, carry):
        for block in range(BLOCKS):
            place = face * BLOCKS + block
            normal, length = face_normals(normal_ref, place)
            start = pl.multiple_of(place * TRACE, TRACE)
            side = pl.multiple_of(place * SIDE, 8)
            rows = [value[0:1] for value in normal + [length]]
            side_ref[pl.ds(side + 16, 8), :] = jnp.concatenate(rows + rows, axis=0)
            partner = wide(partner_ref[pl.ds(place, 1), :])
            late = (partner >= COLUMNS) & ((partner < low) | (partner >= low + PLANE * SLOTS))
            late = jnp.where(late, 16, 0)
            for half, turn in enumerate(turn_indices(wide(code_ref[pl.ds(place, 1), :]))):
                turn_ref[pl.ds(pl.multiple_of(place * 16, 16) + half * 8, 8), :] = turn + late
            for half in range(2):
                at = start + half * 8
                own = [own_ref[pl.ds(at + v * 16, 8), :] for v in range(5)]
                terms, wave = normal_flux(own, normal, length)
                for v in range(5):
                    term_ref[pl.ds(at + v * 16, 8), :] = (0.5 * LIFT_FACTOR) * terms[v]
                side_ref[pl.ds(side + half * 8, 8), :] = wave
        return carry

    lax.fori_loop(0, 6, own_fluxes, 0)
    for direction in range(3):
        for half in range(2):
            for block in range(BLOCKS):
                tensor_ref[pl.ds(direction * 24 + half * 4 + block, 3, stride=8), :] = metric_ref[
                    direction, :, block * LANES : (block + 1) * LANES
                ]

    def fluxes(step, carry):
        at = pl.multiple_of(step * 8, 8)
        density, mom_x, mom_y, mom_z, energy = [
            rows_ref[pl.ds(v * 256 + at, 8), :] for v in range(5)
        ]
        inverse = 1.0 / density
        momentum = [mom_x, mom_y, mom_z]
        velocity = [m * inverse for m in momentum]
        pressure = (HEAT_RATIO - 1.0) * (
            energy
            - 0.5 * (mom_x * velocity[0] + mom_y * velocity[1] + mom_z * velocity[2])
        )
        enthalpy = energy + pressure
        for direction in range(3):
            tensor = [tensor_ref[direction * 24 + k * 8 : direction * 24 + k * 8 + 8, :] for k in range(3)]
            along = tensor[0] * velocity[0] + tensor[1] * velocity[1] + tensor[2] * velocity[2]
            values = [density * along]
            values += [momentum[k] * along + pressure * tensor[k] for k in range(3)]
            values += [enthalpy * along]
            for v in range(5):
                flux_ref[direction, pl.ds(v * 256 + at, 8), :] = values[v]
        return carry

    lax.fori_loop(0, 32, fluxes, 0)
    matrix = derivative_matrix()
    upper = lax.broadcasted_iota(jnp.int32, (8, LANES), 0) < 4

    def pair(first, second):
        return jnp.where(upper, jnp.float32(first), jnp.float32(second))

    straight = [[pair(matrix[2 * t, 2 * s], matrix[2 * t + 1, 2 * s + 1]) for s in range(2)] for t in range(2)]
    crossed = [[pair(matrix[2 * t, 2 * s + 1], matrix[2 * t + 1, 2 * s]) for s in range(2)] for t in range(2)]

    def combine(values, target):
        total = values[0] * float(matrix[target, 0])
        for source in range(1, 4):
            total = total + values[source] * float(matrix[target, source])
        return total

    def diverge(v, carry):
        base = pl.multiple_of(v * 256, 256)
        for rest in range(8):
            values = [flux_ref[0, pl.ds(base + a * 64 + rest * 8, 8), :] for a in range(4)]
            for a in range(4):
                rate_ref[pl.ds(base + a * 64 + rest * 8, 8), :] = -combine(values, a)
        for a in range(4):
            for half in range(2):
                values = [flux_ref[1, pl.ds(base + a * 64 + b * 16 + half * 8, 8), :] for b in range(4)]
                third = [flux_ref[2, pl.ds(base + a * 64 + b * 16 + half * 8, 8), :] for b in range(4)]
                other = [flux_ref[2, pl.ds(base + a * 64 + b * 16 + (1 - half) * 8, 8), :] for b in range(4)]
                for b in range(4):
                    at = pl.ds(base + a * 64 + b * 16 + half * 8, 8)
                    same, far = third[b], other[b]
                    total = combine(values, b)
                    total = total + straight[half][half] * same
                    total = total + crossed[half][half] * pltpu.roll(same, 4, 0)
                    total = total + straight[half][1 - half] * far
                    total = total + crossed[half][1 - half] * pltpu.roll(far, 4, 0)
                    rate_ref[at, :] = rate_ref[at, :] - total
        return carry

    lax.fori_loop(0, 5, diverge, 0)

    def gather_terms(v, carry):
        base = pl.multiple_of(v * 256, 256)
        for block in range(BLOCKS):
            tiles = []
            for tile in range(8):
                old = register_ref[v, tile * 8 : tile * 8 + 8, tile_lanes(block)]
                rate = rate_ref[pl.ds(base + tile * 32 + block, 8, stride=BLOCKS), :]
                tiles.append(rate + SECTION_KEEP * old)
            lift(tiles, term_ref, field_ref, v, block)
        return carry

    lax.fori_loop(0, 5, gather_terms, 0)


def normal_flux(values, normal, length):
    density, momentum, energy = values[0], values[1:4], values[4]
    inverse = 1.0 / density
    velocity = [m * inverse for m in momentum]
    pressure = (HEAT_RATIO - 1.0) * (
        energy
        - 0.5 * (momentum[0] * velocity[0] + momentum[1] * velocity[1] + momentum[2] * velocity[2])
    )
    speed = velocity[0] * normal[0] + velocity[1] * normal[1] + velocity[2] * normal[2]
    terms = [density * speed]
    terms += [momentum[k] * speed + pressure * normal[k] for k in range(3)]
    terms += [(energy + pressure) * speed]
    wave = jnp.abs(speed) + jnp.sqrt(HEAT_RATIO * pressure * inverse) * length
    return terms, wave


def finish_kernel(
    place_ref,
    owner_hbm,
    rate_hbm,
    other_ref,
    side_ref,
    turn_ref,
    state_ref,
    relay_ref,
    section_hbm,
    advanced_hbm,
    low_ref,
    high_ref,
    section_ref,
    advanced_ref,
    board_ref,
    picked_ref,
    rate_ref,
    flat_ref,
    term_ref,
    field_ref,
    sems,
):
    plane, spot = place_ref[0], place_ref[1]
    window = CROSS * SLOTS
    low_slot = jnp.maximum(COLUMNS + ((plane - 1) * PLANE + NEAR) * SLOTS, 0)
    high_slot = jnp.minimum(COLUMNS + (plane + 1) * PLANE * SLOTS, COLUMNS + DEVICES * SLOTS - window)
    sources = [
        (owner_hbm.at[pl.ds(pl.multiple_of(low_slot, 512), window)], low_ref),
        (owner_hbm.at[pl.ds(pl.multiple_of(high_slot, 512), window)], high_ref),
        (rate_hbm, rate_ref),
    ]
    copies = [
        pltpu.make_async_copy(source, target, sems.at[k])
        for k, (source, target) in enumerate(sources)
    ]
    for copy in copies:
        copy.start()
    spread_flat(state_ref, flat_ref)

    def receive(blocks):
        parts = [relay_ref[b * LONG + 8 * k : b * LONG + 8 * k + 8, :] for b in blocks for k in range(5)]
        rows = []
        for k in range(BATCH):
            rows += expand(parts[5 * k : 5 * k + 5])
        for k, block in enumerate(blocks):
            side = jnp.where(block >= spot + NEAR, plane - 1, plane + 1)
            base = pl.multiple_of((side * PLANE + block + MARGIN) * SLOTS, SLOTS)
            for j in range(8):
                board_ref[pl.ds(base + 8 * j, 8), :] = rows[8 * k + j]

    for first in range(0, PLANE, BATCH):
        last = first + BATCH - 1

        @pl.when((first <= spot - NEAR) | (last >= spot + NEAR))
        def _(first=first):
            receive(range(first, first + BATCH))

    def place_rows(columns_ref, base, step):
        at = step * UNROLL
        columns = [columns_ref[at + k] for k in range(UNROLL)]
        rows = [board_ref[pl.ds(base * SLOTS + at + k, 1), :] for k in range(UNROLL)]
        for k in range(UNROLL):
            picked_ref[pl.ds(columns[k], 1), :] = rows[k]

    def place_low(step, carry):
        place_rows(low_ref, (plane - 1) * PLANE + NEAR + MARGIN, step)
        return carry

    def place_high(step, carry):
        place_rows(high_ref, (plane + 1) * PLANE + MARGIN, step)
        return carry

    chunk = SLOTS // UNROLL
    for copy in copies[:2]:
        copy.wait()

    @pl.when(plane > 0)
    def _():
        lax.fori_loop(spot * chunk, CROSS * chunk, place_low, 0)

    @pl.when(plane < 3)
    def _():
        lax.fori_loop(0, jnp.maximum(spot - NEAR + 1, 0) * chunk, place_high, 0)

    tops = [relay_ref[b * LONG + MESSAGE : (b + 1) * LONG, :] for b in range(PLANE)]
    top = jnp.max(functools.reduce(jnp.maximum, tops))
    scale = CFL_NUMBER / top * SECTION_STEP

    def results(block):
        lanes = tile_lanes(block)
        pairs = ((section_ref, section_hbm), (advanced_ref, advanced_hbm))
        return [
            pltpu.make_async_copy(source.at[:, :, lanes], target.at[:, :, lanes], sems.at[3 + 2 * block + k])
            for k, (source, target) in enumerate(pairs)
        ]

    def element_block(block):
        for face in range(6):
            place = face * BLOCKS + block
            square = picked_ref[pl.ds(pl.multiple_of(place * LANES, LANES), LANES), :].T
            start = pl.multiple_of(place * TRACE, TRACE)
            side = pl.multiple_of(place * SIDE, 8)
            at = pl.multiple_of(place * 16, 16)
            turns = [turn_ref[pl.ds(at + half * 8, 8), :] for half in range(2)]
            late = turns[0] >= 16
            known = [
                jnp.where(late, square[8 * k : 8 * k + 8], other_ref[pl.ds(start + 8 * k, 8), :])
                for k in range(10)
            ]
            own = [face_rows(state_ref, flat_ref, v, face, block) for v in range(5)]
            rows = side_ref[pl.ds(side + 16, 8), :]
            normal = [wide(rows[k : k + 1]) for k in range(3)]
            length = wide(rows[3:4])
            for half in range(2):
                upper = turns[half] % 16 >= 8
                sublane = turns[half] % 8
                far = []
                for v in range(5):
                    parts = [
                        jnp.take_along_axis(known[2 * v + k], sublane, axis=0, mode="promise_in_bounds")
                        for k in range(2)
                    ]
                    far.append(jnp.where(upper, parts[1], parts[0]))
                far_terms, far_wave = normal_flux(far, normal, length)
                bound = jnp.maximum(side_ref[pl.ds(side + half * 8, 8), :], far_wave)
                viscous = bound + length
                for v in range(5):
                    rows = pl.ds(start + v * 16 + half * 8, 8)
                    weight = bound if v == 0 else viscous
                    term_ref[rows, :] = (0.5 * LIFT_FACTOR) * (
                        weight * (far[v] - own[v][8 * half : 8 * half + 8]) - far_terms[v]
                    )
        if block == 0:
            copies[2].wait()
        lanes = tile_lanes(block)
        for v in range(5):
            base = block * 320 + v * 64
            tiles = [rate_ref[pl.ds(base + tile * 8, 8), :] for tile in range(8)]
            lift(tiles, term_ref, field_ref, v, block)
            for tile in range(8):
                nodes = slice(tile * 8, tile * 8 + 8)
                section = field_ref[pl.ds(base + tile * 8, 8), :]
                section_ref[v, nodes, lanes] = section
                advanced_ref[v, nodes, lanes] = state_ref[v, nodes, lanes] + scale * section
        for copy in results(block):
            copy.start()

    for block in range(BLOCKS):
        element_block(block)
    for block in range(BLOCKS):
        for copy in results(block):
            copy.wait()


def smem():
    return pl.BlockSpec(memory_space=pltpu.SMEM)


def vmem():
    return pl.BlockSpec(memory_space=pltpu.VMEM)


def params():
    return pltpu.CompilerParams(vmem_limit_bytes=VMEM_LIMIT)


def shape(*sizes):
    return jax.ShapeDtypeStruct(sizes, jnp.float32)


def scratch(*sizes):
    return pltpu.VMEM(sizes, jnp.float32)


def hbm():
    return pl.BlockSpec(memory_space=pltpu.HBM)


def anywhere():
    return pl.BlockSpec(memory_space=pl.ANY)


def in_hbm_shape(*sizes):
    return pltpu.HBM(sizes, jnp.float32)


def pack(place, partner, state):
    return pl.pallas_call(
        pack_kernel,
        out_shape=(
            in_hbm_shape(PLANE * MESSAGE, LANES),
            shape(CROSS * MESSAGE + 8, LANES),
            shape(CROSS * MESSAGE + 8, LANES),
            shape(8, LANES),
        ),
        in_specs=[smem(), hbm(), hbm()],
        out_specs=(hbm(), vmem(), vmem(), vmem()),
        scratch_shapes=[
            scratch(PLANE * MESSAGE, LANES),
            pltpu.SMEM((COLUMNS,), jnp.int32),
            scratch(5, 64, ELEMENTS),
            scratch(6, LANES, LANES),
            scratch(COLUMNS + (DEVICES + CROSS) * SLOTS, LANES),
            scratch(1280, LANES),
            pltpu.SemaphoreType.DMA((5 + PLANE // BATCH,)),
        ],
        compiler_params=params(),
        name="pack",
    )(place, partner, state)


def volume(place, state, register, metric, normal, code, partner):
    return pl.pallas_call(
        volume_kernel,
        out_shape=(
            in_hbm_shape(1280, LANES),
            shape(24 * SIDE, LANES),
            jax.ShapeDtypeStruct((24 * 16, LANES), jnp.int32),
        ),
        in_specs=[smem()] + [vmem()] * 6,
        out_specs=(vmem(),) * 3,
        scratch_shapes=[
            scratch(24 * TRACE, LANES),
            scratch(1280, LANES),
            scratch(72, LANES),
            scratch(3, 1280, LANES),
            scratch(1280, LANES),
            scratch(1280, LANES),
            scratch(24 * TRACE, LANES),
        ],
        compiler_params=params(),
        name="volume",
    )(place, state, register, metric, normal, code, partner)


def relay(place, up, down, best, rate):
    return pl.pallas_call(
        relay_kernel,
        out_shape=(in_hbm_shape(PLANE * LONG, LANES), shape(8, LANES)),
        in_specs=[smem()] + [vmem()] * 3 + [hbm()],
        out_specs=(vmem(), vmem()),
        compiler_params=params(),
        cost_estimate=pl.CostEstimate(flops=10**11, bytes_accessed=10**8, transcendentals=0),
        name="relay",
    )(place, up, down, best, rate)


def spread_top(three, far, relayed):
    return pl.pallas_call(
        top_kernel,
        out_shape=in_hbm_shape(PLANE * LONG, 1, LANES),
        in_specs=[vmem(), vmem(), hbm()],
        out_specs=hbm(),
        scratch_shapes=[scratch(1, 1, LANES), pltpu.SemaphoreType.DMA((PLANE,))],
        input_output_aliases={2: 0},
        compiler_params=params(),
        name="top",
    )(three, far, relayed)


def early(place, partner, blank, state, plane):
    return pl.pallas_call(
        early_kernel,
        out_shape=(
            shape(24 * TRACE, LANES),
            pltpu.HBM((COLUMNS + DEVICES * SLOTS,), jnp.int32),
        ),
        in_specs=[smem(), smem(), anywhere(), vmem(), vmem()],
        out_specs=(vmem(), smem()),
        scratch_shapes=[
            scratch(COLUMNS + DEVICES * SLOTS, LANES),
            scratch(1280, LANES),
            scratch(COLUMNS, LANES),
            pltpu.SemaphoreType.DMA,
        ],
        compiler_params=params(),
        name="early",
    )(place, partner, blank, state, plane)


def finish(place, owner, other, side, turn, rate, state, relayed):
    held = [in_hbm(value) for value in (owner, rate)]
    return pl.pallas_call(
        finish_kernel,
        out_shape=(in_hbm_shape(5, 64, ELEMENTS),) * 2,
        in_specs=[smem(), hbm(), hbm()] + [vmem()] * 5,
        out_specs=(hbm(), hbm()),
        scratch_shapes=[
            pltpu.SMEM((CROSS * SLOTS,), jnp.int32),
            pltpu.SMEM((CROSS * SLOTS,), jnp.int32),
            scratch(5, 64, ELEMENTS),
            scratch(5, 64, ELEMENTS),
            scratch((DEVICES + 2 * MARGIN) * SLOTS, LANES),
            scratch(COLUMNS + 8, LANES),
            scratch(1280, LANES),
            scratch(1280, LANES),
            scratch(24 * TRACE, LANES),
            scratch(1280, LANES),
            pltpu.SemaphoreType.DMA((11,)),
        ],
        compiler_params=params(),
        name="finish",
    )(place, *held, other, side, turn, state, relayed)


def in_hbm(value):
    return pltpu.with_memory_space_constraint(value, pltpu.HBM)


def in_vmem(value):
    return pltpu.with_memory_space_constraint(value, pltpu.VMEM)


def along_y(value, steps):
    return lax.ppermute(value, "y", [(i, (i + steps) % 4) for i in range(4)])


def on_device(state, register, metric, face_normal, partner, flip_code, face_role, send_face):
    plane = lax.axis_index("y").astype(jnp.int32)
    spot = lax.axis_index(("r", "x")).astype(jnp.int32)
    place = jnp.stack([plane, spot])
    state = state.transpose(1, 0, 2)
    rows = (COLUMNS // LANES, LANES)
    in_plane, up, down, best = pack(place, in_hbm(partner), in_hbm(state))
    from_below = along_y(up, 1)
    from_above = along_y(down, -1)
    far = along_y(best, 2)
    got = lax.all_to_all(in_plane, ("r", "x"), 0, 0, tiled=True)
    rate, side, turn = volume(
        place,
        state,
        register.transpose(1, 0, 2),
        metric,
        face_normal,
        flip_code.reshape(rows),
        partner.reshape(rows),
    )
    relayed, three = relay(place, from_below, from_above, best, in_hbm(rate))
    relayed = spread_top(three, far, in_hbm(relayed.reshape(PLANE * LONG, 1, LANES))).reshape(PLANE, LONG, 1, LANES)
    relayed = lax.all_to_all(relayed, ("r", "x"), 0, 0, tiled=True).reshape(PLANE * LONG, LANES)
    blank = jnp.full((COLUMNS + DEVICES * SLOTS,), COLUMNS, jnp.int32)
    other, owner = early(place, partner, blank, state, got)
    section, advanced = finish(place, owner, other, side, turn, rate, state, relayed)
    return section.transpose(1, 0, 2), advanced.transpose(1, 0, 2)


def solution(mesh):
    placed = (
        P(None, None, AXES),
        P(None, None, AXES),
        P(None, None, AXES),
        P(None, AXES),
        P(AXES),
        P(AXES),
        P(AXES),
        P(AXES, None, None),
    )
    return jax.shard_map(
        on_device,
        mesh=Mesh(mesh.devices.reshape(4, 8, 4), AXES),
        in_specs=placed,
        out_specs=(P(None, None, AXES), P(None, None, AXES)),
        check_vma=False,
    )
```

```python
import functools

import jax
import jax.numpy as jnp
import numpy as np
from jax import lax
from jax.experimental import pallas as pl
from jax.experimental.pallas import tpu as pltpu
from jax.sharding import Mesh
from jax.sharding import PartitionSpec as P

HEAT_RATIO = 1.4
LIFT_FACTOR = 6.0
CFL_NUMBER = 0.3
SECTION_KEEP = -0.4178904745
SECTION_STEP = 0.4432226
DEVICES = 128
ELEMENTS = 512
COLUMNS = 6 * ELEMENTS
SLOTS = 64
REACH = 24
LANES = 128
BLOCKS = ELEMENTS // LANES
TRACE = 80
GROUP = COLUMNS // 3
MESSAGE = TRACE * SLOTS // LANES
LONG = MESSAGE + 1
UNROLL = 32
SIDE = 24
BATCH = 4
AXES = ("y", "r", "x")
PLANE = 32
NEAR = PLANE - REACH
CROSS = REACH
MARGIN = PLANE
VMEM_LIMIT = 24 * 1024 * 1024


def derivative_matrix():
    points = np.array([-1.0, -1.0 / np.sqrt(5.0), 1.0 / np.sqrt(5.0), 1.0])
    weights = np.array(
        [
            1.0
            / np.prod([points[target] - points[source] for source in range(4) if source != target])
            for target in range(4)
        ]
    )
    matrix = np.zeros((4, 4))
    for target in range(4):
        for source in range(4):
            if target != source:
                matrix[target, source] = (
                    weights[source] / weights[target] / (points[target] - points[source])
                )
        matrix[target, target] = -np.sum(matrix[target])
    return matrix


def face_nodes(face):
    side = 3 * (face % 2)
    if face < 2:
        return [side * 16 + i * 4 + j for i in range(4) for j in range(4)]
    if face < 4:
        return [i * 16 + side * 4 + j for i in range(4) for j in range(4)]
    return [i * 16 + j * 4 + side for i in range(4) for j in range(4)]


def tile_lanes(block):
    return pl.ds(aligned(block * LANES, LANES), LANES)


def spread_nodes(state_ref, rows_ref):
    for v in range(5):
        for tile in range(8):
            for block in range(BLOCKS):
                rows_ref[pl.ds(v * 256 + tile * 32 + block, 8, stride=BLOCKS), :] = state_ref[
                    v, tile * 8 : tile * 8 + 8, tile_lanes(block)
                ]


def face_rows(state_ref, flat_ref, v, face, block):
    side = 3 * (face % 2)
    lanes = tile_lanes(block)
    if face < 2:
        return state_ref[v, side * 16 : side * 16 + 16, lanes]
    if face < 4:
        return jnp.concatenate(
            [state_ref[v, i * 16 + side * 4 : i * 16 + side * 4 + 4, lanes] for i in range(4)], axis=0
        )
    return flat_ref[pl.ds(aligned(block * 320, 64) + v * 64 + side, 16, stride=4), :]


def aligned(row, step=8):
    return row if isinstance(row, int) else pl.multiple_of(row, step)


def lane_index(shape):
    return lax.broadcasted_iota(jnp.int32, shape, 1)


def compact(rows):
    lane = lane_index((8, LANES))
    low = lane < 80
    mid = lane < 112

    def turn(value, shift):
        return pltpu.roll(value, shift, 1)

    first = [jnp.where(low, rows[k], turn(rows[5 + k], 80)) for k in range(3)]
    fourth = jnp.where(low, rows[3], jnp.where(mid, turn(rows[5], 32), turn(rows[7], 64)))
    fifth = jnp.where(low, rows[4], jnp.where(mid, turn(rows[6], 32), turn(rows[7], 48)))
    return first + [fourth, fifth]


def expand(parts):
    lane = lane_index((8, LANES))
    head = lane < 48
    body = lane < 64

    def turn(value, shift):
        return pltpu.roll(value, shift, 1)

    sixth = jnp.where(head, turn(parts[0], 48), turn(parts[3], 96))
    seventh = jnp.where(head, turn(parts[1], 48), turn(parts[4], 96))
    eighth = jnp.where(
        head, turn(parts[2], 48), jnp.where(body, turn(parts[3], 64), turn(parts[4], 80))
    )
    return list(parts) + [sixth, seventh, eighth]


def compact_into(board_ref, base, to_ref, at):
    rows = [board_ref[pl.ds(base + 8 * k, 8), :] for k in range(8 * BATCH)]
    parts = []
    for block in range(BATCH):
        parts += compact(rows[8 * block : 8 * block + 8])
    for k in range(5 * BATCH):
        to_ref[pl.ds(at + 8 * k, 8), :] = parts[k]


def expand_into(from_ref, start, board_ref, base):
    parts = [from_ref[pl.ds(start + 8 * k, 8), :] for k in range(5 * BATCH)]
    rows = []
    for block in range(BATCH):
        rows += expand(parts[5 * block : 5 * block + 5])
    for k in range(8 * BATCH):
        board_ref[pl.ds(base + 8 * k, 8), :] = rows[k]


def spread_flat(state_ref, flat_ref):
    for block in range(BLOCKS):
        for v in range(5):
            at = block * 320 + v * 64
            flat_ref[at : at + 64, :] = state_ref[v, :, tile_lanes(block)]


def face_trace(state_ref, flat_ref, face, block):
    return jnp.concatenate([face_rows(state_ref, flat_ref, v, face, block) for v in range(5)], axis=0)


def build_tables(state_ref, flat_ref, table_ref):
    spread_flat(state_ref, flat_ref)
    padding = jnp.zeros((LANES - TRACE, LANES), jnp.float32)
    for face in range(6):
        for block in range(BLOCKS):
            trace = face_trace(state_ref, flat_ref, face, block)
            place = face * BLOCKS + block
            square = jnp.concatenate([trace, padding], axis=0)
            table_ref[place * LANES : (place + 1) * LANES, :] = square.T


def pack_kernel(
    place_ref,
    partner_hbm,
    state_hbm,
    plane_hbm,
    up_ref,
    down_ref,
    best_ref,
    plane_ref,
    partner_ref,
    state_ref,
    table_ref,
    board_ref,
    flat_ref,
    sems,
):
    copies = [pltpu.make_async_copy(partner_hbm, partner_ref, sems.at[0])]
    for a in range(4):
        nodes = pl.ds(a * 16, 16)
        copies.append(
            pltpu.make_async_copy(state_hbm.at[:, nodes, :], state_ref.at[:, nodes, :], sems.at[1 + a])
        )
    for copy in copies:
        copy.start()
    for copy in copies[1:]:
        copy.wait()
    spread_flat(state_ref, flat_ref)
    copies[0].wait()
    padding = jnp.zeros((LANES - TRACE, LANES), jnp.float32)

    def build(face, block, slot):
        square = jnp.concatenate([face_trace(state_ref, flat_ref, face, block), padding], axis=0)
        table_ref[slot] = square.T

    def scatter(block):
        for face in range(6):
            build(face, block, face)
            base = face * ELEMENTS + block * LANES
            for start in range(0, LANES, UNROLL):
                targets = [partner_ref[base + start + k] for k in range(UNROLL)]
                rows = [table_ref[face, start + k : start + k + 1, :] for k in range(UNROLL)]
                for k in range(UNROLL):
                    board_ref[pl.ds(targets[k], 1), :] = rows[k]

    for block in range(BLOCKS):
        scatter(block)

    def speeds(step, best):
        density, mom_x, mom_y, mom_z, energy = [
            state_ref[v, pl.ds(pl.multiple_of(step * 8, 8), 8), :] for v in range(5)
        ]
        inverse = 1.0 / density
        speed_x, speed_y, speed_z = mom_x * inverse, mom_y * inverse, mom_z * inverse
        square = speed_x * speed_x + speed_y * speed_y + speed_z * speed_z
        kinetic = mom_x * speed_x + mom_y * speed_y + mom_z * speed_z
        pressure = (HEAT_RATIO - 1.0) * (energy - 0.5 * kinetic)
        wave = jnp.sqrt(square) + jnp.sqrt(HEAT_RATIO * pressure * inverse)
        return jnp.maximum(best, wave)

    best = lax.fori_loop(0, 8, speeds, jnp.zeros((8, ELEMENTS), jnp.float32))
    best = jnp.maximum(
        jnp.maximum(best[:, tile_lanes(0)], best[:, tile_lanes(1)]),
        jnp.maximum(best[:, tile_lanes(2)], best[:, tile_lanes(3)]),
    )
    best_ref[...] = best
    up_ref[CROSS * MESSAGE :, :] = best
    down_ref[CROSS * MESSAGE :, :] = best
    plane, spot = place_ref[0], place_ref[1]

    def send(to_ref, peer, step):
        base = pl.multiple_of(COLUMNS + (peer + step * BATCH) * SLOTS, SLOTS)
        compact_into(board_ref, base, to_ref, aligned(step * BATCH * MESSAGE))

    def send_up(step, carry):
        send(up_ref, (plane + 1) * PLANE, step)
        return carry

    def send_down(step, carry):
        send(down_ref, (plane - 1) * PLANE + NEAR, step)
        return carry

    sent = []
    for step in range(PLANE // BATCH):
        send(plane_ref, plane * PLANE, step)
        part = pl.ds(step * BATCH * MESSAGE, BATCH * MESSAGE)
        sent.append(
            pltpu.make_async_copy(plane_ref.at[part, :], plane_hbm.at[part, :], sems.at[5 + step])
        )
        sent[-1].start()
    upward = (jnp.maximum(spot - NEAR + 1, 0) + BATCH - 1) // BATCH
    lax.fori_loop(0, jnp.where(plane < 3, upward, 0), send_up, 0)
    lax.fori_loop(jnp.where(plane > 0, spot // BATCH, CROSS // BATCH), CROSS // BATCH, send_down, 0)
    for copy in sent:
        copy.wait()


def relay_kernel(place_ref, up_ref, down_ref, best_ref, rate_hbm, relay_ref, three_ref):
    spot = place_ref[1]
    for block in range(PLANE):
        for k in range(5):
            if block < CROSS:
                value = up_ref[block * MESSAGE + 8 * k : block * MESSAGE + 8 * k + 8, :]
            if block >= NEAR:
                at = (block - NEAR) * MESSAGE + 8 * k
                other = down_ref[at : at + 8, :]
                value = other if block >= CROSS else jnp.where(block <= spot - NEAR, value, other)
            relay_ref[block * LONG + 8 * k : block * LONG + 8 * k + 8, :] = value
    three_ref[...] = jnp.maximum(
        best_ref[...], jnp.maximum(up_ref[CROSS * MESSAGE :, :], down_ref[CROSS * MESSAGE :, :])
    )


def top_kernel(three_ref, far_ref, relay_in, relay_hbm, top_ref, sems):
    top = jnp.max(jnp.maximum(three_ref[...], far_ref[...]), axis=0, keepdims=True)
    top_ref[0] = top
    copies = [
        pltpu.make_async_copy(top_ref, relay_hbm.at[pl.ds(block * LONG + MESSAGE, 1)], sems.at[block])
        for block in range(PLANE)
    ]
    for copy in copies:
        copy.start()
    for copy in copies:
        copy.wait()


def early_kernel(
    place_ref,
    partner_ref,
    blank_hbm,
    state_ref,
    plane_ref,
    other_ref,
    owner_ref,
    board_ref,
    flat_ref,
    picked_ref,
    sem,
):
    plane, spot = place_ref[0], place_ref[1]
    blank = pltpu.make_async_copy(blank_hbm, owner_ref, sem)
    blank.start()
    build_tables(state_ref, flat_ref, board_ref)

    def receive(step, carry):
        start = pl.multiple_of(step * BATCH * MESSAGE, 8)
        base = pl.multiple_of(COLUMNS + (plane * PLANE + step * BATCH) * SLOTS, SLOTS)
        expand_into(plane_ref, start, board_ref, base)
        return carry

    lax.fori_loop(jnp.maximum(spot - REACH, 0) // BATCH, PLANE // BATCH, receive, 0)

    def gather(step, carry):
        base = step * UNROLL
        indices = [partner_ref[base + k] for k in range(UNROLL)]
        rows = [board_ref[pl.ds(index, 1), :] for index in indices]
        for k in range(UNROLL):
            picked_ref[pl.ds(base + k, 1), :] = rows[k]
            owner_ref[indices[k]] = base + k
        return carry

    blank.wait()
    lax.fori_loop(0, COLUMNS // UNROLL, gather, 0)
    for place in range(COLUMNS // LANES):
        square = picked_ref[place * LANES : (place + 1) * LANES, :].T
        other_ref[place * TRACE : (place + 1) * TRACE, :] = square[0:TRACE]


def sublane_index():
    return lax.broadcasted_iota(jnp.int32, (8, LANES), 0)


def wide(row):
    return jnp.broadcast_to(row, (8, LANES))


def face_normals(normal_ref, place):
    lanes = pl.ds(pl.multiple_of(place * LANES, LANES), LANES)
    normal = [wide(normal_ref[k : k + 1, lanes]) for k in range(3)]
    length = jnp.sqrt(normal[0] * normal[0] + normal[1] * normal[1] + normal[2] * normal[2])
    return normal, length


def lift(tiles, flux_ref, field_ref, v, block):
    first = sublane_index() < 4

    def piece(face, half):
        start = aligned((face * BLOCKS + block) * TRACE + v * 16)
        return flux_ref[pl.ds(start + half * 8, 8), :]

    tiles = list(tiles)
    for half in range(2):
        tiles[half] = tiles[half] + piece(0, half)
        tiles[6 + half] = tiles[6 + half] + piece(1, half)
        low, high = piece(2, half), piece(3, half)
        tiles[4 * half] = tiles[4 * half] + jnp.where(first, low, 0.0)
        tiles[4 * half + 2] = tiles[4 * half + 2] + jnp.where(first, pltpu.roll(low, 4, 0), 0.0)
        tiles[4 * half + 1] = tiles[4 * half + 1] + jnp.where(first, 0.0, pltpu.roll(high, 4, 0))
        tiles[4 * half + 3] = tiles[4 * half + 3] + jnp.where(first, 0.0, high)
    base = aligned(v * 64 + block * 320)
    for tile in range(8):
        field_ref[pl.ds(base + tile * 8, 8), :] = tiles[tile]
    for half in range(2):
        for face in (4, 5):
            nodes = pl.ds(base + half * 32 + 3 * (face - 4), 8, stride=4)
            field_ref[nodes, :] = field_ref[nodes, :] + piece(face, half)


def turn_indices(code):
    flip_first = jnp.where(code % 2 == 1, 3, 0)
    flip_second = jnp.where((code // 2) % 2 == 1, 3, 0)
    swapped = code >= 4
    sublane = sublane_index()
    result = []
    for half in range(2):
        i, j = 2 * half + sublane // 4, sublane % 4
        first = jnp.where(swapped, j, i) ^ flip_first
        second = jnp.where(swapped, i, j) ^ flip_second
        result.append(first * 4 + second)
    return result


def volume_kernel(
    place_ref,
    state_ref,
    register_ref,
    metric_ref,
    normal_ref,
    code_ref,
    partner_ref,
    field_ref,
    side_ref,
    turn_ref,
    own_ref,
    rows_ref,
    tensor_ref,
    flux_ref,
    flat_ref,
    rate_ref,
    term_ref,
):
    low = COLUMNS + place_ref[0] * (PLANE * SLOTS)
    spread_nodes(state_ref, rows_ref)
    spread_flat(state_ref, flat_ref)
    for face in range(6):
        for block in range(BLOCKS):
            place = face * BLOCKS + block
            own_ref[place * TRACE : (place + 1) * TRACE, :] = face_trace(state_ref, flat_ref, face, block)

    def own_fluxes(face, carry):
        for block in range(BLOCKS):
            place = face * BLOCKS + block
            normal, length = face_normals(normal_ref, place)
            start = pl.multiple_of(place * TRACE, TRACE)
            side = pl.multiple_of(place * SIDE, 8)
            rows = [value[0:1] for value in normal + [length]]
            side_ref[pl.ds(side + 16, 8), :] = jnp.concatenate(rows + rows, axis=0)
            partner = wide(partner_ref[pl.ds(place, 1), :])
            late = (partner >= COLUMNS) & ((partner < low) | (partner >= low + PLANE * SLOTS))
            late = jnp.where(late, 16, 0)
            for half, turn in enumerate(turn_indices(wide(code_ref[pl.ds(place, 1), :]))):
                turn_ref[pl.ds(pl.multiple_of(place * 16, 16) + half * 8, 8), :] = turn + late
            for half in range(2):
                at = start + half * 8
                own = [own_ref[pl.ds(at + v * 16, 8), :] for v in range(5)]
                terms, wave = normal_flux(own, normal, length)
                for v in range(5):
                    term_ref[pl.ds(at + v * 16, 8), :] = (0.5 * LIFT_FACTOR) * terms[v]
                side_ref[pl.ds(side + half * 8, 8), :] = wave
        return carry

    lax.fori_loop(0, 6, own_fluxes, 0)
    for direction in range(3):
        for half in range(2):
            for block in range(BLOCKS):
                tensor_ref[pl.ds(direction * 24 + half * 4 + block, 3, stride=8), :] = metric_ref[
                    direction, :, block * LANES : (block + 1) * LANES
                ]

    def fluxes(step, carry):
        at = pl.multiple_of(step * 8, 8)
        density, mom_x, mom_y, mom_z, energy = [
            rows_ref[pl.ds(v * 256 + at, 8), :] for v in range(5)
        ]
        inverse = 1.0 / density
        momentum = [mom_x, mom_y, mom_z]
        velocity = [m * inverse for m in momentum]
        pressure = (HEAT_RATIO - 1.0) * (
            energy
            - 0.5 * (mom_x * velocity[0] + mom_y * velocity[1] + mom_z * velocity[2])
        )
        enthalpy = energy + pressure
        for direction in range(3):
            tensor = [tensor_ref[direction * 24 + k * 8 : direction * 24 + k * 8 + 8, :] for k in range(3)]
            along = tensor[0] * velocity[0] + tensor[1] * velocity[1] + tensor[2] * velocity[2]
            values = [density * along]
            values += [momentum[k] * along + pressure * tensor[k] for k in range(3)]
            values += [enthalpy * along]
            for v in range(5):
                flux_ref[direction, pl.ds(v * 256 + at, 8), :] = values[v]
        return carry

    lax.fori_loop(0, 32, fluxes, 0)
    matrix = derivative_matrix()
    upper = lax.broadcasted_iota(jnp.int32, (8, LANES), 0) < 4

    def pair(first, second):
        return jnp.where(upper, jnp.float32(first), jnp.float32(second))

    straight = [[pair(matrix[2 * t, 2 * s], matrix[2 * t + 1, 2 * s + 1]) for s in range(2)] for t in range(2)]
    crossed = [[pair(matrix[2 * t, 2 * s + 1], matrix[2 * t + 1, 2 * s]) for s in range(2)] for t in range(2)]

    def combine(values, target):
        total = values[0] * float(matrix[target, 0])
        for source in range(1, 4):
            total = total + values[source] * float(matrix[target, source])
        return total

    def diverge(v, carry):
        base = pl.multiple_of(v * 256, 256)
        for rest in range(8):
            values = [flux_ref[0, pl.ds(base + a * 64 + rest * 8, 8), :] for a in range(4)]
            for a in range(4):
                rate_ref[pl.ds(base + a * 64 + rest * 8, 8), :] = -combine(values, a)
        for a in range(4):
            for half in range(2):
                values = [flux_ref[1, pl.ds(base + a * 64 + b * 16 + half * 8, 8), :] for b in range(4)]
                third = [flux_ref[2, pl.ds(base + a * 64 + b * 16 + half * 8, 8), :] for b in range(4)]
                other = [flux_ref[2, pl.ds(base + a * 64 + b * 16 + (1 - half) * 8, 8), :] for b in range(4)]
                for b in range(4):
                    at = pl.ds(base + a * 64 + b * 16 + half * 8, 8)
                    same, far = third[b], other[b]
                    total = combine(values, b)
                    total = total + straight[half][half] * same
                    total = total + crossed[half][half] * pltpu.roll(same, 4, 0)
                    total = total + straight[half][1 - half] * far
                    total = total + crossed[half][1 - half] * pltpu.roll(far, 4, 0)
                    rate_ref[at, :] = rate_ref[at, :] - total
        return carry

    lax.fori_loop(0, 5, diverge, 0)

    def gather_terms(v, carry):
        base = pl.multiple_of(v * 256, 256)
        for block in range(BLOCKS):
            tiles = []
            for tile in range(8):
                old = register_ref[v, tile * 8 : tile * 8 + 8, tile_lanes(block)]
                rate = rate_ref[pl.ds(base + tile * 32 + block, 8, stride=BLOCKS), :]
                tiles.append(rate + SECTION_KEEP * old)
            lift(tiles, term_ref, field_ref, v, block)
        return carry

    lax.fori_loop(0, 5, gather_terms, 0)


def normal_flux(values, normal, length):
    density, momentum, energy = values[0], values[1:4], values[4]
    inverse = 1.0 / density
    velocity = [m * inverse for m in momentum]
    pressure = (HEAT_RATIO - 1.0) * (
        energy
        - 0.5 * (momentum[0] * velocity[0] + momentum[1] * velocity[1] + momentum[2] * velocity[2])
    )
    speed = velocity[0] * normal[0] + velocity[1] * normal[1] + velocity[2] * normal[2]
    terms = [density * speed]
    terms += [momentum[k] * speed + pressure * normal[k] for k in range(3)]
    terms += [(energy + pressure) * speed]
    wave = jnp.abs(speed) + jnp.sqrt(HEAT_RATIO * pressure * inverse) * length
    return terms, wave


def finish_kernel(
    place_ref,
    owner_hbm,
    rate_hbm,
    other_ref,
    side_ref,
    turn_ref,
    state_ref,
    relay_ref,
    section_hbm,
    advanced_hbm,
    low_ref,
    high_ref,
    section_ref,
    advanced_ref,
    board_ref,
    picked_ref,
    rate_ref,
    flat_ref,
    term_ref,
    field_ref,
    sems,
):
    plane, spot = place_ref[0], place_ref[1]
    window = CROSS * SLOTS
    low_slot = jnp.maximum(COLUMNS + ((plane - 1) * PLANE + NEAR) * SLOTS, 0)
    high_slot = jnp.minimum(COLUMNS + (plane + 1) * PLANE * SLOTS, COLUMNS + DEVICES * SLOTS - window)
    sources = [
        (owner_hbm.at[pl.ds(pl.multiple_of(low_slot, 512), window)], low_ref),
        (owner_hbm.at[pl.ds(pl.multiple_of(high_slot, 512), window)], high_ref),
        (rate_hbm, rate_ref),
    ]
    copies = [
        pltpu.make_async_copy(source, target, sems.at[k])
        for k, (source, target) in enumerate(sources)
    ]
    for copy in copies:
        copy.start()
    spread_flat(state_ref, flat_ref)

    def receive(blocks):
        parts = [relay_ref[b * LONG + 8 * k : b * LONG + 8 * k + 8, :] for b in blocks for k in range(5)]
        rows = []
        for k in range(BATCH):
            rows += expand(parts[5 * k : 5 * k + 5])
        for k, block in enumerate(blocks):
            side = jnp.where(block >= spot + NEAR, plane - 1, plane + 1)
            base = pl.multiple_of((side * PLANE + block + MARGIN) * SLOTS, SLOTS)
            for j in range(8):
                board_ref[pl.ds(base + 8 * j, 8), :] = rows[8 * k + j]

    for first in range(0, PLANE, BATCH):
        last = first + BATCH - 1

        @pl.when((first <= spot - NEAR) | (last >= spot + NEAR))
        def _(first=first):
            receive(range(first, first + BATCH))

    def place_rows(columns_ref, base, step):
        at = step * UNROLL
        columns = [columns_ref[at + k] for k in range(UNROLL)]
        rows = [board_ref[pl.ds(base * SLOTS + at + k, 1), :] for k in range(UNROLL)]
        for k in range(UNROLL):
            picked_ref[pl.ds(columns[k], 1), :] = rows[k]

    def place_low(step, carry):
        place_rows(low_ref, (plane - 1) * PLANE + NEAR + MARGIN, step)
        return carry

    def place_high(step, carry):
        place_rows(high_ref, (plane + 1) * PLANE + MARGIN, step)
        return carry

    chunk = SLOTS // UNROLL
    for copy in copies[:2]:
        copy.wait()

    @pl.when(plane > 0)
    def _():
        lax.fori_loop(spot * chunk, CROSS * chunk, place_low, 0)

    @pl.when(plane < 3)
    def _():
        lax.fori_loop(0, jnp.maximum(spot - NEAR + 1, 0) * chunk, place_high, 0)

    tops = [relay_ref[b * LONG + MESSAGE : (b + 1) * LONG, :] for b in range(PLANE)]
    top = jnp.max(functools.reduce(jnp.maximum, tops))
    scale = CFL_NUMBER / top * SECTION_STEP

    def results(block):
        lanes = tile_lanes(block)
        pairs = ((section_ref, section_hbm), (advanced_ref, advanced_hbm))
        return [
            pltpu.make_async_copy(source.at[:, :, lanes], target.at[:, :, lanes], sems.at[3 + 2 * block + k])
            for k, (source, target) in enumerate(pairs)
        ]

    def element_block(block):
        for face in range(6):
            place = face * BLOCKS + block
            square = picked_ref[pl.ds(pl.multiple_of(place * LANES, LANES), LANES), :].T
            start = pl.multiple_of(place * TRACE, TRACE)
            side = pl.multiple_of(place * SIDE, 8)
            at = pl.multiple_of(place * 16, 16)
            turns = [turn_ref[pl.ds(at + half * 8, 8), :] for half in range(2)]
            late = turns[0] >= 16
            known = [
                jnp.where(late, square[8 * k : 8 * k + 8], other_ref[pl.ds(start + 8 * k, 8), :])
                for k in range(10)
            ]
            own = [face_rows(state_ref, flat_ref, v, face, block) for v in range(5)]
            rows = side_ref[pl.ds(side + 16, 8), :]
            normal = [wide(rows[k : k + 1]) for k in range(3)]
            length = wide(rows[3:4])
            for half in range(2):
                upper = turns[half] % 16 >= 8
                sublane = turns[half] % 8
                far = []
                for v in range(5):
                    parts = [
                        jnp.take_along_axis(known[2 * v + k], sublane, axis=0, mode="promise_in_bounds")
                        for k in range(2)
                    ]
                    far.append(jnp.where(upper, parts[1], parts[0]))
                far_terms, far_wave = normal_flux(far, normal, length)
                bound = jnp.maximum(side_ref[pl.ds(side + half * 8, 8), :], far_wave)
                viscous = bound + length
                for v in range(5):
                    rows = pl.ds(start + v * 16 + half * 8, 8)
                    weight = bound if v == 0 else viscous
                    term_ref[rows, :] = (0.5 * LIFT_FACTOR) * (
                        weight * (far[v] - own[v][8 * half : 8 * half + 8]) - far_terms[v]
                    )
        if block == 0:
            copies[2].wait()
        lanes = tile_lanes(block)
        for v in range(5):
            base = block * 320 + v * 64
            tiles = [rate_ref[pl.ds(base + tile * 8, 8), :] for tile in range(8)]
            lift(tiles, term_ref, field_ref, v, block)
            for tile in range(8):
                nodes = slice(tile * 8, tile * 8 + 8)
                section = field_ref[pl.ds(base + tile * 8, 8), :]
                section_ref[v, nodes, lanes] = section
                advanced_ref[v, nodes, lanes] = state_ref[v, nodes, lanes] + scale * section
        for copy in results(block):
            copy.start()

    for block in range(BLOCKS):
        element_block(block)
    for block in range(BLOCKS):
        for copy in results(block):
            copy.wait()


def smem():
    return pl.BlockSpec(memory_space=pltpu.SMEM)


def vmem():
    return pl.BlockSpec(memory_space=pltpu.VMEM)


def params():
    return pltpu.CompilerParams(vmem_limit_bytes=VMEM_LIMIT)


def shape(*sizes):
    return jax.ShapeDtypeStruct(sizes, jnp.float32)


def scratch(*sizes):
    return pltpu.VMEM(sizes, jnp.float32)


def hbm():
    return pl.BlockSpec(memory_space=pltpu.HBM)


def anywhere():
    return pl.BlockSpec(memory_space=pl.ANY)


def in_hbm_shape(*sizes):
    return pltpu.HBM(sizes, jnp.float32)


def pack(place, partner, state):
    return pl.pallas_call(
        pack_kernel,
        out_shape=(
            in_hbm_shape(PLANE * MESSAGE, LANES),
            shape(CROSS * MESSAGE + 8, LANES),
            shape(CROSS * MESSAGE + 8, LANES),
            shape(8, LANES),
        ),
        in_specs=[smem(), hbm(), hbm()],
        out_specs=(hbm(), vmem(), vmem(), vmem()),
        scratch_shapes=[
            scratch(PLANE * MESSAGE, LANES),
            pltpu.SMEM((COLUMNS,), jnp.int32),
            scratch(5, 64, ELEMENTS),
            scratch(6, LANES, LANES),
            scratch(COLUMNS + (DEVICES + CROSS) * SLOTS, LANES),
            scratch(1280, LANES),
            pltpu.SemaphoreType.DMA((5 + PLANE // BATCH,)),
        ],
        compiler_params=params(),
        name="pack",
    )(place, partner, state)


def volume(place, state, register, metric, normal, code, partner):
    return pl.pallas_call(
        volume_kernel,
        out_shape=(
            in_hbm_shape(1280, LANES),
            shape(24 * SIDE, LANES),
            jax.ShapeDtypeStruct((24 * 16, LANES), jnp.int32),
        ),
        in_specs=[smem()] + [vmem()] * 6,
        out_specs=(vmem(),) * 3,
        scratch_shapes=[
            scratch(24 * TRACE, LANES),
            scratch(1280, LANES),
            scratch(72, LANES),
            scratch(3, 1280, LANES),
            scratch(1280, LANES),
            scratch(1280, LANES),
            scratch(24 * TRACE, LANES),
        ],
        compiler_params=params(),
        name="volume",
    )(place, state, register, metric, normal, code, partner)


def relay(place, up, down, best, rate):
    return pl.pallas_call(
        relay_kernel,
        out_shape=(in_hbm_shape(PLANE * LONG, LANES), shape(8, LANES)),
        in_specs=[smem()] + [vmem()] * 3 + [hbm()],
        out_specs=(vmem(), vmem()),
        compiler_params=params(),
        cost_estimate=pl.CostEstimate(flops=10**11, bytes_accessed=10**8, transcendentals=0),
        name="relay",
    )(place, up, down, best, rate)


def spread_top(three, far, relayed):
    return pl.pallas_call(
        top_kernel,
        out_shape=in_hbm_shape(PLANE * LONG, 1, LANES),
        in_specs=[vmem(), vmem(), hbm()],
        out_specs=hbm(),
        scratch_shapes=[scratch(1, 1, LANES), pltpu.SemaphoreType.DMA((PLANE,))],
        input_output_aliases={2: 0},
        compiler_params=params(),
        name="top",
    )(three, far, relayed)


def early(place, partner, blank, state, plane):
    return pl.pallas_call(
        early_kernel,
        out_shape=(
            shape(24 * TRACE, LANES),
            pltpu.HBM((COLUMNS + DEVICES * SLOTS,), jnp.int32),
        ),
        in_specs=[smem(), smem(), anywhere(), vmem(), vmem()],
        out_specs=(vmem(), smem()),
        scratch_shapes=[
            scratch(COLUMNS + DEVICES * SLOTS, LANES),
            scratch(1280, LANES),
            scratch(COLUMNS, LANES),
            pltpu.SemaphoreType.DMA,
        ],
        compiler_params=params(),
        name="early",
    )(place, partner, blank, state, plane)


def finish(place, owner, other, side, turn, rate, state, relayed):
    held = [in_hbm(value) for value in (owner, rate)]
    return pl.pallas_call(
        finish_kernel,
        out_shape=(in_hbm_shape(5, 64, ELEMENTS),) * 2,
        in_specs=[smem(), hbm(), hbm()] + [vmem()] * 5,
        out_specs=(hbm(), hbm()),
        scratch_shapes=[
            pltpu.SMEM((CROSS * SLOTS,), jnp.int32),
            pltpu.SMEM((CROSS * SLOTS,), jnp.int32),
            scratch(5, 64, ELEMENTS),
            scratch(5, 64, ELEMENTS),
            scratch((DEVICES + 2 * MARGIN) * SLOTS, LANES),
            scratch(COLUMNS + 8, LANES),
            scratch(1280, LANES),
            scratch(1280, LANES),
            scratch(24 * TRACE, LANES),
            scratch(1280, LANES),
            pltpu.SemaphoreType.DMA((11,)),
        ],
        compiler_params=params(),
        name="finish",
    )(place, *held, other, side, turn, state, relayed)


def in_hbm(value):
    return pltpu.with_memory_space_constraint(value, pltpu.HBM)


def in_vmem(value):
    return pltpu.with_memory_space_constraint(value, pltpu.VMEM)


def along_y(value, steps):
    return lax.ppermute(value, "y", [(i, (i + steps) % 4) for i in range(4)])


def on_device(state, register, metric, face_normal, partner, flip_code, face_role, send_face):
    plane = lax.axis_index("y").astype(jnp.int32)
    spot = lax.axis_index(("r", "x")).astype(jnp.int32)
    place = jnp.stack([plane, spot])
    state = state.transpose(1, 0, 2)
    rows = (COLUMNS // LANES, LANES)
    in_plane, up, down, best = pack(place, in_hbm(partner), in_hbm(state))
    from_below = along_y(up, 1)
    from_above = along_y(down, -1)
    far = along_y(best, 2)
    got = lax.all_to_all(in_plane, ("r", "x"), 0, 0, tiled=True)
    rate, side, turn = volume(
        place,
        state,
        register.transpose(1, 0, 2),
        metric,
        face_normal,
        flip_code.reshape(rows),
        partner.reshape(rows),
    )
    relayed, three = relay(place, from_below, from_above, best, in_hbm(rate))
    relayed = spread_top(three, far, in_hbm(relayed.reshape(PLANE * LONG, 1, LANES))).reshape(PLANE, LONG, 1, LANES)
    relayed = lax.all_to_all(relayed, ("r", "x"), 0, 0, tiled=True).reshape(PLANE * LONG, LANES)
    blank = jnp.full((COLUMNS + DEVICES * SLOTS,), COLUMNS, jnp.int32)
    other, owner = early(place, partner, blank, state, got)
    section, advanced = finish(place, owner, other, side, turn, rate, state, relayed)
    return section.transpose(1, 0, 2), advanced.transpose(1, 0, 2)


def solution(mesh):
    placed = (
        P(None, None, AXES),
        P(None, None, AXES),
        P(None, None, AXES),
        P(None, AXES),
        P(AXES),
        P(AXES),
        P(AXES),
        P(AXES, None, None),
    )
    return jax.shard_map(
        on_device,
        mesh=Mesh(mesh.devices.reshape(4, 8, 4), AXES),
        in_specs=placed,
        out_specs=(P(None, None, AXES), P(None, None, AXES)),
        check_vma=False,
    )
```

```python
import functools

import jax
import jax.numpy as jnp
import numpy as np
from jax import lax
from jax.experimental import pallas as pl
from jax.experimental.pallas import tpu as pltpu
from jax.sharding import Mesh
from jax.sharding import PartitionSpec as P

HEAT_RATIO = 1.4
LIFT_FACTOR = 6.0
CFL_NUMBER = 0.3
SECTION_KEEP = -0.4178904745
SECTION_STEP = 0.4432226
DEVICES = 128
ELEMENTS = 512
COLUMNS = 6 * ELEMENTS
SLOTS = 64
REACH = 24
LANES = 128
BLOCKS = ELEMENTS // LANES
TRACE = 80
GROUP = COLUMNS // 3
MESSAGE = TRACE * SLOTS // LANES
LONG = MESSAGE + 1
UNROLL = 32
SIDE = 24
BATCH = 4
AXES = ("y", "r", "x")
PLANE = 32
NEAR = PLANE - REACH
CROSS = REACH
MARGIN = PLANE
VMEM_LIMIT = 24 * 1024 * 1024


def derivative_matrix():
    points = np.array([-1.0, -1.0 / np.sqrt(5.0), 1.0 / np.sqrt(5.0), 1.0])
    weights = np.array(
        [
            1.0
            / np.prod([points[target] - points[source] for source in range(4) if source != target])
            for target in range(4)
        ]
    )
    matrix = np.zeros((4, 4))
    for target in range(4):
        for source in range(4):
            if target != source:
                matrix[target, source] = (
                    weights[source] / weights[target] / (points[target] - points[source])
                )
        matrix[target, target] = -np.sum(matrix[target])
    return matrix


def face_nodes(face):
    side = 3 * (face % 2)
    if face < 2:
        return [side * 16 + i * 4 + j for i in range(4) for j in range(4)]
    if face < 4:
        return [i * 16 + side * 4 + j for i in range(4) for j in range(4)]
    return [i * 16 + j * 4 + side for i in range(4) for j in range(4)]


def tile_lanes(block):
    return pl.ds(aligned(block * LANES, LANES), LANES)


def spread_nodes(state_ref, rows_ref):
    for v in range(5):
        for tile in range(8):
            for block in range(BLOCKS):
                rows_ref[pl.ds(v * 256 + tile * 32 + block, 8, stride=BLOCKS), :] = state_ref[
                    v, tile * 8 : tile * 8 + 8, tile_lanes(block)
                ]


def face_rows(state_ref, flat_ref, v, face, block):
    side = 3 * (face % 2)
    lanes = tile_lanes(block)
    if face < 2:
        return state_ref[v, side * 16 : side * 16 + 16, lanes]
    if face < 4:
        return jnp.concatenate(
            [state_ref[v, i * 16 + side * 4 : i * 16 + side * 4 + 4, lanes] for i in range(4)], axis=0
        )
    return flat_ref[pl.ds(aligned(block * 320, 64) + v * 64 + side, 16, stride=4), :]


def aligned(row, step=8):
    return row if isinstance(row, int) else pl.multiple_of(row, step)


def lane_index(shape):
    return lax.broadcasted_iota(jnp.int32, shape, 1)


def compact(rows):
    lane = lane_index((8, LANES))
    low = lane < 80
    mid = lane < 112

    def turn(value, shift):
        return pltpu.roll(value, shift, 1)

    first = [jnp.where(low, rows[k], turn(rows[5 + k], 80)) for k in range(3)]
    fourth = jnp.where(low, rows[3], jnp.where(mid, turn(rows[5], 32), turn(rows[7], 64)))
    fifth = jnp.where(low, rows[4], jnp.where(mid, turn(rows[6], 32), turn(rows[7], 48)))
    return first + [fourth, fifth]


def expand(parts):
    lane = lane_index((8, LANES))
    head = lane < 48
    body = lane < 64

    def turn(value, shift):
        return pltpu.roll(value, shift, 1)

    sixth = jnp.where(head, turn(parts[0], 48), turn(parts[3], 96))
    seventh = jnp.where(head, turn(parts[1], 48), turn(parts[4], 96))
    eighth = jnp.where(
        head, turn(parts[2], 48), jnp.where(body, turn(parts[3], 64), turn(parts[4], 80))
    )
    return list(parts) + [sixth, seventh, eighth]


def compact_into(board_ref, base, to_ref, at):
    rows = [board_ref[pl.ds(base + 8 * k, 8), :] for k in range(8 * BATCH)]
    parts = []
    for block in range(BATCH):
        parts += compact(rows[8 * block : 8 * block + 8])
    for k in range(5 * BATCH):
        to_ref[pl.ds(at + 8 * k, 8), :] = parts[k]


def expand_into(from_ref, start, board_ref, base):
    parts = [from_ref[pl.ds(start + 8 * k, 8), :] for k in range(5 * BATCH)]
    rows = []
    for block in range(BATCH):
        rows += expand(parts[5 * block : 5 * block + 5])
    for k in range(8 * BATCH):
        board_ref[pl.ds(base + 8 * k, 8), :] = rows[k]


def spread_flat(state_ref, flat_ref):
    for block in range(BLOCKS):
        for v in range(5):
            at = block * 320 + v * 64
            flat_ref[at : at + 64, :] = state_ref[v, :, tile_lanes(block)]


def face_trace(state_ref, flat_ref, face, block):
    return jnp.concatenate([face_rows(state_ref, flat_ref, v, face, block) for v in range(5)], axis=0)


def build_tables(state_ref, flat_ref, table_ref):
    spread_flat(state_ref, flat_ref)
    padding = jnp.zeros((LANES - TRACE, LANES), jnp.float32)
    for face in range(6):
        for block in range(BLOCKS):
            trace = face_trace(state_ref, flat_ref, face, block)
            place = face * BLOCKS + block
            square = jnp.concatenate([trace, padding], axis=0)
            table_ref[place * LANES : (place + 1) * LANES, :] = square.T


def pack_kernel(
    place_ref,
    partner_hbm,
    state_hbm,
    plane_hbm,
    up_ref,
    down_ref,
    best_ref,
    plane_ref,
    partner_ref,
    state_ref,
    table_ref,
    board_ref,
    flat_ref,
    sems,
):
    copies = [pltpu.make_async_copy(partner_hbm, partner_ref, sems.at[0])]
    for a in range(4):
        nodes = pl.ds(a * 16, 16)
        copies.append(
            pltpu.make_async_copy(state_hbm.at[:, nodes, :], state_ref.at[:, nodes, :], sems.at[1 + a])
        )
    for copy in copies:
        copy.start()
    for copy in copies[1:]:
        copy.wait()
    spread_flat(state_ref, flat_ref)
    copies[0].wait()
    padding = jnp.zeros((LANES - TRACE, LANES), jnp.float32)

    def build(face, block, slot):
        square = jnp.concatenate([face_trace(state_ref, flat_ref, face, block), padding], axis=0)
        table_ref[slot] = square.T

    def scatter(block):
        for face in range(6):
            build(face, block, face)
            base = face * ELEMENTS + block * LANES
            for start in range(0, LANES, UNROLL):
                targets = [partner_ref[base + start + k] for k in range(UNROLL)]
                rows = [table_ref[face, start + k : start + k + 1, :] for k in range(UNROLL)]
                for k in range(UNROLL):
                    board_ref[pl.ds(targets[k], 1), :] = rows[k]

    for block in range(BLOCKS):
        scatter(block)

    def speeds(step, best):
        density, mom_x, mom_y, mom_z, energy = [
            state_ref[v, pl.ds(pl.multiple_of(step * 8, 8), 8), :] for v in range(5)
        ]
        inverse = 1.0 / density
        speed_x, speed_y, speed_z = mom_x * inverse, mom_y * inverse, mom_z * inverse
        square = speed_x * speed_x + speed_y * speed_y + speed_z * speed_z
        kinetic = mom_x * speed_x + mom_y * speed_y + mom_z * speed_z
        pressure = (HEAT_RATIO - 1.0) * (energy - 0.5 * kinetic)
        wave = jnp.sqrt(square) + jnp.sqrt(HEAT_RATIO * pressure * inverse)
        return jnp.maximum(best, wave)

    best = lax.fori_loop(0, 8, speeds, jnp.zeros((8, ELEMENTS), jnp.float32))
    best = jnp.maximum(
        jnp.maximum(best[:, tile_lanes(0)], best[:, tile_lanes(1)]),
        jnp.maximum(best[:, tile_lanes(2)], best[:, tile_lanes(3)]),
    )
    best_ref[...] = best
    up_ref[CROSS * MESSAGE :, :] = best
    down_ref[CROSS * MESSAGE :, :] = best
    plane, spot = place_ref[0], place_ref[1]

    def send(to_ref, peer, step):
        base = pl.multiple_of(COLUMNS + (peer + step * BATCH) * SLOTS, SLOTS)
        compact_into(board_ref, base, to_ref, aligned(step * BATCH * MESSAGE))

    def send_up(step, carry):
        send(up_ref, (plane + 1) * PLANE, step)
        return carry

    def send_down(step, carry):
        send(down_ref, (plane - 1) * PLANE + NEAR, step)
        return carry

    sent = []
    for step in range(PLANE // BATCH):
        send(plane_ref, plane * PLANE, step)
        part = pl.ds(step * BATCH * MESSAGE, BATCH * MESSAGE)
        sent.append(
            pltpu.make_async_copy(plane_ref.at[part, :], plane_hbm.at[part, :], sems.at[5 + step])
        )
        sent[-1].start()
    upward = (jnp.maximum(spot - NEAR + 1, 0) + BATCH - 1) // BATCH
    lax.fori_loop(0, jnp.where(plane < 3, upward, 0), send_up, 0)
    lax.fori_loop(jnp.where(plane > 0, spot // BATCH, CROSS // BATCH), CROSS // BATCH, send_down, 0)
    for copy in sent:
        copy.wait()


def relay_kernel(place_ref, up_ref, down_ref, best_ref, rate_hbm, relay_ref, three_ref):
    spot = place_ref[1]
    for block in range(PLANE):
        for k in range(5):
            if block < CROSS:
                value = up_ref[block * MESSAGE + 8 * k : block * MESSAGE + 8 * k + 8, :]
            if block >= NEAR:
                at = (block - NEAR) * MESSAGE + 8 * k
                other = down_ref[at : at + 8, :]
                value = other if block >= CROSS else jnp.where(block <= spot - NEAR, value, other)
            relay_ref[block * LONG + 8 * k : block * LONG + 8 * k + 8, :] = value
    three_ref[...] = jnp.maximum(
        best_ref[...], jnp.maximum(up_ref[CROSS * MESSAGE :, :], down_ref[CROSS * MESSAGE :, :])
    )


def top_kernel(three_ref, far_ref, relay_in, relay_hbm, top_ref, sems):
    top = jnp.max(jnp.maximum(three_ref[...], far_ref[...]), axis=0, keepdims=True)
    top_ref[0] = top
    copies = [
        pltpu.make_async_copy(top_ref, relay_hbm.at[pl.ds(block * LONG + MESSAGE, 1)], sems.at[block])
        for block in range(PLANE)
    ]
    for copy in copies:
        copy.start()
    for copy in copies:
        copy.wait()


def early_kernel(
    place_ref,
    partner_ref,
    blank_hbm,
    state_ref,
    plane_ref,
    other_ref,
    owner_ref,
    board_ref,
    flat_ref,
    picked_ref,
    sem,
):
    plane, spot = place_ref[0], place_ref[1]
    blank = pltpu.make_async_copy(blank_hbm, owner_ref, sem)
    blank.start()
    build_tables(state_ref, flat_ref, board_ref)

    def receive(step, carry):
        start = pl.multiple_of(step * BATCH * MESSAGE, 8)
        base = pl.multiple_of(COLUMNS + (plane * PLANE + step * BATCH) * SLOTS, SLOTS)
        expand_into(plane_ref, start, board_ref, base)
        return carry

    lax.fori_loop(jnp.maximum(spot - REACH, 0) // BATCH, PLANE // BATCH, receive, 0)

    def gather(step, carry):
        base = step * UNROLL
        indices = [partner_ref[base + k] for k in range(UNROLL)]
        rows = [board_ref[pl.ds(index, 1), :] for index in indices]
        for k in range(UNROLL):
            picked_ref[pl.ds(base + k, 1), :] = rows[k]
            owner_ref[indices[k]] = base + k
        return carry

    blank.wait()
    lax.fori_loop(0, COLUMNS // UNROLL, gather, 0)
    for place in range(COLUMNS // LANES):
        square = picked_ref[place * LANES : (place + 1) * LANES, :].T
        other_ref[place * TRACE : (place + 1) * TRACE, :] = square[0:TRACE]


def sublane_index():
    return lax.broadcasted_iota(jnp.int32, (8, LANES), 0)


def wide(row):
    return jnp.broadcast_to(row, (8, LANES))


def face_normals(normal_ref, place):
    lanes = pl.ds(pl.multiple_of(place * LANES, LANES), LANES)
    normal = [wide(normal_ref[k : k + 1, lanes]) for k in range(3)]
    length = jnp.sqrt(normal[0] * normal[0] + normal[1] * normal[1] + normal[2] * normal[2])
    return normal, length


def lift(tiles, flux_ref, field_ref, v, block):
    first = sublane_index() < 4

    def piece(face, half):
        start = aligned((face * BLOCKS + block) * TRACE + v * 16)
        return flux_ref[pl.ds(start + half * 8, 8), :]

    tiles = list(tiles)
    for half in range(2):
        tiles[half] = tiles[half] + piece(0, half)
        tiles[6 + half] = tiles[6 + half] + piece(1, half)
        low, high = piece(2, half), piece(3, half)
        tiles[4 * half] = tiles[4 * half] + jnp.where(first, low, 0.0)
        tiles[4 * half + 2] = tiles[4 * half + 2] + jnp.where(first, pltpu.roll(low, 4, 0), 0.0)
        tiles[4 * half + 1] = tiles[4 * half + 1] + jnp.where(first, 0.0, pltpu.roll(high, 4, 0))
        tiles[4 * half + 3] = tiles[4 * half + 3] + jnp.where(first, 0.0, high)
    base = aligned(v * 64 + block * 320)
    for tile in range(8):
        field_ref[pl.ds(base + tile * 8, 8), :] = tiles[tile]
    for half in range(2):
        for face in (4, 5):
            nodes = pl.ds(base + half * 32 + 3 * (face - 4), 8, stride=4)
            field_ref[nodes, :] = field_ref[nodes, :] + piece(face, half)


def turn_indices(code):
    flip_first = jnp.where(code % 2 == 1, 3, 0)
    flip_second = jnp.where((code // 2) % 2 == 1, 3, 0)
    swapped = code >= 4
    sublane = sublane_index()
    result = []
    for half in range(2):
        i, j = 2 * half + sublane // 4, sublane % 4
        first = jnp.where(swapped, j, i) ^ flip_first
        second = jnp.where(swapped, i, j) ^ flip_second
        result.append(first * 4 + second)
    return result


def volume_kernel(
    place_ref,
    state_ref,
    register_ref,
    metric_ref,
    normal_ref,
    code_ref,
    partner_ref,
    field_ref,
    side_ref,
    turn_ref,
    own_ref,
    rows_ref,
    tensor_ref,
    flux_ref,
    flat_ref,
    rate_ref,
    term_ref,
):
    low = COLUMNS + place_ref[0] * (PLANE * SLOTS)
    spread_nodes(state_ref, rows_ref)
    spread_flat(state_ref, flat_ref)
    for face in range(6):
        for block in range(BLOCKS):
            place = face * BLOCKS + block
            own_ref[place * TRACE : (place + 1) * TRACE, :] = face_trace(state_ref, flat_ref, face, block)

    def own_fluxes(face, carry):
        for block in range(BLOCKS):
            place = face * BLOCKS + block
            normal, length = face_normals(normal_ref, place)
            start = pl.multiple_of(place * TRACE, TRACE)
            side = pl.multiple_of(place * SIDE, 8)
            rows = [value[0:1] for value in normal + [length]]
            side_ref[pl.ds(side + 16, 8), :] = jnp.concatenate(rows + rows, axis=0)
            partner = wide(partner_ref[pl.ds(place, 1), :])
            late = (partner >= COLUMNS) & ((partner < low) | (partner >= low + PLANE * SLOTS))
            late = jnp.where(late, 16, 0)
            for half, turn in enumerate(turn_indices(wide(code_ref[pl.ds(place, 1), :]))):
                turn_ref[pl.ds(pl.multiple_of(place * 16, 16) + half * 8, 8), :] = turn + late
            for half in range(2):
                at = start + half * 8
                own = [own_ref[pl.ds(at + v * 16, 8), :] for v in range(5)]
                terms, wave = normal_flux(own, normal, length)
                for v in range(5):
                    term_ref[pl.ds(at + v * 16, 8), :] = (0.5 * LIFT_FACTOR) * terms[v]
                side_ref[pl.ds(side + half * 8, 8), :] = wave
        return carry

    lax.fori_loop(0, 6, own_fluxes, 0)
    for direction in range(3):
        for half in range(2):
            for block in range(BLOCKS):
                tensor_ref[pl.ds(direction * 24 + half * 4 + block, 3, stride=8), :] = metric_ref[
                    direction, :, block * LANES : (block + 1) * LANES
                ]

    def fluxes(step, carry):
        at = pl.multiple_of(step * 8, 8)
        density, mom_x, mom_y, mom_z, energy = [
            rows_ref[pl.ds(v * 256 + at, 8), :] for v in range(5)
        ]
        inverse = 1.0 / density
        momentum = [mom_x, mom_y, mom_z]
        velocity = [m * inverse for m in momentum]
        pressure = (HEAT_RATIO - 1.0) * (
            energy
            - 0.5 * (mom_x * velocity[0] + mom_y * velocity[1] + mom_z * velocity[2])
        )
        enthalpy = energy + pressure
        for direction in range(3):
            tensor = [tensor_ref[direction * 24 + k * 8 : direction * 24 + k * 8 + 8, :] for k in range(3)]
            along = tensor[0] * velocity[0] + tensor[1] * velocity[1] + tensor[2] * velocity[2]
            values = [density * along]
            values += [momentum[k] * along + pressure * tensor[k] for k in range(3)]
            values += [enthalpy * along]
            for v in range(5):
                flux_ref[direction, pl.ds(v * 256 + at, 8), :] = values[v]
        return carry

    lax.fori_loop(0, 32, fluxes, 0)
    matrix = derivative_matrix()
    upper = lax.broadcasted_iota(jnp.int32, (8, LANES), 0) < 4

    def pair(first, second):
        return jnp.where(upper, jnp.float32(first), jnp.float32(second))

    straight = [[pair(matrix[2 * t, 2 * s], matrix[2 * t + 1, 2 * s + 1]) for s in range(2)] for t in range(2)]
    crossed = [[pair(matrix[2 * t, 2 * s + 1], matrix[2 * t + 1, 2 * s]) for s in range(2)] for t in range(2)]

    def combine(values, target):
        total = values[0] * float(matrix[target, 0])
        for source in range(1, 4):
            total = total + values[source] * float(matrix[target, source])
        return total

    def diverge(v, carry):
        base = pl.multiple_of(v * 256, 256)
        for rest in range(8):
            values = [flux_ref[0, pl.ds(base + a * 64 + rest * 8, 8), :] for a in range(4)]
            for a in range(4):
                rate_ref[pl.ds(base + a * 64 + rest * 8, 8), :] = -combine(values, a)
        for a in range(4):
            for half in range(2):
                values = [flux_ref[1, pl.ds(base + a * 64 + b * 16 + half * 8, 8), :] for b in range(4)]
                third = [flux_ref[2, pl.ds(base + a * 64 + b * 16 + half * 8, 8), :] for b in range(4)]
                other = [flux_ref[2, pl.ds(base + a * 64 + b * 16 + (1 - half) * 8, 8), :] for b in range(4)]
                for b in range(4):
                    at = pl.ds(base + a * 64 + b * 16 + half * 8, 8)
                    same, far = third[b], other[b]
                    total = combine(values, b)
                    total = total + straight[half][half] * same
                    total = total + crossed[half][half] * pltpu.roll(same, 4, 0)
                    total = total + straight[half][1 - half] * far
                    total = total + crossed[half][1 - half] * pltpu.roll(far, 4, 0)
                    rate_ref[at, :] = rate_ref[at, :] - total
        return carry

    lax.fori_loop(0, 5, diverge, 0)

    def gather_terms(v, carry):
        base = pl.multiple_of(v * 256, 256)
        for block in range(BLOCKS):
            tiles = []
            for tile in range(8):
                old = register_ref[v, tile * 8 : tile * 8 + 8, tile_lanes(block)]
                rate = rate_ref[pl.ds(base + tile * 32 + block, 8, stride=BLOCKS), :]
                tiles.append(rate + SECTION_KEEP * old)
            lift(tiles, term_ref, field_ref, v, block)
        return carry

    lax.fori_loop(0, 5, gather_terms, 0)


def normal_flux(values, normal, length):
    density, momentum, energy = values[0], values[1:4], values[4]
    inverse = 1.0 / density
    velocity = [m * inverse for m in momentum]
    pressure = (HEAT_RATIO - 1.0) * (
        energy
        - 0.5 * (momentum[0] * velocity[0] + momentum[1] * velocity[1] + momentum[2] * velocity[2])
    )
    speed = velocity[0] * normal[0] + velocity[1] * normal[1] + velocity[2] * normal[2]
    terms = [density * speed]
    terms += [momentum[k] * speed + pressure * normal[k] for k in range(3)]
    terms += [(energy + pressure) * speed]
    wave = jnp.abs(speed) + jnp.sqrt(HEAT_RATIO * pressure * inverse) * length
    return terms, wave


def finish_kernel(
    place_ref,
    owner_hbm,
    rate_hbm,
    other_ref,
    side_ref,
    turn_ref,
    state_ref,
    relay_ref,
    section_hbm,
    advanced_hbm,
    low_ref,
    high_ref,
    section_ref,
    advanced_ref,
    board_ref,
    picked_ref,
    rate_ref,
    flat_ref,
    term_ref,
    field_ref,
    sems,
):
    plane, spot = place_ref[0], place_ref[1]
    window = CROSS * SLOTS
    low_slot = jnp.maximum(COLUMNS + ((plane - 1) * PLANE + NEAR) * SLOTS, 0)
    high_slot = jnp.minimum(COLUMNS + (plane + 1) * PLANE * SLOTS, COLUMNS + DEVICES * SLOTS - window)
    sources = [
        (owner_hbm.at[pl.ds(pl.multiple_of(low_slot, 512), window)], low_ref),
        (owner_hbm.at[pl.ds(pl.multiple_of(high_slot, 512), window)], high_ref),
        (rate_hbm, rate_ref),
    ]
    copies = [
        pltpu.make_async_copy(source, target, sems.at[k])
        for k, (source, target) in enumerate(sources)
    ]
    for copy in copies:
        copy.start()
    spread_flat(state_ref, flat_ref)

    def receive(blocks):
        parts = [relay_ref[b * LONG + 8 * k : b * LONG + 8 * k + 8, :] for b in blocks for k in range(5)]
        rows = []
        for k in range(BATCH):
            rows += expand(parts[5 * k : 5 * k + 5])
        for k, block in enumerate(blocks):
            side = jnp.where(block >= spot + NEAR, plane - 1, plane + 1)
            base = pl.multiple_of((side * PLANE + block + MARGIN) * SLOTS, SLOTS)
            for j in range(8):
                board_ref[pl.ds(base + 8 * j, 8), :] = rows[8 * k + j]

    for first in range(0, PLANE, BATCH):
        last = first + BATCH - 1

        @pl.when((first <= spot - NEAR) | (last >= spot + NEAR))
        def _(first=first):
            receive(range(first, first + BATCH))

    def place_rows(columns_ref, base, step):
        at = step * UNROLL
        columns = [columns_ref[at + k] for k in range(UNROLL)]
        rows = [board_ref[pl.ds(base * SLOTS + at + k, 1), :] for k in range(UNROLL)]
        for k in range(UNROLL):
            picked_ref[pl.ds(columns[k], 1), :] = rows[k]

    def place_low(step, carry):
        place_rows(low_ref, (plane - 1) * PLANE + NEAR + MARGIN, step)
        return carry

    def place_high(step, carry):
        place_rows(high_ref, (plane + 1) * PLANE + MARGIN, step)
        return carry

    chunk = SLOTS // UNROLL
    from_low = (plane > 0) & (spot < CROSS)
    from_high = (plane < 3) & (spot >= NEAR)

    @pl.when(from_low)
    def _():
        copies[0].wait()
        lax.fori_loop(spot * chunk, CROSS * chunk, place_low, 0)

    @pl.when(from_high)
    def _():
        copies[1].wait()
        lax.fori_loop(0, (spot - NEAR + 1) * chunk, place_high, 0)

    tops = [relay_ref[b * LONG + MESSAGE : (b + 1) * LONG, :] for b in range(PLANE)]
    top = jnp.max(functools.reduce(jnp.maximum, tops))
    scale = CFL_NUMBER / top * SECTION_STEP

    def results(block):
        lanes = tile_lanes(block)
        pairs = ((section_ref, section_hbm), (advanced_ref, advanced_hbm))
        return [
            pltpu.make_async_copy(source.at[:, :, lanes], target.at[:, :, lanes], sems.at[3 + 2 * block + k])
            for k, (source, target) in enumerate(pairs)
        ]

    def element_block(block):
        for face in range(6):
            place = face * BLOCKS + block
            square = picked_ref[pl.ds(pl.multiple_of(place * LANES, LANES), LANES), :].T
            start = pl.multiple_of(place * TRACE, TRACE)
            side = pl.multiple_of(place * SIDE, 8)
            at = pl.multiple_of(place * 16, 16)
            turns = [turn_ref[pl.ds(at + half * 8, 8), :] for half in range(2)]
            late = turns[0] >= 16
            known = [
                jnp.where(late, square[8 * k : 8 * k + 8], other_ref[pl.ds(start + 8 * k, 8), :])
                for k in range(10)
            ]
            own = [face_rows(state_ref, flat_ref, v, face, block) for v in range(5)]
            rows = side_ref[pl.ds(side + 16, 8), :]
            normal = [wide(rows[k : k + 1]) for k in range(3)]
            length = wide(rows[3:4])
            for half in range(2):
                upper = turns[half] % 16 >= 8
                sublane = turns[half] % 8
                far = []
                for v in range(5):
                    parts = [
                        jnp.take_along_axis(known[2 * v + k], sublane, axis=0, mode="promise_in_bounds")
                        for k in range(2)
                    ]
                    far.append(jnp.where(upper, parts[1], parts[0]))
                far_terms, far_wave = normal_flux(far, normal, length)
                bound = jnp.maximum(side_ref[pl.ds(side + half * 8, 8), :], far_wave)
                viscous = bound + length
                for v in range(5):
                    rows = pl.ds(start + v * 16 + half * 8, 8)
                    weight = bound if v == 0 else viscous
                    term_ref[rows, :] = (0.5 * LIFT_FACTOR) * (
                        weight * (far[v] - own[v][8 * half : 8 * half + 8]) - far_terms[v]
                    )
        if block == 0:
            copies[2].wait()
        lanes = tile_lanes(block)
        for v in range(5):
            base = block * 320 + v * 64
            tiles = [rate_ref[pl.ds(base + tile * 8, 8), :] for tile in range(8)]
            lift(tiles, term_ref, field_ref, v, block)
            for tile in range(8):
                nodes = slice(tile * 8, tile * 8 + 8)
                section = field_ref[pl.ds(base + tile * 8, 8), :]
                section_ref[v, nodes, lanes] = section
                advanced_ref[v, nodes, lanes] = state_ref[v, nodes, lanes] + scale * section
        for copy in results(block):
            copy.start()

    for block in range(BLOCKS):
        element_block(block)
    pl.when(jnp.logical_not(from_low))(copies[0].wait)
    pl.when(jnp.logical_not(from_high))(copies[1].wait)
    for block in range(BLOCKS):
        for copy in results(block):
            copy.wait()


def smem():
    return pl.BlockSpec(memory_space=pltpu.SMEM)


def vmem():
    return pl.BlockSpec(memory_space=pltpu.VMEM)


def params():
    return pltpu.CompilerParams(vmem_limit_bytes=VMEM_LIMIT)


def shape(*sizes):
    return jax.ShapeDtypeStruct(sizes, jnp.float32)


def scratch(*sizes):
    return pltpu.VMEM(sizes, jnp.float32)


def hbm():
    return pl.BlockSpec(memory_space=pltpu.HBM)


def anywhere():
    return pl.BlockSpec(memory_space=pl.ANY)


def in_hbm_shape(*sizes):
    return pltpu.HBM(sizes, jnp.float32)


def pack(place, partner, state):
    return pl.pallas_call(
        pack_kernel,
        out_shape=(
            in_hbm_shape(PLANE * MESSAGE, LANES),
            shape(CROSS * MESSAGE + 8, LANES),
            shape(CROSS * MESSAGE + 8, LANES),
            shape(8, LANES),
        ),
        in_specs=[smem(), hbm(), hbm()],
        out_specs=(hbm(), vmem(), vmem(), vmem()),
        scratch_shapes=[
            scratch(PLANE * MESSAGE, LANES),
            pltpu.SMEM((COLUMNS,), jnp.int32),
            scratch(5, 64, ELEMENTS),
            scratch(6, LANES, LANES),
            scratch(COLUMNS + (DEVICES + CROSS) * SLOTS, LANES),
            scratch(1280, LANES),
            pltpu.SemaphoreType.DMA((5 + PLANE // BATCH,)),
        ],
        compiler_params=params(),
        name="pack",
    )(place, partner, state)


def volume(place, state, register, metric, normal, code, partner):
    return pl.pallas_call(
        volume_kernel,
        out_shape=(
            in_hbm_shape(1280, LANES),
            shape(24 * SIDE, LANES),
            jax.ShapeDtypeStruct((24 * 16, LANES), jnp.int32),
        ),
        in_specs=[smem()] + [vmem()] * 6,
        out_specs=(vmem(),) * 3,
        scratch_shapes=[
            scratch(24 * TRACE, LANES),
            scratch(1280, LANES),
            scratch(72, LANES),
            scratch(3, 1280, LANES),
            scratch(1280, LANES),
            scratch(1280, LANES),
            scratch(24 * TRACE, LANES),
        ],
        compiler_params=params(),
        name="volume",
    )(place, state, register, metric, normal, code, partner)


def relay(place, up, down, best, rate):
    return pl.pallas_call(
        relay_kernel,
        out_shape=(in_hbm_shape(PLANE * LONG, LANES), shape(8, LANES)),
        in_specs=[smem()] + [vmem()] * 3 + [hbm()],
        out_specs=(vmem(), vmem()),
        compiler_params=params(),
        cost_estimate=pl.CostEstimate(flops=10**11, bytes_accessed=10**8, transcendentals=0),
        name="relay",
    )(place, up, down, best, rate)


def spread_top(three, far, relayed):
    return pl.pallas_call(
        top_kernel,
        out_shape=in_hbm_shape(PLANE * LONG, 1, LANES),
        in_specs=[vmem(), vmem(), hbm()],
        out_specs=hbm(),
        scratch_shapes=[scratch(1, 1, LANES), pltpu.SemaphoreType.DMA((PLANE,))],
        input_output_aliases={2: 0},
        compiler_params=params(),
        name="top",
    )(three, far, relayed)


def early(place, partner, blank, state, plane):
    return pl.pallas_call(
        early_kernel,
        out_shape=(
            shape(24 * TRACE, LANES),
            pltpu.HBM((COLUMNS + DEVICES * SLOTS,), jnp.int32),
        ),
        in_specs=[smem(), smem(), anywhere(), vmem(), vmem()],
        out_specs=(vmem(), smem()),
        scratch_shapes=[
            scratch(COLUMNS + DEVICES * SLOTS, LANES),
            scratch(1280, LANES),
            scratch(COLUMNS, LANES),
            pltpu.SemaphoreType.DMA,
        ],
        compiler_params=params(),
        name="early",
    )(place, partner, blank, state, plane)


def finish(place, owner, other, side, turn, rate, state, relayed):
    held = [in_hbm(value) for value in (owner, rate)]
    return pl.pallas_call(
        finish_kernel,
        out_shape=(in_hbm_shape(5, 64, ELEMENTS),) * 2,
        in_specs=[smem(), hbm(), hbm()] + [vmem()] * 5,
        out_specs=(hbm(), hbm()),
        scratch_shapes=[
            pltpu.SMEM((CROSS * SLOTS,), jnp.int32),
            pltpu.SMEM((CROSS * SLOTS,), jnp.int32),
            scratch(5, 64, ELEMENTS),
            scratch(5, 64, ELEMENTS),
            scratch((DEVICES + 2 * MARGIN) * SLOTS, LANES),
            scratch(COLUMNS + 8, LANES),
            scratch(1280, LANES),
            scratch(1280, LANES),
            scratch(24 * TRACE, LANES),
            scratch(1280, LANES),
            pltpu.SemaphoreType.DMA((11,)),
        ],
        compiler_params=params(),
        name="finish",
    )(place, *held, other, side, turn, state, relayed)


def in_hbm(value):
    return pltpu.with_memory_space_constraint(value, pltpu.HBM)


def in_vmem(value):
    return pltpu.with_memory_space_constraint(value, pltpu.VMEM)


def along_y(value, steps):
    return lax.ppermute(value, "y", [(i, (i + steps) % 4) for i in range(4)])


def on_device(state, register, metric, face_normal, partner, flip_code, face_role, send_face):
    plane = lax.axis_index("y").astype(jnp.int32)
    spot = lax.axis_index(("r", "x")).astype(jnp.int32)
    place = jnp.stack([plane, spot])
    state = state.transpose(1, 0, 2)
    rows = (COLUMNS // LANES, LANES)
    in_plane, up, down, best = pack(place, in_hbm(partner), in_hbm(state))
    from_below = along_y(up, 1)
    from_above = along_y(down, -1)
    far = along_y(best, 2)
    got = lax.all_to_all(in_plane, ("r", "x"), 0, 0, tiled=True)
    rate, side, turn = volume(
        place,
        state,
        register.transpose(1, 0, 2),
        metric,
        face_normal,
        flip_code.reshape(rows),
        partner.reshape(rows),
    )
    relayed, three = relay(place, from_below, from_above, best, in_hbm(rate))
    relayed = spread_top(three, far, in_hbm(relayed.reshape(PLANE * LONG, 1, LANES))).reshape(PLANE, LONG, 1, LANES)
    relayed = lax.all_to_all(relayed, ("r", "x"), 0, 0, tiled=True).reshape(PLANE * LONG, LANES)
    blank = jnp.full((COLUMNS + DEVICES * SLOTS,), COLUMNS, jnp.int32)
    other, owner = early(place, partner, blank, state, got)
    section, advanced = finish(place, owner, other, side, turn, rate, state, relayed)
    return section.transpose(1, 0, 2), advanced.transpose(1, 0, 2)


def solution(mesh):
    placed = (
        P(None, None, AXES),
        P(None, None, AXES),
        P(None, None, AXES),
        P(None, AXES),
        P(AXES),
        P(AXES),
        P(AXES),
        P(AXES, None, None),
    )
    return jax.shard_map(
        on_device,
        mesh=Mesh(mesh.devices.reshape(4, 8, 4), AXES),
        in_specs=placed,
        out_specs=(P(None, None, AXES), P(None, None, AXES)),
        check_vma=False,
    )
```
